32 devices in a mesh: seq: 8 (over z, x), head: 4 (over y, core).
Axes of the slice: x: 2, y: 2, z: 4, core: 2. Of those that a mesh axis runs over, the one named last changes fastest.
Arguments:
- tokens: bfloat16 [3, 1024, 2048], P(None, 'seq'), may hold values from -6 to 6
- lengths: int32 [3], replicated, may hold values from 256 to 1024, as said below
- norm_first: float32 [2048], replicated, may hold values from 0.5 to 1.5
- mix_weight: bfloat16 [4, 2048, 2048], P(None, None, 'head'), may hold values from -0.125 to 0.125
- lower_bound: float32 [2048], P('head'), may hold values from 0.9 to 1, as said below
- out_gain: float32 [2048], P('head'), may hold values from 0.5 to 1.5
- w_out: bfloat16 [2048, 2048], P('head'), may hold values from -0.25 to 0.25
- norm_second: float32 [2048], replicated, may hold values from 0.5 to 1.5
- ffn_in: bfloat16 [2, 2048, 5632], P(None, None, 'head'), may hold values from -0.125 to 0.125
- ffn_out: bfloat16 [5632, 2048], P('head'), may hold values from -0.078125 to 0.078125
- cotangent: bfloat16 [3, 1024, 2048], P(None, 'seq'), may hold values from -6 to 6
Outputs:
- output: bfloat16 [3, 1024, 2048], P(None, 'seq')
- grad_tokens: bfloat16 [3, 1024, 2048], P(None, 'seq')
- grad_norm_first: float32 [2048], replicated
- grad_mix: float32 [4, 2048, 2048], P(None, 'seq', 'head')
- grad_bound: float32 [2048], P('head')
- grad_out_gain: float32 [2048], P('head')
- grad_w_out: float32 [2048, 2048], P('head', 'seq')
- grad_norm_second: float32 [2048], replicated
- grad_ffn_in: float32 [2, 2048, 5632], P(None, 'seq', 'head')
- grad_ffn_out: float32 [5632, 2048], P('head', 'seq')
The draws below stay inside these ranges and needn't reach their ends.
Inputs may be any that keep to these rules, and one draw needn't show every extreme that they name: `lengths`: positions at or past a slot's length are padding; some slot is full. `lower_bound`: channel-wise lower bounds below one.
All inputs are finite; a program needn't handle non-finite values.
Results may differ from the reference program's by a relative error of at most 0.01.
Values sent between devices are 32-bit elements; how exact they have to be, the bound alone decides.
No kernel may reach another device: no remote copies, remote signals or barrier semaphores. Data moves between devices by JAX's collectives and lax.ppermute only.
A program may use at most 320 MiB of HBM per device.

```python
import math
import jax
import jax.numpy as jnp
from jax import lax

D = 2048
HEADS = 16
FF = 5632
SLOTS = 3
SLOT = 1024


def draw_lengths(key, part):
    first = jax.random.fold_in(key, 11)
    second = jax.random.fold_in(key, 12)
    drawn = jax.random.randint(first, (SLOTS,), SLOT // 4, SLOT + 1, dtype=jnp.int32)
    pick = jax.random.randint(second, (), 0, SLOTS, dtype=jnp.int32)
    return jnp.where(jnp.arange(SLOTS, dtype=jnp.int32) == pick, SLOT, drawn).astype(jnp.int32)


def draw_lower_bound(key, part):
    gap = jnp.exp(jax.random.uniform(key, (D,), jnp.float32, math.log(0.0001), math.log(0.1)))
    return (1.0 - gap).astype(jnp.float32)


def block_levels(rng, shape, split, smallest, top_value):
    def one(axis_at, blocks):
        heights = jax.random.uniform(jax.random.fold_in(jax.random.fold_in(rng, 6), axis_at), (blocks,), jnp.float32, smallest / len(split), top_value / len(split))
        return jnp.repeat(jnp.exp(heights), shape[axis_at] // blocks).reshape((-1,) + (1,) * (len(shape) - axis_at - 1))

    gain = one(*split[0])
    for cut in split[1:]:
        gain = gain * one(*cut)
    return gain


def scatter_about(rng, shape, deviation, bound, pieces=(), kind=jnp.bfloat16):
    values = jax.random.normal(rng, shape, jnp.float32) * deviation
    if len(pieces) > 0:
        values = block_levels(rng, shape, pieces, -0.22, 0.18) * values
    return jnp.clip(values, min=-bound, max=bound).astype(kind)


def setup_inputs(seed: int = 0) -> dict:
    seeds = jax.random.split(jax.random.key(seed), 12)
    tokens = scatter_about(seeds[0], (SLOTS, SLOT, D), 1.0, 6.0, ((1, 8),))
    lengths = draw_lengths(jax.random.fold_in(seeds[11], 71), 0)
    norm_first = jnp.clip(1.0 + 0.1 * jax.random.normal(seeds[2], (D,), jnp.float32), 0.5, 1.5)
    mix_weight = scatter_about(seeds[3], (4, D, D), D ** -0.5, 0.125, ((2, 4),))
    lower_bound = draw_lower_bound(jax.random.fold_in(seeds[11], 71), 0)
    out_gain = jnp.clip(1.0 + 0.1 * jax.random.normal(seeds[5], (D,), jnp.float32), 0.5, 1.5)
    w_out = scatter_about(seeds[6], (D, D), (D // 4) ** -0.5, 0.25, ((0, 4),))
    norm_second = jnp.clip(1.0 + 0.1 * jax.random.normal(seeds[7], (D,), jnp.float32), 0.5, 1.5)
    ffn_in = scatter_about(seeds[8], (2, D, FF), D ** -0.5, 0.125, ((2, 4),))
    ffn_out = scatter_about(seeds[9], (FF, D), FF ** -0.5, 0.078125, ((0, 4),))
    cotangent = scatter_about(seeds[10], (SLOTS, SLOT, D), 1.0, 6.0, ((1, 8),))
    return {"tokens": tokens, "lengths": lengths, "norm_first": norm_first, "mix_weight": mix_weight, "lower_bound": lower_bound, "out_gain": out_gain, "w_out": w_out, "norm_second": norm_second, "ffn_in": ffn_in, "ffn_out": ffn_out, "cotangent": cotangent}


EPS = 1e-06
HIGHEST_ACCURACY = lax.Precision.HIGHEST

@jax.custom_vjp
def low(v):
    return lax.optimization_barrier(v.astype(jnp.bfloat16)).astype(jnp.float32)

@jax.custom_vjp
def low_back(v):
    return v

def low_keep(v):
    return (low(v), None)

def low_pass(kept, grad):
    return (grad,)

def back_keep(v):
    return (v, None)

def back_low(kept, grad):
    return (low(grad),)
low.defvjp(low_keep, low_pass)
low_back.defvjp(back_keep, back_low)

def rms_scale(v):
    return lax.rsqrt(lax.optimization_barrier(jnp.mean(v * v, axis=-1, keepdims=True)) + EPS)

def block_step(hidden_state, inputs):
    query_vectors, logf, key_vectors, value_vectors = inputs
    running_total = jnp.cumsum(logf, axis=1)
    cross_segment = jnp.einsum('raf,rfj->raj', query_vectors * jnp.exp(running_total), hidden_state, precision=HIGHEST_ACCURACY)
    size = query_vectors.shape[1]
    lower = (jnp.arange(size)[:, None] >= jnp.arange(size)[None, :])[None, :, :, None]
    diff = running_total[:, :, None, :] - running_total[:, None, :, :]
    rel = jnp.where(lower, jnp.exp(jnp.where(lower, diff, 0.0)), 0.0)
    scores = jnp.einsum('htk,hsk,htsk->hts', query_vectors, key_vectors, rel, precision=HIGHEST_ACCURACY)
    intra = jnp.einsum('hts,hsv->htv', scores, value_vectors, precision=HIGHEST_ACCURACY)
    final_position = running_total[:, -1:, :]
    hidden_state = jnp.exp(final_position[:, 0, :])[:, :, None] * hidden_state + jnp.einsum('ndp,ndi->npi', key_vectors * jnp.exp(final_position - running_total), value_vectors, precision=HIGHEST_ACCURACY)
    return (hidden_state, cross_segment + intra)

def recur_slot(query_vectors, logf, key_vectors, value_vectors):
    heads, length, width = query_vectors.shape
    size = min(64, length)
    count = length // size

    def cut(a):
        return jnp.moveaxis(a.reshape(heads, count, size, width), 1, 0)
    start = jnp.zeros((heads, width, width), jnp.float32)
    final, outs = lax.scan(jax.checkpoint(block_step), start, (cut(query_vectors), cut(logf), cut(key_vectors), cut(value_vectors)))
    return jnp.moveaxis(outs, 0, 1).reshape(heads, length, width)

def to_heads(a):
    slots, length, width = a.shape
    return a.reshape(slots, length, HEADS, width // HEADS).transpose(0, 2, 1, 3)

def forward(x, norm_first, mix_weight, lower_bound, out_gain, w_out, norm_second, ffn_in, ffn_out, valid):
    xn1 = low(x * rms_scale(x) * norm_first)
    proj = low_back(jnp.einsum('std,cde->cste', xn1, mix_weight, precision=HIGHEST_ACCURACY))
    query_vectors = jax.nn.silu(proj[0])
    forget = lower_bound + (1.0 - lower_bound) * jax.nn.sigmoid(proj[1])
    forget = jnp.where(valid[:, :, None], forget, 1.0)
    logf = jnp.log(forget)
    key_vectors = 1.0 - forget
    value_vectors = proj[2]
    mixed = lax.map(lambda a: recur_slot(a[0], a[1], a[2], a[3]), (to_heads(query_vectors), to_heads(logf), to_heads(key_vectors), to_heads(value_vectors)))
    mixed = mixed.transpose(0, 2, 1, 3)
    normed = (mixed * rms_scale(mixed)).reshape(x.shape)
    gated = low(normed * out_gain * jax.nn.silu(proj[3]))
    branch = low_back(jnp.einsum('std,de->ste', gated, w_out, precision=HIGHEST_ACCURACY))
    hidden = x + branch
    xn2 = low(hidden * rms_scale(hidden) * norm_second)
    gate_up = low_back(jnp.einsum('std,cdf->cstf', xn2, ffn_in, precision=HIGHEST_ACCURACY))
    act = low(jax.nn.silu(gate_up[0]) * gate_up[1])
    ffn = low_back(jnp.einsum('stf,fd->std', act, ffn_out, precision=HIGHEST_ACCURACY))
    return hidden + ffn

def reference(tokens, lengths, norm_first, mix_weight, lower_bound, out_gain, w_out, norm_second, ffn_in, ffn_out, cotangent):
    valid = jnp.arange(SLOT, dtype=jnp.int32)[None, :] < lengths[:, None]

    def run(x, a, b, c, d, e, f, g, h):
        return forward(x, a, b, c, d, e, f, g, h, valid)
    inputs = (tokens, norm_first, mix_weight, lower_bound, out_gain, w_out, norm_second, ffn_in, ffn_out)
    inputs = tuple((a.astype(jnp.float32) for a in inputs))
    result, pullback = jax.vjp(run, *inputs)
    grads = pullback(cotangent.astype(jnp.float32))
    return (result.astype(jnp.bfloat16), grads[0].astype(jnp.bfloat16), grads[1], grads[2], grads[3], grads[4], grads[5], grads[6], grads[7], grads[8])
```

```python
import jax
import jax.numpy as jnp
from jax import lax
from jax.experimental import pallas as pl
from jax.experimental.pallas import tpu as pltpu
from jax.sharding import PartitionSpec as P

HD = 128
EPS = 1e-06
F32 = jnp.float32
BF16 = jnp.bfloat16
MIB = 1 << 20
PACKED = HD + 8

X_SWAP = [(p, p ^ 1) for p in range(8)]
CORE_SWAP = [(h, h ^ 1) for h in range(4)]
Y_SWAP = [(h, h ^ 2) for h in range(4)]


def z_shift(k):
    return [(p, (p + 2 * k) % 8) for p in range(8)]


def z_line(k):
    return [(p, p + 2 * k) for p in range(8) if 0 <= p + 2 * k < 8]


def flip(bit):
    return [(p, p ^ bit) for p in range(8)]


def rms_scale(v):
    return lax.rsqrt(jnp.mean(v * v, axis=-1, keepdims=True) + EPS)


def norm_back(grad_normed, gain, scale, normed_hat):
    scaled = grad_normed * gain
    return scale * (scaled - normed_hat * jnp.mean(scaled * normed_hat, axis=-1, keepdims=True))


def dot(a, b, dims=((1,), (0,))):
    return lax.dot_general(a, b, (dims, ((), ())), preferred_element_type=F32)


NT = ((1,), (1,))
TN = ((0,), (0,))


def sigmoid(v):
    return 1.0 / (1.0 + jnp.exp(-v))


def triangle(kind):
    row = lax.broadcasted_iota(jnp.int32, (HD, HD), 0)
    col = lax.broadcasted_iota(jnp.int32, (HD, HD), 1)
    return {"lower": row >= col, "strict": row > col, "upper": row <= col}[kind]


def exact_dot(ones, v):
    total = None
    for _ in range(3):
        part = v.astype(BF16)
        v = v - part.astype(F32)
        term = dot(ones, part)
        total = term if total is None else total + term
    return total


def valid_rows(pos, length):
    row = lax.broadcasted_iota(jnp.int32, (HD, 1), 0)
    return (pos * HD + row) < length


def open_forget(pre, bound, ok):
    sig = sigmoid(pre)
    return sig, jnp.where(ok, bound + (1.0 - bound) * sig, 1.0)


def project_kernel(pos, lengths, x_ref, gain_ref, w_ref, bound_ref, xn_ref, away_ref, proj_ref, c_ref, qe_ref, ke_ref, intra_ref, sum_ref):
    @pl.when(pl.program_id(0) == 0)
    def _():
        x = x_ref[...].astype(F32)
        xn_ref[...] = (x * rms_scale(x) * gain_ref[...]).astype(BF16)
        n = away_ref.shape[1] // 4
        for z in range(4):
            at = pl.multiple_of((2 * z + 1 - pos[0] % 2) * n, n)
            away_ref[:, pl.ds(z * n, n)] = xn_ref[:, pl.ds(at, n)].astype(F32)

    xn = xn_ref[...]
    for c in range(4):
        proj_ref[c] = dot(xn, w_ref[c])
    slots, heads = sum_ref.shape[:2]
    lower = triangle("lower")
    ones = lower.astype(BF16)
    for s in range(slots):
        rows = pl.ds(s * HD, HD)
        ok = valid_rows(pos[0], lengths[s])
        for h in range(heads):
            cols = pl.ds(h * HD, HD)
            pre_q, pre_f, v = (proj_ref[c, rows, cols] for c in range(3))
            _, forget = open_forget(pre_f, bound_ref[:, cols], ok)
            cum = exact_dot(ones, jnp.log(forget))
            c_ref[rows, cols] = cum
            keys = 1.0 - forget
            qe = (pre_q * sigmoid(pre_q) * jnp.exp(cum)).astype(BF16)
            ke = (keys * jnp.exp(-cum)).astype(BF16)
            qe_ref[rows, cols] = qe
            ke_ref[rows, cols] = ke
            vb = v.astype(BF16)
            scores = jnp.where(lower, dot(qe, ke, NT), 0.0).astype(BF16)
            intra_ref[rows, cols] = dot(scores, vb)
            last = cum[HD - 1 :, :]
            to_end = (keys * jnp.exp(last - cum)).astype(BF16)
            sum_ref[s, h, pl.ds(0, HD), :] = dot(vb, to_end, TN)
            sum_ref[s, h, pl.ds(HD, 8), :] = jnp.broadcast_to(jnp.exp(last), (8, HD))


def split_store(keep_ref, send_ref, core, make):
    half = keep_ref.shape[1]
    keep_ref[...] = make(pl.multiple_of(core * half, half), half)
    send_ref[...] = make(pl.multiple_of((1 - core) * half, half), half)


def mixer_out_kernel(core, qe_ref, state_ref, intra_ref, pre_ref, gain_ref, w_ref, mixed_ref, gated_ref, keep_ref, send_ref):
    slots, heads = state_ref.shape[:2]
    for s in range(slots):
        rows = pl.ds(s * HD, HD)
        for h in range(heads):
            cols = pl.ds(h * HD, HD)
            mixed = intra_ref[rows, cols] + dot(qe_ref[rows, cols], state_ref[s, h].astype(BF16), NT)
            mixed_ref[rows, cols] = mixed
            pre = pre_ref[0, rows, cols]
            gated = mixed * rms_scale(mixed) * gain_ref[:, cols] * (pre * sigmoid(pre))
            gated_ref[rows, cols] = gated.astype(BF16)
    split_store(keep_ref, send_ref, core[0], lambda at, n: dot(gated_ref[...], w_ref[:, pl.ds(at, n)]))


def ffn_unit(xn, dy, w_gate, w_up, w_out):
    gate, up = dot(xn, w_gate), dot(xn, w_up)
    dact = dot(dy, w_out, NT)
    sig = sigmoid(gate)
    swish = gate * sig
    act = (swish * up).astype(BF16)
    dgate = (dact * up * (sig * (1.0 + gate * (1.0 - sig)))).astype(BF16)
    dup = (dact * swish).astype(BF16)
    return act, dgate, dup


def ffn_own_kernel(core, xn_ref, dy_ref, in_ref, in_tail, out_ref, out_tail, f_keep, f_send, d_keep, d_send, f_acc, d_acc):
    step = pl.program_id(0)

    @pl.when(step == 0)
    def _():
        f_acc[...] = jnp.zeros_like(f_acc)
        d_acc[...] = jnp.zeros_like(d_acc)

    def add(w_in, w_out):
        act, dgate, dup = ffn_unit(xn_ref[...], dy_ref[...], w_in[0], w_in[1], w_out[...])
        f_acc[...] += dot(act, w_out[...])
        d_acc[...] += dot(dgate, w_in[0], NT) + dot(dup, w_in[1], NT)

    add(in_ref, out_ref)

    @pl.when(step == pl.num_programs(0) - 1)
    def _():
        add(in_tail, out_tail)
        split_store(f_keep, f_send, core[0], lambda at, n: f_acc[:, pl.ds(at, n)])
        split_store(d_keep, d_send, core[0], lambda at, n: d_acc[:, pl.ds(at, n)])


def widen_kernel(at, a_ref, out_ref):
    n = out_ref.shape[1]
    out_ref[...] = a_ref[:, pl.ds(pl.multiple_of(at[0] * n, n), n)].astype(F32)


def assemble_kernel(at, *refs):
    out_ref = refs[-1]
    for k, piece in enumerate(refs[:-1]):
        n = piece.shape[1]
        out_ref[:, pl.ds(pl.multiple_of(at[k] * n, n), n)] = piece[...].astype(BF16)


def ffn_grad_kernel(rows, xn_ref, xn_line, dy_ref, dy_line, in_ref, in_tail, out_ref, out_tail, in_mine, in_other, out_mine, out_other, tail_in_mine, tail_in_other, tail_out_mine, tail_out_other):
    step = pl.program_id(0)
    n = in_mine.shape[1]
    count = xn_ref.shape[0]

    def put(w_in, w_out, targets):
        blocks = [(xn_ref, dy_ref, pl.ds(0, count))]
        blocks += [(xn_line, dy_line, pl.ds(k * count, count)) for k in range(xn_line.shape[0] // count)]
        for k, (xs, dys, tokens) in enumerate(blocks):
            act, dgate, dup = ffn_unit(xs[tokens, :], dys[tokens, :], w_in[0], w_in[1], w_out[...])
            for which, (gin, gout) in enumerate(targets):
                at = pl.ds(pl.multiple_of(rows[which] * n, n), n)
                x = xs[tokens, at]
                sums = dot(x, dgate, TN), dot(x, dup, TN), dot(act, dys[tokens, at], TN)
                if k == 0:
                    gin[0], gin[1], gout[...] = sums
                else:
                    gin[0] += sums[0]
                    gin[1] += sums[1]
                    gout[...] += sums[2]

    put(in_ref, out_ref, ((in_mine, out_mine), (in_other, out_other)))

    @pl.when(step == pl.num_programs(0) - 1)
    def _():
        put(in_tail, out_tail, ((tail_in_mine, tail_out_mine), (tail_in_other, tail_out_other)))


def mix_grad_kernel(place, xn_ref, xn_got, *refs):
    keep_ref, send_ref = refs[-2:]
    n = keep_ref.shape[2]
    z, x = place[0] // 2, place[0] % 2
    for c in range(keep_ref.shape[0]):
        own, got = refs[2 * c][...].astype(BF16), refs[2 * c + 1][...].astype(BF16)
        for high in range(2):
            for out, low in ((keep_ref, z % 2), (send_ref, 1 - z % 2)):
                row = 2 * high + low
                a = xn_ref[:, pl.ds(pl.multiple_of((2 * row + x) * n, n), n)]
                b = xn_got[:, pl.ds(pl.multiple_of(row * n, n), n)].astype(BF16)
                out[c, high] = dot(a, own, TN) + dot(b, got, TN)


def norm_back_kernel(db_ref, w_ref, mixed_ref, pre_ref, gain_ref, qe_ref, sum_ref, dpre_ref, dm_ref, dgain_ref, back_ref, dg_ref):
    dg_ref[...] = dot(db_ref[...], w_ref[...], NT)
    slots, heads = sum_ref.shape[:2]
    for h in range(heads):
        cols = pl.ds(h * HD, HD)
        gain = gain_ref[:, cols]
        total = jnp.zeros((1, HD), F32)
        for s in range(slots):
            rows = pl.ds(s * HD, HD)
            mixed, pre, dgated = mixed_ref[rows, cols], pre_ref[0, rows, cols], dg_ref[rows, cols]
            scale = rms_scale(mixed)
            hat = mixed * scale
            sig = sigmoid(pre)
            swish = pre * sig
            total += jnp.sum(dgated * hat * swish, axis=0, keepdims=True)
            dpre_ref[rows, cols] = (dgated * hat * gain * (sig * (1.0 + pre * (1.0 - sig)))).astype(BF16).astype(F32)
            dm = norm_back(dgated * swish, gain, scale, hat).astype(BF16)
            dm_ref[rows, cols] = dm
            back_ref[s, h, pl.ds(0, HD), :] = dot(dm, qe_ref[rows, cols], TN)
            back_ref[s, h, pl.ds(HD, 8), :] = sum_ref[s, h, pl.ds(HD, 8), :]
        dgain_ref[:, cols] = total


def intra_back_kernel(dm_ref, qe_ref, ke_ref, proj_ref, c_ref, state_ref, dq_ref, dk_ref, dv_ref, dl_ref):
    slots, heads = state_ref.shape[:2]
    lower = triangle("lower")
    upper = triangle("upper").astype(BF16)
    for s in range(slots):
        rows = pl.ds(s * HD, HD)
        for h in range(heads):
            cols = pl.ds(h * HD, HD)
            dm, qe, ke, cum = (r[rows, cols] for r in (dm_ref, qe_ref, ke_ref, c_ref))
            vb = proj_ref[2, rows, cols].astype(BF16)
            dscores = jnp.where(lower, dot(dm, vb, NT), 0.0).astype(BF16)
            to_q = dot(dscores, ke) + dot(dm, state_ref[s, h].astype(BF16))
            to_k = dot(dscores, qe, TN)
            pre = proj_ref[0, rows, cols]
            sig = sigmoid(pre)
            dq_ref[rows, cols] = (jnp.exp(cum) * to_q * (sig * (1.0 + pre * (1.0 - sig)))).astype(BF16).astype(F32)
            dk_ref[rows, cols] = jnp.exp(-cum) * to_k
            scores = jnp.where(lower, dot(qe, ke, NT), 0.0).astype(BF16)
            dv_ref[rows, cols] = dot(scores, dm, TN)
            dl_ref[rows, cols] = exact_dot(upper, qe.astype(F32) * to_q - ke.astype(F32) * to_k)


def state_back_kernel(pos, lengths, carried_ref, state_ref, ke_ref, forget_ref, value_ref, c_ref, bound_ref, dk_ref, dv_ref, dl_ref, df_ref, dval_ref, dbound_ref):
    slots, heads = state_ref.shape[:2]
    strict = triangle("strict").astype(BF16)
    for h in range(heads):
        cols = pl.ds(h * HD, HD)
        bound = bound_ref[:, cols]
        total = jnp.zeros((1, HD), F32)
        for s in range(slots):
            rows = pl.ds(s * HD, HD)
            ok = valid_rows(pos[0], lengths[s])
            cum, ke = c_ref[rows, cols], ke_ref[rows, cols]
            ending = carried_ref[s, h] * jnp.exp(cum[HD - 1 :, :])
            ending_low = ending.astype(BF16)
            to_k = dot(value_ref[0, rows, cols].astype(BF16), ending_low)
            dval_ref[rows, cols] = (dv_ref[rows, cols] + dot(ke, ending_low, NT)).astype(BF16).astype(F32)
            through = jnp.sum(ending * state_ref[s, h], axis=0, keepdims=True)
            dlogf = dl_ref[rows, cols] + exact_dot(strict, ke.astype(F32) * to_k) + through
            dkeys = dk_ref[rows, cols] + jnp.exp(-cum) * to_k
            sig, forget = open_forget(forget_ref[0, rows, cols], bound, ok)
            dforget = jnp.where(ok, dlogf / forget - dkeys, 0.0)
            total += jnp.sum(dforget * (1.0 - sig), axis=0, keepdims=True)
            df_ref[rows, cols] = (dforget * (1.0 - bound) * sig * (1.0 - sig)).astype(BF16).astype(F32)
        dbound_ref[:, cols] = total


SMEM = pl.BlockSpec(memory_space=pltpu.SMEM)


def whole(shape, *index):
    index = index or (0,) * len(shape)
    return pl.BlockSpec(shape, lambda *_: index)


def sds(shape, dtype=F32):
    return jax.ShapeDtypeStruct(shape, dtype)


def call(kernel, name, outs, in_specs, out_specs, flops, moved, grid=(1,), scratch=(), vmem=48):
    return pl.pallas_call(
        kernel,
        name=name,
        grid=grid,
        out_shape=outs,
        in_specs=in_specs,
        out_specs=out_specs,
        scratch_shapes=list(scratch),
        compiler_params=pltpu.CompilerParams(vmem_limit_bytes=vmem * MIB),
        cost_estimate=pl.CostEstimate(flops=int(flops), bytes_accessed=int(moved), transcendentals=0),
    )


def entering_all(packed, backward):
    count, mine = lax.axis_size("seq"), lax.axis_index("seq")
    pieces = lax.all_gather(packed, "seq")
    if backward:
        pieces, mine = pieces[::-1], count - 1 - mine

    def step(position, state):
        piece = pieces[position]
        longer = piece[:, :, HD : HD + 1] * state + piece[:, :, :HD]
        return jnp.where(position < mine, longer, state)

    return lax.fori_loop(0, count - 1, step, jnp.zeros_like(packed[:, :, :HD]))


def entering_lines(packed, backward):
    shape = packed.shape
    packed = packed.reshape(-1, PACKED, HD)
    half = packed.shape[0] // 2
    is_low = lax.axis_index("seq") % 2 == 0
    first = ~is_low if backward else is_low
    step = -1 if backward else 1
    mine = jnp.where(is_low, packed[:half], packed[half:])
    other = lax.ppermute(jnp.where(is_low, packed[half:], packed[:half]), "seq", X_SWAP)
    early, late = jnp.where(first, mine, other), jnp.where(first, other, mine)

    def decay(a):
        return a[:, HD : HD + 1]

    def state(a):
        return a[:, :HD]

    def join(a, b):
        both = decay(b) * state(a) + state(b)
        return jnp.concatenate([both, jnp.broadcast_to(decay(a) * decay(b), (half, 8, HD))], axis=1)

    pair = join(early, late)
    before = lax.ppermute(pair, "seq", z_line(step))
    further = lax.ppermute(join(before, pair), "seq", z_line(2 * step))
    into_first = decay(before) * state(further) + state(before)
    into_second = decay(early) * into_first + state(early)
    kept = jnp.where(first, into_first, into_second)
    given = lax.ppermute(jnp.where(first, into_second, into_first), "seq", X_SWAP)
    low, high = jnp.where(is_low, kept, given), jnp.where(is_low, given, kept)
    return jnp.concatenate([low, high]).reshape(*shape[:2], HD, HD)


def sum_heads(keep, send, fast):
    if not fast:
        return lax.psum(jnp.concatenate([keep, send], axis=1), "head")
    half = keep + lax.ppermute(send, "head", CORE_SWAP)
    half = half + lax.ppermute(half, "head", Y_SWAP)
    other = lax.ppermute(half, "head", CORE_SWAP)
    low = lax.axis_index("head") % 2 == 0
    return jnp.concatenate([jnp.where(low, half, other), jnp.where(low, other, half)], axis=1)


def gather_line(piece):
    rows, quarter = piece.shape
    head = lax.axis_index("head")
    own = jnp.concatenate([lax.ppermute(piece, "seq", z_shift(k)) for k in (1, 2, 3)])
    over = lax.ppermute(own, "head", Y_SWAP)
    pieces = [own, lax.ppermute(own, "head", CORE_SWAP), over, lax.ppermute(over, "head", CORE_SWAP)]
    return call(
        assemble_kernel,
        "assemble",
        sds((3 * rows, 4 * quarter), BF16),
        [SMEM] + [pl.BlockSpec((rows, quarter), lambda i: (i, 0))] * 4,
        pl.BlockSpec((rows, 4 * quarter), lambda i: (i, 0)),
        0,
        18 * rows * 4 * quarter,
        grid=(3,),
    )(jnp.stack([head ^ k for k in range(4)]).astype(jnp.int32), *pieces)


def sum_line(keep, send, axis):
    high = lax.axis_index("seq") // 4

    def take(a, at):
        return lax.dynamic_index_in_dim(a, at, axis, keepdims=False)

    near = keep + lax.ppermute(send, "seq", flip(2))
    return take(near, high) + lax.ppermute(take(near, 1 - high), "seq", flip(4))


def sum_small(v, fast):
    if not fast:
        return lax.psum(v, "seq")
    for bit in (1, 2, 4):
        v = v + lax.ppermute(v, "seq", flip(bit))
    return v


def body(tokens, lengths, norm_first, mix_weight, lower_bound, out_gain, w_out, norm_second, ffn_in, ffn_out, cotangent):
    slots, length, width = tokens.shape
    count = slots * length
    local = lower_bound.shape[0]
    heads = local // HD
    units = ffn_out.shape[0]
    fast = lax.axis_size("seq") == 8 and lax.axis_size("head") == 4
    entering = entering_lines if fast else entering_all
    seq = lax.axis_index("seq")
    pos = seq.astype(jnp.int32).reshape(1)
    core = (lax.axis_index("head") % 2 if fast else jnp.int32(0)).astype(jnp.int32).reshape(1)
    tokens = tokens.reshape(count, width)
    dy = cotangent.reshape(count, width)
    bound, gain = lower_bound.reshape(1, local), out_gain.reshape(1, local)
    norm_first, norm_second = norm_first.reshape(1, width), norm_second.reshape(1, width)

    pair = 2 * HD
    tall = whole((count, width))
    channel = whole((count, local))
    state_shape = (slots, heads, HD, HD)
    packed_shape = (slots, heads, PACKED, HD)
    state_spec, packed_spec, row_spec = whole(state_shape), whole(packed_shape), whole((1, local))
    w_spec = whole((local, width))
    half_out, half_spec = sds((count, width // 2)), whole((count, width // 2))

    def block(rows):
        return pl.BlockSpec((rows, pair), lambda i: (0, i))

    xn1, xn1_away, proj, cum, qe, ke, intra, packed = call(
        project_kernel,
        "project",
        [sds((count, width), BF16), sds((count, width // 2)), sds((4, count, local)), sds((count, local)), sds((count, local), BF16), sds((count, local), BF16), sds((count, local)), sds(packed_shape)],
        [SMEM, SMEM, tall, whole((1, width)), pl.BlockSpec((4, width, pair), lambda i: (0, 0, i)), block(1)],
        [tall, half_spec, pl.BlockSpec((4, count, pair), lambda i: (0, 0, i)), block(count), block(count), block(count), block(count), pl.BlockSpec((slots, 2, PACKED, HD), lambda i: (0, i, 0, 0))],
        8 * count * width * local,
        20e6,
        grid=(local // pair,),
    )(pos, lengths, tokens, norm_first, mix_weight, bound)

    state = entering(packed, False)

    gate_spec = whole((1, count, local), 3, 0, 0)
    mixed, gated, keep, send = call(
        mixer_out_kernel,
        "mixer_out",
        [sds((count, local)), sds((count, local), BF16), half_out, half_out],
        [SMEM, channel, state_spec, channel, gate_spec, row_spec, w_spec],
        [channel, channel, half_spec, half_spec],
        2 * count * width * local,
        10e6,
    )(core, qe, state, intra, proj, gain, w_out)
    hidden = tokens.astype(F32) + sum_heads(keep, send, fast)
    scale_two = rms_scale(hidden)
    hat_two = hidden * scale_two
    xn2 = (hat_two * norm_second).astype(BF16)

    steps = units // pair
    rest = units - steps * pair
    in_specs = [
        pl.BlockSpec((2, width, pair), lambda i: (0, 0, i)),
        whole((2, width, rest), 0, 0, steps * pair // rest),
        pl.BlockSpec((pair, width), lambda i: (i, 0)),
        whole((rest, width), steps * pair // rest, 0),
    ]
    keep, send, dkeep, dsend = call(
        ffn_own_kernel,
        "ffn_own",
        [half_out] * 4,
        [SMEM, tall, tall, *in_specs],
        [half_spec] * 4,
        12 * count * width * units,
        30e6,
        grid=(steps,),
        scratch=[pltpu.VMEM((count, width), F32)] * 2,
        vmem=60,
    )(core, xn2, dy, ffn_in, ffn_in, ffn_out, ffn_out)
    dxn2 = sum_heads(dkeep, dsend, fast)
    output = (hidden + sum_heads(keep, send, fast)).astype(BF16)
    part_norm_second = jnp.sum(dxn2 * hat_two, axis=0)
    dhidden = dy.astype(F32) + norm_back(dxn2, norm_second, scale_two, hat_two)
    dbranch = dhidden.astype(BF16)

    dpre_gate, dmixed, part_gain, back = call(
        norm_back_kernel,
        "norm_back",
        [sds((count, local)), sds((count, local), BF16), sds((1, local)), sds(packed_shape)],
        [tall, w_spec, channel, gate_spec, row_spec, channel, packed_spec],
        [channel, channel, row_spec, packed_spec],
        2 * count * width * local,
        10e6,
        scratch=[pltpu.VMEM((count, local), F32)],
    )(dbranch, w_out, mixed, proj, gain, qe, packed)

    carried = entering(back, True)

    three, two = whole((3, count, local)), whole((1, count, local), 1, 0, 0)
    dpre_query, dkeys, dvalues, dlogf = call(
        intra_back_kernel,
        "intra_back",
        [sds((count, local))] * 4,
        [channel, channel, channel, three, channel, state_spec],
        [channel] * 4,
        14 * count * local * HD,
        10e6,
    )(dmixed, qe, ke, proj, cum, state)
    dpre_forget, dpre_values, part_bound = call(
        state_back_kernel,
        "state_back",
        [sds((count, local)), sds((count, local)), sds((1, local))],
        [SMEM, SMEM, state_spec, state_spec, channel, two, whole((1, count, local), 2, 0, 0), channel, row_spec, channel, channel, channel],
        [channel, channel, row_spec],
        8 * count * local * HD,
        10e6,
    )(pos, lengths, carried, state, ke, proj, proj, cum, bound, dkeys, dvalues, dlogf)
    dproj = (dpre_query, dpre_forget, dpre_values, dpre_gate)

    x = tokens.astype(F32)
    scale_one = rms_scale(x)
    hat_one = x * scale_one
    dxn1 = sum(dot(d.astype(BF16), mix_weight[c], NT) for c, d in enumerate(dproj))
    if fast:
        at = core[0] * (width // 2)
        keep = lax.dynamic_slice_in_dim(dxn1, at, width // 2, 1)
        send = lax.dynamic_slice_in_dim(dxn1, width // 2 - at, width // 2, 1)
    else:
        keep, send = jnp.split(dxn1, 2, axis=1)
    dxn1 = sum_heads(keep, send, fast)
    part_norm_first = jnp.sum(dxn1 * hat_one, axis=0)
    grad_tokens = (dhidden + norm_back(dxn1, norm_first, scale_one, hat_one)).astype(BF16)

    if fast:
        weights = weight_grads(xn1, xn1_away, dproj, gated, dbranch, xn2, hat_two * norm_second, dy, ffn_in, ffn_out, in_specs, steps)
    else:
        weights = weight_grads_whole(xn1, dproj, gated, dbranch, xn2, dy, ffn_in, ffn_out)
    sizes = (width, width, local, local)
    small = jnp.concatenate([part_norm_first, part_norm_second, part_bound[0], part_gain[0]])
    small = sum_small(small, fast)
    first, second, bound_sum, gain_sum = jnp.split(small, [sum(sizes[: i + 1]) for i in range(3)])
    shape = (slots, length, width)
    return (output.reshape(shape), grad_tokens.reshape(shape), first, weights[0], bound_sum, gain_sum, weights[1], second, weights[2], weights[3])


def weight_grads_whole(xn1, dproj, gated, dbranch, xn2, dy, ffn_in, ffn_out):
    gate, up = dot(xn2, ffn_in[0]), dot(xn2, ffn_in[1])
    dact = dot(dy, ffn_out, NT)
    sig = sigmoid(gate)
    swish = gate * sig
    act = (swish * up).astype(BF16)
    dgate = (dact * up * (sig * (1.0 + gate * (1.0 - sig)))).astype(BF16)
    dup = (dact * swish).astype(BF16)

    def scatter(a, axis):
        return lax.psum_scatter(a, "seq", scatter_dimension=axis, tiled=True)

    return (
        jnp.stack([scatter(dot(xn1, d.astype(BF16), TN), 0) for d in dproj]),
        scatter(dot(gated, dbranch, TN), 1),
        jnp.stack([scatter(dot(xn2, d, TN), 0) for d in (dgate, dup)]),
        scatter(dot(act, dy, TN), 1),
    )


def weight_grads(xn1, xn1_away, dproj, gated, dbranch, xn2, xn2_wide, dy, ffn_in, ffn_out, in_specs, steps):
    count, width = xn1.shape
    units = ffn_out.shape[0]
    local = gated.shape[1]
    n = width // 8
    seq, head = lax.axis_index("seq"), lax.axis_index("head")
    x, z = seq % 2, seq // 2
    place = seq.astype(jnp.int32).reshape(1)
    tall, channel = whole((count, width)), whole((count, local))

    def swap(a):
        return lax.ppermute(a, "seq", X_SWAP)

    xn1_got = swap(xn1_away)

    def mix_pair(*grads):
        shape = (len(grads), 2, n, local)
        keep, send = call(
            mix_grad_kernel,
            "mix_grad",
            [sds(shape)] * 2,
            [SMEM, tall, whole((count, width // 2))] + [channel] * (2 * len(grads)),
            [whole(shape)] * 2,
            2 * len(grads) * 2 * count * width // 2 * local,
            10e6,
        )(place, xn1, xn1_got, *(a for d in grads for a in (d, swap(d))))
        return sum_line(keep, send, 1)

    early, late = mix_pair(dproj[0], dproj[3]), mix_pair(dproj[1], dproj[2])
    mix = jnp.stack([early[0], late[0], late[1], early[1]])

    blocks = dbranch.reshape(count, 2, 2, 2, n)

    def columns(at):
        return jnp.einsum("td,thln->lhdn", gated, lax.dynamic_index_in_dim(blocks, at, 3, keepdims=False), preferred_element_type=F32)

    two = columns(x) + swap(columns(1 - x))
    keep, send = (lax.dynamic_index_in_dim(two, at, 0, keepdims=False) for at in (z % 2, 1 - z % 2))
    grad_w_out = sum_line(keep, send, 0)

    quarter = width // 4
    dy_wide = call(widen_kernel, "widen", sds((count, quarter)), [SMEM, tall], whole((count, quarter)), 0, 4e6)(
        head.astype(jnp.int32).reshape(1), dy
    )
    dy_line = gather_line(dy_wide)
    xn_line = gather_line(lax.dynamic_slice_in_dim(xn2_wide, head * quarter, quarter, 1))
    pair = 2 * HD
    rest = units - steps * pair
    line = whole(xn_line.shape)
    rows = jnp.stack([seq, seq ^ 1]).astype(jnp.int32)
    main = steps * pair
    outs = [sds((2, n, main))] * 2 + [sds((main, n))] * 2 + [sds((2, n, rest))] * 2 + [sds((rest, n))] * 2
    gin, gout = pl.BlockSpec((2, n, pair), lambda i: (0, 0, i)), pl.BlockSpec((pair, n), lambda i: (i, 0))
    got = call(
        ffn_grad_kernel,
        "ffn_grad",
        outs,
        [SMEM, tall, line, tall, line, *in_specs],
        [gin, gin, gout, gout] + [whole(o.shape) for o in outs[4:]],
        6 * 4 * count * width * units + 6 * 4 * count * 2 * n * units,
        40e6,
        grid=(steps,),
        vmem=60,
    )(rows, xn2, xn_line, dy, dy_line, ffn_in, ffn_in, ffn_out, ffn_out)
    in_mine, in_other, out_mine, out_other, tin_mine, tin_other, tout_mine, tout_other = got

    def finish(mine, other):
        return mine + lax.ppermute(other, "seq", X_SWAP)

    grad_in = jnp.concatenate([finish(in_mine, in_other), finish(tin_mine, tin_other)], axis=2)
    grad_out = jnp.concatenate([finish(out_mine, out_other), finish(tout_mine, tout_other)], axis=0)
    return mix, grad_w_out, grad_in, grad_out


def solution(mesh):
    in_specs = (
        P(None, "seq", None),
        P(),
        P(),
        P(None, None, "head"),
        P("head"),
        P("head"),
        P("head", None),
        P(),
        P(None, None, "head"),
        P("head", None),
        P(None, "seq", None),
    )
    out_specs = (
        P(None, "seq", None),
        P(None, "seq", None),
        P(),
        P(None, "seq", "head"),
        P("head"),
        P("head"),
        P("head", "seq"),
        P(),
        P(None, "seq", "head"),
        P("head", "seq"),
    )
    return jax.shard_map(body, mesh=mesh, in_specs=in_specs, out_specs=out_specs, check_vma=False)
```

```python
import functools

import jax
import jax.numpy as jnp
from jax import lax
from jax.experimental import pallas as pl
from jax.experimental.pallas import tpu as pltpu
from jax.sharding import PartitionSpec as P

HD = 128
EPS = 1e-06
F32 = jnp.float32
BF16 = jnp.bfloat16
MIB = 1 << 20
PACKED = HD + 8

X_SWAP = [(p, p ^ 1) for p in range(8)]
CORE_SWAP = [(h, h ^ 1) for h in range(4)]
Y_SWAP = [(h, h ^ 2) for h in range(4)]


def z_shift(k):
    return [(p, (p + 2 * k) % 8) for p in range(8)]


def z_line(k):
    return [(p, p + 2 * k) for p in range(8) if 0 <= p + 2 * k < 8]


def flip(bit):
    return [(p, p ^ bit) for p in range(8)]


def rms_scale(v):
    return lax.rsqrt(jnp.mean(v * v, axis=-1, keepdims=True) + EPS)


def norm_back(grad_normed, gain, scale, normed_hat):
    scaled = grad_normed * gain
    return scale * (scaled - normed_hat * jnp.mean(scaled * normed_hat, axis=-1, keepdims=True))


def dot(a, b, dims=((1,), (0,))):
    return lax.dot_general(a, b, (dims, ((), ())), preferred_element_type=F32)


NT = ((1,), (1,))
TN = ((0,), (0,))


def sigmoid(v):
    return 1.0 / (1.0 + jnp.exp(-v))


def triangle(kind):
    row = lax.broadcasted_iota(jnp.int32, (HD, HD), 0)
    col = lax.broadcasted_iota(jnp.int32, (HD, HD), 1)
    return {"lower": row >= col, "strict": row > col, "upper": row <= col}[kind]


def exact_dot(ones, v):
    total = None
    for _ in range(3):
        part = v.astype(BF16)
        v = v - part.astype(F32)
        term = dot(ones, part)
        total = term if total is None else total + term
    return total


def valid_rows(pos, length):
    row = lax.broadcasted_iota(jnp.int32, (HD, 1), 0)
    return (pos * HD + row) < length


def open_forget(pre, bound, ok):
    sig = sigmoid(pre)
    return sig, jnp.where(ok, bound + (1.0 - bound) * sig, 1.0)


def project_kernel(pos, lengths, x_ref, gain_ref, w_ref, bound_ref, xn_ref, away_ref, proj_ref, c_ref, qe_ref, ke_ref, intra_ref, sum_ref):
    @pl.when(pl.program_id(0) == 0)
    def _():
        x = x_ref[...].astype(F32)
        xn_ref[...] = (x * rms_scale(x) * gain_ref[...]).astype(BF16)
        n = away_ref.shape[1] // 4
        for z in range(4):
            at = pl.multiple_of((2 * z + 1 - pos[0] % 2) * n, n)
            away_ref[:, pl.ds(z * n, n)] = xn_ref[:, pl.ds(at, n)].astype(F32)

    xn = xn_ref[...]
    for c in range(4):
        proj_ref[c] = dot(xn, w_ref[c])
    slots, heads = sum_ref.shape[:2]
    lower = triangle("lower")
    ones = lower.astype(BF16)
    for s in range(slots):
        rows = pl.ds(s * HD, HD)
        ok = valid_rows(pos[0], lengths[s])
        for h in range(heads):
            cols = pl.ds(h * HD, HD)
            pre_q, pre_f, v = (proj_ref[c, rows, cols] for c in range(3))
            _, forget = open_forget(pre_f, bound_ref[:, cols], ok)
            cum = exact_dot(ones, jnp.log(forget))
            c_ref[rows, cols] = cum
            keys = 1.0 - forget
            qe = (pre_q * sigmoid(pre_q) * jnp.exp(cum)).astype(BF16)
            ke = (keys * jnp.exp(-cum)).astype(BF16)
            qe_ref[rows, cols] = qe
            ke_ref[rows, cols] = ke
            vb = v.astype(BF16)
            scores = jnp.where(lower, dot(qe, ke, NT), 0.0).astype(BF16)
            intra_ref[rows, cols] = dot(scores, vb)
            last = cum[HD - 1 :, :]
            to_end = (keys * jnp.exp(last - cum)).astype(BF16)
            sum_ref[s, h, pl.ds(0, HD), :] = dot(vb, to_end, TN)
            sum_ref[s, h, pl.ds(HD, 8), :] = jnp.broadcast_to(jnp.exp(last), (8, HD))


def split_store(keep_ref, send_ref, core, make):
    half = keep_ref.shape[1]
    keep_ref[...] = make(pl.multiple_of(core * half, half), half)
    send_ref[...] = make(pl.multiple_of((1 - core) * half, half), half)


def mixer_out_kernel(core, qe_ref, state_ref, intra_ref, pre_ref, gain_ref, w_ref, mixed_ref, gated_ref, wide_ref, keep_ref, send_ref):
    slots, heads = state_ref.shape[:2]
    for s in range(slots):
        rows = pl.ds(s * HD, HD)
        for h in range(heads):
            cols = pl.ds(h * HD, HD)
            mixed = intra_ref[rows, cols] + dot(qe_ref[rows, cols], state_ref[s, h].astype(BF16), NT)
            mixed_ref[rows, cols] = mixed
            pre = pre_ref[0, rows, cols]
            gated = mixed * rms_scale(mixed) * gain_ref[:, cols] * (pre * sigmoid(pre))
            gated_ref[rows, cols] = gated.astype(BF16)
            wide_ref[rows, cols] = gated_ref[rows, cols].astype(F32)
    split_store(keep_ref, send_ref, core[0], lambda at, n: dot(gated_ref[...], w_ref[:, pl.ds(at, n)]))


def ffn_unit(xn, dy, w_gate, w_up, w_out):
    gate, up = dot(xn, w_gate), dot(xn, w_up)
    dact = dot(dy, w_out, NT)
    sig = sigmoid(gate)
    swish = gate * sig
    act = (swish * up).astype(BF16)
    dgate = (dact * up * (sig * (1.0 + gate * (1.0 - sig)))).astype(BF16)
    dup = (dact * swish).astype(BF16)
    return act, dgate, dup


def ffn_own_kernel(core, xn_ref, dy_ref, in_ref, out_ref, in_tail, out_tail, f_keep, f_send, d_keep, d_send, f_acc, d_acc):
    step = pl.program_id(0)

    @pl.when(step == 0)
    def _():
        f_acc[...] = jnp.zeros_like(f_acc)
        d_acc[...] = jnp.zeros_like(d_acc)

    def add(w_in, w_out):
        act, dgate, dup = ffn_unit(xn_ref[...], dy_ref[...], w_in[0], w_in[1], w_out[...])
        f_acc[...] += dot(act, w_out[...])
        d_acc[...] += dot(dgate, w_in[0], NT) + dot(dup, w_in[1], NT)

    add(in_ref, out_ref)

    @pl.when(step == pl.num_programs(0) - 1)
    def _():
        add(in_tail, out_tail)
        split_store(f_keep, f_send, core[0], lambda at, n: f_acc[:, pl.ds(at, n)])
        split_store(d_keep, d_send, core[0], lambda at, n: d_acc[:, pl.ds(at, n)])


def widen_kernel(at, a_ref, out_ref):
    n = out_ref.shape[1]
    out_ref[...] = a_ref[:, pl.ds(pl.multiple_of(at[0] * n, n), n)].astype(F32)


def assemble_kernel(at, *refs):
    out_ref = refs[-1]
    for k, piece in enumerate(refs[:-1]):
        n = piece.shape[1]
        out_ref[:, pl.ds(pl.multiple_of(at[k], n), n)] = piece[...].astype(BF16)


def ffn_grad_kernel(lines, tail, rows, *refs):
    step = pl.program_id(0)
    tokens, refs = refs[: 2 * lines], refs[2 * lines :]
    weights, outs = (refs[:4], refs[4:]) if tail else (refs[:2], refs[2:])
    n = outs[0].shape[1]

    def put(w_in, w_out, targets):
        for k in range(lines):
            xs, dys = tokens[2 * k], tokens[2 * k + 1]
            act, dgate, dup = ffn_unit(xs[...], dys[...], w_in[0], w_in[1], w_out[...])
            for which in range(2):
                gin, gout = targets[which], targets[2 + which]
                at = pl.ds(pl.multiple_of(rows[which] * n, n), n)
                x = xs[:, at]
                sums = dot(x, dgate, TN), dot(x, dup, TN), dot(act, dys[:, at], TN)
                if k == 0:
                    gin[0], gin[1], gout[...] = sums
                else:
                    gin[0] += sums[0]
                    gin[1] += sums[1]
                    gout[...] += sums[2]

    put(weights[0], weights[1], outs[:4])
    if tail:

        @pl.when(step == pl.num_programs(0) - 1)
        def _():
            put(weights[2], weights[3], outs[4:])


def mix_grad_kernel(turned, place, xn_ref, xn_got, *refs):
    keep_ref, send_ref = refs[-2:]
    n = xn_ref.shape[1] // 8
    z, x = place[0] // 2, place[0] % 2
    for c in range(keep_ref.shape[0]):
        own, got = refs[2 * c][...].astype(BF16), refs[2 * c + 1][...].astype(BF16)
        for high in range(2):
            for out, low in ((keep_ref, z % 2), (send_ref, 1 - z % 2)):
                row = 2 * high + low
                a = xn_ref[:, pl.ds(pl.multiple_of((2 * row + x) * n, n), n)]
                b = xn_got[:, pl.ds(pl.multiple_of(row * n, n), n)].astype(BF16)
                out[c, high] = dot(own, a, TN) + dot(got, b, TN) if turned else dot(a, own, TN) + dot(b, got, TN)


def norm_back_kernel(db_ref, w_ref, mixed_ref, pre_ref, gain_ref, qe_ref, sum_ref, dpre_ref, dm_ref, dgain_ref, back_ref, dg_ref):
    dg_ref[...] = dot(db_ref[...], w_ref[...], NT)
    slots, heads = sum_ref.shape[:2]
    for h in range(heads):
        cols = pl.ds(h * HD, HD)
        gain = gain_ref[:, cols]
        total = jnp.zeros((1, HD), F32)
        for s in range(slots):
            rows = pl.ds(s * HD, HD)
            mixed, pre, dgated = mixed_ref[rows, cols], pre_ref[0, rows, cols], dg_ref[rows, cols]
            scale = rms_scale(mixed)
            hat = mixed * scale
            sig = sigmoid(pre)
            swish = pre * sig
            total += jnp.sum(dgated * hat * swish, axis=0, keepdims=True)
            dpre_ref[rows, cols] = (dgated * hat * gain * (sig * (1.0 + pre * (1.0 - sig)))).astype(BF16).astype(F32)
            dm = norm_back(dgated * swish, gain, scale, hat).astype(BF16)
            dm_ref[rows, cols] = dm
            back_ref[s, h, pl.ds(0, HD), :] = dot(dm, qe_ref[rows, cols], TN)
            back_ref[s, h, pl.ds(HD, 8), :] = sum_ref[s, h, pl.ds(HD, 8), :]
        dgain_ref[:, cols] = total


def intra_back_kernel(dm_ref, qe_ref, ke_ref, proj_ref, c_ref, state_ref, dq_ref, dk_ref, dv_ref, dl_ref):
    slots, heads = state_ref.shape[:2]
    lower = triangle("lower")
    upper = triangle("upper").astype(BF16)
    for s in range(slots):
        rows = pl.ds(s * HD, HD)
        for h in range(heads):
            cols = pl.ds(h * HD, HD)
            dm, qe, ke, cum = (r[rows, cols] for r in (dm_ref, qe_ref, ke_ref, c_ref))
            vb = proj_ref[2, rows, cols].astype(BF16)
            dscores = jnp.where(lower, dot(dm, vb, NT), 0.0).astype(BF16)
            to_q = dot(dscores, ke) + dot(dm, state_ref[s, h].astype(BF16))
            to_k = dot(dscores, qe, TN)
            pre = proj_ref[0, rows, cols]
            sig = sigmoid(pre)
            dq_ref[rows, cols] = (jnp.exp(cum) * to_q * (sig * (1.0 + pre * (1.0 - sig)))).astype(BF16).astype(F32)
            dk_ref[rows, cols] = jnp.exp(-cum) * to_k
            scores = jnp.where(lower, dot(qe, ke, NT), 0.0).astype(BF16)
            dv_ref[rows, cols] = dot(scores, dm, TN)
            dl_ref[rows, cols] = exact_dot(upper, qe.astype(F32) * to_q - ke.astype(F32) * to_k)


def state_back_kernel(pos, lengths, carried_ref, state_ref, ke_ref, forget_ref, value_ref, c_ref, bound_ref, dk_ref, dv_ref, dl_ref, df_ref, dval_ref, dbound_ref):
    slots, heads = state_ref.shape[:2]
    strict = triangle("strict").astype(BF16)
    for h in range(heads):
        cols = pl.ds(h * HD, HD)
        bound = bound_ref[:, cols]
        total = jnp.zeros((1, HD), F32)
        for s in range(slots):
            rows = pl.ds(s * HD, HD)
            ok = valid_rows(pos[0], lengths[s])
            cum, ke = c_ref[rows, cols], ke_ref[rows, cols]
            ending = carried_ref[s, h] * jnp.exp(cum[HD - 1 :, :])
            ending_low = ending.astype(BF16)
            to_k = dot(value_ref[0, rows, cols].astype(BF16), ending_low)
            dval_ref[rows, cols] = (dv_ref[rows, cols] + dot(ke, ending_low, NT)).astype(BF16).astype(F32)
            through = jnp.sum(ending * state_ref[s, h], axis=0, keepdims=True)
            dlogf = dl_ref[rows, cols] + exact_dot(strict, ke.astype(F32) * to_k) + through
            dkeys = dk_ref[rows, cols] + jnp.exp(-cum) * to_k
            sig, forget = open_forget(forget_ref[0, rows, cols], bound, ok)
            dforget = jnp.where(ok, dlogf / forget - dkeys, 0.0)
            total += jnp.sum(dforget * (1.0 - sig), axis=0, keepdims=True)
            df_ref[rows, cols] = (dforget * (1.0 - bound) * sig * (1.0 - sig)).astype(BF16).astype(F32)
        dbound_ref[:, cols] = total


SMEM = pl.BlockSpec(memory_space=pltpu.SMEM)


def whole(shape, *index):
    index = index or (0,) * len(shape)
    return pl.BlockSpec(shape, lambda *_: index)


def sds(shape, dtype=F32):
    return jax.ShapeDtypeStruct(shape, dtype)


def call(kernel, name, outs, in_specs, out_specs, flops, moved, grid=(1,), scratch=(), vmem=48):
    return pl.pallas_call(
        kernel,
        name=name,
        grid=grid,
        out_shape=outs,
        in_specs=in_specs,
        out_specs=out_specs,
        scratch_shapes=list(scratch),
        compiler_params=pltpu.CompilerParams(vmem_limit_bytes=vmem * MIB),
        cost_estimate=pl.CostEstimate(flops=int(flops), bytes_accessed=int(moved), transcendentals=0),
    )


def entering_all(packed, backward):
    count, mine = lax.axis_size("seq"), lax.axis_index("seq")
    pieces = lax.all_gather(packed, "seq")
    if backward:
        pieces, mine = pieces[::-1], count - 1 - mine

    def step(position, state):
        piece = pieces[position]
        longer = piece[:, :, HD : HD + 1] * state + piece[:, :, :HD]
        return jnp.where(position < mine, longer, state)

    return lax.fori_loop(0, count - 1, step, jnp.zeros_like(packed[:, :, :HD]))


def decay(a):
    return a[:, HD : HD + 1]


def state(a):
    return a[:, :HD]


def join(a, b):
    both = decay(b) * state(a) + state(b)
    return jnp.concatenate([both, jnp.broadcast_to(decay(a) * decay(b), (a.shape[0], 8, HD))], axis=1)


def is_first(backward):
    is_low = lax.axis_index("seq") % 2 == 0
    return is_low, (~is_low if backward else is_low)


def pair_states(packed, backward):
    packed = packed.reshape(-1, PACKED, HD)
    half = packed.shape[0] // 2
    is_low, first = is_first(backward)
    mine = jnp.where(is_low, packed[:half], packed[half:])
    other = lax.ppermute(jnp.where(is_low, packed[half:], packed[:half]), "seq", X_SWAP)
    return jnp.where(first, mine, other), jnp.where(first, other, mine)


def pass_states(pair, backward):
    step = -1 if backward else 1
    before = lax.ppermute(pair, "seq", z_line(step))
    further = lax.ppermute(join(before, pair), "seq", z_line(2 * step))
    return decay(before) * state(further) + state(before)


def enter_states(early, into_first, shape, backward):
    is_low, first = is_first(backward)
    into_second = decay(early) * into_first + state(early)
    kept = jnp.where(first, into_first, into_second)
    given = lax.ppermute(jnp.where(first, into_second, into_first), "seq", X_SWAP)
    low, high = jnp.where(is_low, kept, given), jnp.where(is_low, given, kept)
    return jnp.concatenate([low, high]).reshape(shape)


def tie(*values):
    return lax.optimization_barrier(values)


def core_swap(a):
    return lax.ppermute(a, "head", CORE_SWAP)


def y_swap(a):
    return lax.ppermute(a, "head", Y_SWAP)


def x_swap(a):
    return lax.ppermute(a, "seq", X_SWAP)


def join_halves(half):
    other = core_swap(half)
    low = lax.axis_index("head") % 2 == 0
    return jnp.concatenate([jnp.where(low, half, other), jnp.where(low, other, half)], axis=1)


def assemble(pieces, width):
    head = lax.axis_index("head")
    arrays, at = [], []
    for own, over, offset in pieces:
        for k, a in enumerate((own, core_swap(own), over, core_swap(over))):
            arrays.append(a)
            at.append((head ^ k) * (width // 4) + offset)
    tokens = arrays[0].shape[0]
    step = tokens // 3
    return call(
        assemble_kernel,
        "assemble",
        sds((tokens, width), BF16),
        [SMEM] + [pl.BlockSpec((step, a.shape[1]), lambda i: (i, 0)) for a in arrays],
        pl.BlockSpec((step, width), lambda i: (i, 0)),
        0,
        6 * tokens * width,
        grid=(3,),
    )(jnp.stack(at).astype(jnp.int32), *arrays)


class Calls:
    def __init__(self, slots, length, width, local, units):
        self.slots, self.count, self.width, self.local, self.units = slots, slots * length, width, local, units
        self.heads = local // HD
        self.pair = 2 * HD
        self.steps = units // self.pair
        self.rest = units - self.steps * self.pair
        self.tall, self.channel = whole((self.count, width)), whole((self.count, local))
        self.row, self.w_spec = whole((1, local)), whole((local, width))
        self.half, self.half_spec = sds((self.count, width // 2)), whole((self.count, width // 2))
        self.state_shape = (slots, self.heads, HD, HD)
        self.packed_shape = (slots, self.heads, PACKED, HD)
        self.state_spec, self.packed_spec = whole(self.state_shape), whole(self.packed_shape)
        self.low = sds((self.count, local), BF16)
        self.full = sds((self.count, local))

    def proj(self, *index):
        return whole((1, self.count, self.local), *index)

    def project(self, pos, lengths, tokens, norm, weight, bound):
        count, width, local, pair = self.count, self.width, self.local, self.pair
        block = pl.BlockSpec((count, pair), lambda i: (0, i))
        return call(
            project_kernel,
            "project",
            [sds((count, width), BF16), self.half, sds((4, count, local)), self.full, self.low, self.low, self.full, sds(self.packed_shape)],
            [SMEM, SMEM, self.tall, whole((1, width)), pl.BlockSpec((4, width, pair), lambda i: (0, 0, i)), pl.BlockSpec((1, pair), lambda i: (0, i))],
            [self.tall, self.half_spec, pl.BlockSpec((4, count, pair), lambda i: (0, 0, i))] + [block] * 4 + [pl.BlockSpec((self.slots, 2, PACKED, HD), lambda i: (0, i, 0, 0))],
            8 * count * width * local,
            20e6,
            grid=(local // pair,),
        )(pos, lengths, tokens, norm, weight, bound)

    def mixer_out(self, core, qe, states, intra, proj, gain, weight):
        return call(
            mixer_out_kernel,
            "mixer_out",
            [self.full, self.low, self.full, self.half, self.half],
            [SMEM, self.channel, self.state_spec, self.channel, self.proj(3, 0, 0), self.row, self.w_spec],
            [self.channel] * 3 + [self.half_spec] * 2,
            2 * self.count * self.width * self.local,
            10e6,
        )(core, qe, states, intra, proj, gain, weight)

    def ffn_specs(self, first=0, tail=True):
        width, pair, rest = self.width, self.pair, self.rest
        last = self.steps * pair // rest
        specs = [
            pl.BlockSpec((2, width, pair), lambda i: (0, 0, i + first)),
            pl.BlockSpec((pair, width), lambda i: (i + first, 0)),
            whole((2, width, rest), 0, 0, last),
            whole((rest, width), last, 0),
        ]
        return specs if tail else specs[:2]

    def ffn_own(self, core, xn2, dy, ffn_in, ffn_out):
        return call(
            ffn_own_kernel,
            "ffn_own",
            [self.half] * 4,
            [SMEM, self.tall, self.tall, *self.ffn_specs()],
            [self.half_spec] * 4,
            12 * self.count * self.width * self.units,
            30e6,
            grid=(self.steps,),
            scratch=[pltpu.VMEM((self.count, self.width), F32)] * 2,
            vmem=60,
        )(core, xn2, dy, ffn_in, ffn_out, ffn_in, ffn_out)

    def norm_back(self, dbranch, weight, mixed, proj, gain, qe, packed):
        return call(
            norm_back_kernel,
            "norm_back",
            [self.full, self.low, sds((1, self.local)), sds(self.packed_shape)],
            [self.tall, self.w_spec, self.channel, self.proj(3, 0, 0), self.row, self.channel, self.packed_spec],
            [self.channel, self.channel, self.row, self.packed_spec],
            2 * self.count * self.width * self.local,
            10e6,
            scratch=[pltpu.VMEM((self.count, self.local), F32)],
        )(dbranch, weight, mixed, proj, gain, qe, packed)

    def intra_back(self, dmixed, qe, ke, proj, cum, states):
        return call(
            intra_back_kernel,
            "intra_back",
            [self.full] * 4,
            [self.channel, self.channel, self.channel, whole((3, self.count, self.local)), self.channel, self.state_spec],
            [self.channel] * 4,
            14 * self.count * self.local * HD,
            10e6,
        )(dmixed, qe, ke, proj, cum, states)

    def state_back(self, pos, lengths, carried, states, ke, proj, cum, bound, dkeys, dvalues, dlogf):
        return call(
            state_back_kernel,
            "state_back",
            [self.full, self.full, sds((1, self.local))],
            [SMEM, SMEM, self.state_spec, self.state_spec, self.channel, self.proj(1, 0, 0), self.proj(2, 0, 0), self.channel, self.row] + [self.channel] * 3,
            [self.channel, self.channel, self.row],
            8 * self.count * self.local * HD,
            10e6,
        )(pos, lengths, carried, states, ke, proj, proj, cum, bound, dkeys, dvalues, dlogf)

    def widen(self, head, dy):
        quarter = self.width // 4
        return call(widen_kernel, "widen", sds((self.count, quarter)), [SMEM, self.tall], whole((self.count, quarter)), 0, 4e6)(head, dy)

    def mix_grad(self, place, xn, xn_got, *grads, turned=False):
        n = self.width // 8
        shape = (len(grads) // 2, 2, *((self.local, n) if turned else (n, self.local)))
        return call(
            functools.partial(mix_grad_kernel, turned),
            "mix_grad",
            [sds(shape)] * 2,
            [SMEM, self.tall, self.half_spec] + [self.channel] * len(grads),
            [whole(shape)] * 2,
            len(grads) * self.count * self.width * self.local,
            10e6,
        )(place, xn, xn_got, *grads)

    def ffn_grad(self, rows, lines, ffn_in, ffn_out, first, steps):
        n, pair, rest = self.width // 8, self.pair, self.rest
        tail = first + steps == self.steps and rest > 0
        main = steps * pair
        outs = [sds((2, n, main))] * 2 + [sds((main, n))] * 2
        gin, gout = pl.BlockSpec((2, n, pair), lambda i: (0, 0, i)), pl.BlockSpec((pair, n), lambda i: (i, 0))
        specs = [gin, gin, gout, gout]
        if tail:
            outs += [sds((2, n, rest))] * 2 + [sds((rest, n))] * 2
            specs += [whole(o.shape) for o in outs[4:]]
        tokens = [a for line in lines for a in line]
        return call(
            functools.partial(ffn_grad_kernel, len(lines), tail),
            "ffn_grad",
            outs,
            [SMEM] + [self.tall] * len(tokens) + self.ffn_specs(first, tail),
            specs,
            6 * len(lines) * self.count * (self.width + 2 * n) * (main + rest * tail),
            20e6,
            grid=(steps,),
            vmem=60,
        )(rows, *tokens, *([ffn_in, ffn_out] * (2 if tail else 1)))


def scalar(v):
    return jnp.asarray(v, jnp.int32).reshape(1)


def body(tokens, lengths, norm_first, mix_weight, lower_bound, out_gain, w_out, norm_second, ffn_in, ffn_out, cotangent):
    shape = tokens.shape
    slots, length, width = shape
    local = lower_bound.shape[0]
    do = Calls(slots, length, width, local, ffn_out.shape[0])
    fast = lax.axis_size("seq") == 8 and lax.axis_size("head") == 4
    run = run_lines if fast else run_any
    output, grad_tokens, small, weights = run(
        do,
        tokens.reshape(do.count, width),
        lengths,
        norm_first.reshape(1, width),
        mix_weight,
        lower_bound.reshape(1, local),
        out_gain.reshape(1, local),
        w_out,
        norm_second.reshape(1, width),
        ffn_in,
        ffn_out,
        cotangent.reshape(do.count, width),
    )
    first, second = small[:width], small[width : 2 * width]
    bound_sum, gain_sum = small[2 * width : 2 * width + local], small[2 * width + local :]
    return (output.reshape(shape), grad_tokens.reshape(shape), first, weights[0], bound_sum, gain_sum, weights[1], second, weights[2], weights[3])


def second_norm(tokens, branch, gain):
    hidden = tokens.astype(F32) + branch
    scale = rms_scale(hidden)
    hat = hidden * scale
    return hidden, scale, hat, hat * gain


def run_any(do, tokens, lengths, norm_first, mix_weight, bound, gain, w_out, norm_second, ffn_in, ffn_out, dy):
    def total(keep, send):
        return lax.psum(jnp.concatenate([keep, send], axis=1), "head")

    pos, core = scalar(lax.axis_index("seq")), scalar(0)
    xn1, _, proj, cum, qe, ke, intra, packed = do.project(pos, lengths, tokens, norm_first, mix_weight, bound)
    states = entering_all(packed, False)
    mixed, gated, _, keep, send = do.mixer_out(core, qe, states, intra, proj, gain, w_out)
    hidden, scale_two, hat_two, wide = second_norm(tokens, total(keep, send), norm_second)
    xn2 = wide.astype(BF16)
    keep, send, dkeep, dsend = do.ffn_own(core, xn2, dy, ffn_in, ffn_out)
    dxn2 = total(dkeep, dsend)
    output = (hidden + total(keep, send)).astype(BF16)
    part_norm_second = jnp.sum(dxn2 * hat_two, axis=0)
    dhidden = dy.astype(F32) + norm_back(dxn2, norm_second, scale_two, hat_two)
    dbranch = dhidden.astype(BF16)
    dpre_gate, dmixed, part_gain, back = do.norm_back(dbranch, w_out, mixed, proj, gain, qe, packed)
    carried = entering_all(back, True)
    dpre_query, dkeys, dvalues, dlogf = do.intra_back(dmixed, qe, ke, proj, cum, states)
    dpre_forget, dpre_values, part_bound = do.state_back(pos, lengths, carried, states, ke, proj, cum, bound, dkeys, dvalues, dlogf)
    dproj = (dpre_query, dpre_forget, dpre_values, dpre_gate)
    x = tokens.astype(F32)
    scale_one = rms_scale(x)
    hat_one = x * scale_one
    dxn1 = lax.psum(sum(dot(d.astype(BF16), mix_weight[c], NT) for c, d in enumerate(dproj)), "head")
    part_norm_first = jnp.sum(dxn1 * hat_one, axis=0)
    grad_tokens = (dhidden + norm_back(dxn1, norm_first, scale_one, hat_one)).astype(BF16)
    weights = weight_grads_whole(xn1, dproj, gated, dbranch, xn2, dy, ffn_in, ffn_out)
    small = lax.psum(jnp.concatenate([part_norm_first, part_norm_second, part_bound[0], part_gain[0]]), "seq")
    return output, grad_tokens, small, weights


def run_lines(do, tokens, lengths, norm_first, mix_weight, bound, gain, w_out, norm_second, ffn_in, ffn_out, dy):
    width, local, quarter = do.width, do.local, do.width // 4
    seq, head = lax.axis_index("seq"), lax.axis_index("head")
    x, z = seq % 2, seq // 2
    place, core = scalar(seq), scalar(head % 2)

    def shift(a, k):
        return lax.ppermute(a, "seq", z_shift(k))

    def head_quarter(a):
        n = a.shape[1] // 4
        return lax.dynamic_slice_in_dim(a, head * n, n, 1)

    dy_quarter = do.widen(scalar(head), dy)
    dy_left, dy_right = jnp.split(dy_quarter, 2, axis=1)
    dy1, dy3a = shift(dy_quarter, 1), shift(dy_left, 3)
    xn1, xn1_away, proj, cum, qe, ke, intra, packed = do.project(place, lengths, tokens, norm_first, mix_weight, bound)
    early, late = pair_states(packed, False)
    early, late, dy1, dy3a = tie(early, late, dy1, dy3a)

    into = pass_states(join(early, late), False)
    dy1_over = y_swap(dy1)
    early, into, dy1_over, dy3a, dy_right = tie(early, into, dy1_over, dy3a, dy_right)

    states = enter_states(early, into, do.state_shape, False)
    dy3b = shift(dy_right, 3)
    dy3a_over = y_swap(dy3a)
    states, dy3b, dy3a_over = tie(states, dy3b, dy3a_over)
    mixed, gated, gated_wide, keep, send = do.mixer_out(core, qe, states, intra, proj, gain, w_out)
    half = keep + core_swap(send)
    half, dy_quarter, dy3b, xn1_away = tie(half, dy_quarter, dy3b, xn1_away)

    half = half + y_swap(half)
    dy2 = shift(dy_quarter, 2)
    xn1_got = x_swap(xn1_away)
    half, dy2, dy3b, gated_wide, xn1_got = tie(half, dy2, dy3b, gated_wide, xn1_got)

    dy2_over, dy3b_over = y_swap(dy2), y_swap(dy3b)
    hidden, scale_two, hat_two, wide = second_norm(tokens, join_halves(half), norm_second)
    xn2 = wide.astype(BF16)
    xn_quarter = head_quarter(wide)
    xnl1 = shift(xn_quarter, 1)
    gated_got = x_swap(gated_wide)
    keep, send, dkeep, dsend = do.ffn_own(core, xn2, dy, ffn_in, ffn_out)
    dkeep, dsend, xn_quarter, dy2_over, dy3b_over, xnl1, gated_got, keep, send = tie(dkeep, dsend, xn_quarter, dy2_over, dy3b_over, xnl1, gated_got, keep, send)

    dhalf = dkeep + core_swap(dsend)
    dhalf, xn_quarter = tie(dhalf, xn_quarter)
    dhalf = dhalf + y_swap(dhalf)
    xnl2 = shift(xn_quarter, 2)
    dhalf, xnl2, xn_quarter, xnl1 = tie(dhalf, xnl2, xn_quarter, xnl1)

    dxn2 = join_halves(dhalf)
    xnl3 = shift(xn_quarter, 3)
    xnl1_over = y_swap(xnl1)
    part_norm_second = jnp.sum(dxn2 * hat_two, axis=0)
    dhidden = dy.astype(F32) + norm_back(dxn2, norm_second, scale_two, hat_two)
    dbranch = dhidden.astype(BF16)
    dbranch_away = lax.dynamic_index_in_dim(dhidden.reshape(do.count, 8, width // 8), 2 * head + 1 - x, 1, keepdims=False)
    dpre_gate, dmixed, part_gain, back = do.norm_back(dbranch, w_out, mixed, proj, gain, qe, packed)
    back, dpre_gate, xnl3, xnl1_over, dmixed, dbranch, xnl2, dbranch_away = tie(back, dpre_gate, xnl3, xnl1_over, dmixed, dbranch, xnl2, dbranch_away)

    early, late = pair_states(back, True)
    early, late, dpre_gate, dmixed, dbranch_away, xnl2 = tie(early, late, dpre_gate, dmixed, dbranch_away, xnl2)
    into = pass_states(join(early, late), True)
    dpre_query, dkeys, dvalues, dlogf = do.intra_back(dmixed, qe, ke, proj, cum, states)
    gate_got, dbranch_own = x_swap(dpre_gate), x_swap(dbranch_away)
    xnl2_over = y_swap(xnl2)
    early, into, gate_got, xnl2_over, dpre_query, dbranch_own, xnl3 = tie(early, into, gate_got, xnl2_over, dpre_query, dbranch_own, xnl3)

    carried = enter_states(early, into, do.state_shape, True)
    xnl3_over, dbranch_over = y_swap(xnl3), y_swap(dbranch_own)
    dpre_forget, dpre_values, part_bound = do.state_back(place, lengths, carried, states, ke, proj, cum, bound, dkeys, dvalues, dlogf)
    gate_keep, gate_send = do.mix_grad(place, xn1, xn1_got, dpre_gate, gate_got)
    dbranch_got = assemble([(dbranch_own, dbranch_over, 0)], width // 2)
    w_keep, w_send = do.mix_grad(place, dbranch, dbranch_got, gated, gated_got, turned=True)
    dpre_forget, dpre_values, dpre_query, gate_keep, gate_send, w_keep, w_send, xnl3_over = tie(
        dpre_forget, dpre_values, dpre_query, gate_keep, gate_send, w_keep, w_send, xnl3_over
    )

    forget_got, query_got, values_got = x_swap(dpre_forget), x_swap(dpre_query), x_swap(dpre_values)
    gate_near = gate_keep + lax.ppermute(gate_send, "seq", flip(2))
    w_near = w_keep + lax.ppermute(w_send, "seq", flip(2))
    lines = [
        (xn2, dy),
        (assemble([(xnl1, xnl1_over, 0)], width), assemble([(dy1, dy1_over, 0)], width)),
        (assemble([(xnl2, xnl2_over, 0)], width), assemble([(dy2, dy2_over, 0)], width)),
        (assemble([(xnl3, xnl3_over, 0)], width), assemble([(dy3a, dy3a_over, 0), (dy3b, dy3b_over, quarter // 2)], width)),
    ]
    rows = jnp.stack([seq, seq ^ 1]).astype(jnp.int32)
    cut = (do.steps + 1) // 2
    in_a, in_away_a, out_a, out_away_a = do.ffn_grad(rows, lines, ffn_in, ffn_out, 0, cut)
    dproj = (dpre_query, dpre_forget, dpre_values, dpre_gate)
    dxn1 = sum(dot(d.astype(BF16), mix_weight[c], NT) for c, d in enumerate(dproj))
    at = core[0] * (width // 2)
    half = lax.dynamic_slice_in_dim(dxn1, at, width // 2, 1) + core_swap(lax.dynamic_slice_in_dim(dxn1, width // 2 - at, width // 2, 1))
    forget_got, query_got, values_got, gate_near, w_near, in_away_a, out_away_a, half = tie(
        forget_got, query_got, values_got, gate_near, w_near, in_away_a, out_away_a, half
    )

    def high_bit(near):
        high = z // 2
        return (lax.dynamic_index_in_dim(near, at, 1, keepdims=False) for at in (high, 1 - high))

    gate_part, gate_far = high_bit(gate_near)
    w_part, w_far = high_bit(w_near)
    grad_gate = gate_part + lax.ppermute(gate_far, "seq", flip(4))
    grad_w_out = (w_part + lax.ppermute(w_far, "seq", flip(4)))[0]
    keep2, send2 = do.mix_grad(place, xn1, xn1_got, dpre_query, query_got, dpre_forget, forget_got)
    near2 = keep2 + lax.ppermute(send2, "seq", flip(2))
    v_keep, v_send = do.mix_grad(place, xn1, xn1_got, dpre_values, values_got)
    grad_in_a, grad_out_a = in_a + x_swap(in_away_a), out_a + x_swap(out_away_a)
    half = half + y_swap(half)
    in_b, in_away_b, out_b, out_away_b, tin, tin_away, tout, tout_away = do.ffn_grad(rows, lines, ffn_in, ffn_out, cut, do.steps - cut)
    grad_gate, grad_w_out, near2, v_send, grad_in_a, grad_out_a, half, in_away_b, out_away_b, tin_away, tout_away, send, keep = tie(
        grad_gate, grad_w_out, near2, v_send, grad_in_a, grad_out_a, half, in_away_b, out_away_b, tin_away, tout_away, send, keep
    )

    tokens_wide = tokens.astype(F32)
    scale_one = rms_scale(tokens_wide)
    hat_one = tokens_wide * scale_one
    dxn1 = join_halves(half)
    part_norm_first = jnp.sum(dxn1 * hat_one, axis=0)
    grad_tokens = (dhidden + norm_back(dxn1, norm_first, scale_one, hat_one)).astype(BF16)
    part2, far2 = high_bit(near2)
    grad2 = part2 + lax.ppermute(far2, "seq", flip(4))
    v_near = v_keep + lax.ppermute(v_send, "seq", flip(2))
    grad_in = jnp.concatenate([grad_in_a, in_b + x_swap(in_away_b), tin + x_swap(tin_away)], axis=2)
    grad_out = jnp.concatenate([grad_out_a, out_b + x_swap(out_away_b), tout + x_swap(tout_away)], axis=0)
    half = keep + core_swap(send)
    half = half + y_swap(half)
    v_near, half, part_norm_first, grad2 = tie(v_near, half, part_norm_first, grad2)

    output = (hidden + join_halves(half)).astype(BF16)
    v_part, v_far = high_bit(v_near)
    grad_v = v_part + lax.ppermute(v_far, "seq", flip(4))
    grad_mix = jnp.concatenate([grad2, grad_v, grad_gate])

    small = jnp.concatenate([part_norm_first, part_norm_second, part_bound[0], part_gain[0]])
    for bit in (1, 2, 4):
        small = small + lax.ppermute(small, "seq", flip(bit))
    return output, grad_tokens, small, (grad_mix, grad_w_out, grad_in, grad_out)


def weight_grads_whole(xn1, dproj, gated, dbranch, xn2, dy, ffn_in, ffn_out):
    gate, up = dot(xn2, ffn_in[0]), dot(xn2, ffn_in[1])
    dact = dot(dy, ffn_out, NT)
    sig = sigmoid(gate)
    swish = gate * sig
    act = (swish * up).astype(BF16)
    dgate = (dact * up * (sig * (1.0 + gate * (1.0 - sig)))).astype(BF16)
    dup = (dact * swish).astype(BF16)

    def scatter(a, axis):
        return lax.psum_scatter(a, "seq", scatter_dimension=axis, tiled=True)

    return (
        jnp.stack([scatter(dot(xn1, d.astype(BF16), TN), 0) for d in dproj]),
        scatter(dot(gated, dbranch, TN), 1),
        jnp.stack([scatter(dot(xn2, d, TN), 0) for d in (dgate, dup)]),
        scatter(dot(act, dy, TN), 1),
    )


def solution(mesh):
    in_specs = (
        P(None, "seq", None),
        P(),
        P(),
        P(None, None, "head"),
        P("head"),
        P("head"),
        P("head", None),
        P(),
        P(None, None, "head"),
        P("head", None),
        P(None, "seq", None),
    )
    out_specs = (
        P(None, "seq", None),
        P(None, "seq", None),
        P(),
        P(None, "seq", "head"),
        P("head"),
        P("head"),
        P("head", "seq"),
        P(),
        P(None, "seq", "head"),
        P("head", "seq"),
    )
    return jax.shard_map(body, mesh=mesh, in_specs=in_specs, out_specs=out_specs, check_vma=False)
```

```python
import functools

import jax
import jax.numpy as jnp
from jax import lax
from jax.experimental import pallas as pl
from jax.experimental.pallas import tpu as pltpu
from jax.sharding import PartitionSpec as P

HD = 128
EPS = 1e-06
F32 = jnp.float32
BF16 = jnp.bfloat16
MIB = 1 << 20
PACKED = HD + 8

X_SWAP = [(p, p ^ 1) for p in range(8)]
CORE_SWAP = [(h, h ^ 1) for h in range(4)]
Y_SWAP = [(h, h ^ 2) for h in range(4)]


def z_shift(k):
    return [(p, (p + 2 * k) % 8) for p in range(8)]


def z_line(k):
    return [(p, p + 2 * k) for p in range(8) if 0 <= p + 2 * k < 8]


def flip(bit):
    return [(p, p ^ bit) for p in range(8)]


def rms_scale(v):
    return lax.rsqrt(jnp.mean(v * v, axis=-1, keepdims=True) + EPS)


def norm_back(grad_normed, gain, scale, normed_hat):
    scaled = grad_normed * gain
    return scale * (scaled - normed_hat * jnp.mean(scaled * normed_hat, axis=-1, keepdims=True))


def dot(a, b, dims=((1,), (0,))):
    return lax.dot_general(a, b, (dims, ((), ())), preferred_element_type=F32)


NT = ((1,), (1,))
TN = ((0,), (0,))


def sigmoid(v):
    return 1.0 / (1.0 + jnp.exp(-v))


def triangle(kind):
    row = lax.broadcasted_iota(jnp.int32, (HD, HD), 0)
    col = lax.broadcasted_iota(jnp.int32, (HD, HD), 1)
    return {"lower": row >= col, "strict": row > col, "upper": row <= col}[kind]


def exact_dot(ones, v, parts=3):
    total = None
    for _ in range(parts):
        part = v.astype(BF16)
        v = v - part.astype(F32)
        term = dot(ones, part)
        total = term if total is None else total + term
    return total


def valid_rows(pos, length):
    row = lax.broadcasted_iota(jnp.int32, (HD, 1), 0)
    return (pos * HD + row) < length


def open_forget(pre, bound, ok):
    sig = sigmoid(pre)
    return sig, jnp.where(ok, bound + (1.0 - bound) * sig, 1.0)


def project_kernel(pos, lengths, x_ref, gain_ref, w_ref, bound_ref, xn_ref, away_ref, proj_ref, c_ref, qe_ref, ke_ref, intra_ref, sum_ref):
    @pl.when(pl.program_id(0) == 0)
    def _():
        x = x_ref[...].astype(F32)
        xn_ref[...] = (x * rms_scale(x) * gain_ref[...]).astype(BF16)
        n = away_ref.shape[1] // 4
        for z in range(4):
            at = pl.multiple_of((2 * z + 1 - pos[0] % 2) * n, n)
            away_ref[:, pl.ds(z * n, n)] = xn_ref[:, pl.ds(at, n)].astype(F32)

    xn = xn_ref[...]
    for c in range(4):
        proj_ref[c] = dot(xn, w_ref[c])
    slots, heads = sum_ref.shape[:2]
    lower = triangle("lower")
    ones = lower.astype(BF16)
    for s in range(slots):
        rows = pl.ds(s * HD, HD)
        ok = valid_rows(pos[0], lengths[s])
        _, forget = open_forget(proj_ref[1, rows, :], bound_ref[...], ok)
        c_ref[rows, :] = exact_dot(ones, jnp.log(forget), 2)
        for h in range(heads):
            cols = pl.ds(h * HD, HD)
            pre_q, v, cum = proj_ref[0, rows, cols], proj_ref[2, rows, cols], c_ref[rows, cols]
            keys = 1.0 - forget[:, h * HD : (h + 1) * HD]
            qe = (pre_q * sigmoid(pre_q) * jnp.exp(cum)).astype(BF16)
            ke = (keys * jnp.exp(-cum)).astype(BF16)
            qe_ref[rows, cols] = qe
            ke_ref[rows, cols] = ke
            vb = v.astype(BF16)
            scores = jnp.where(lower, dot(qe, ke, NT), 0.0).astype(BF16)
            intra_ref[rows, cols] = dot(scores, vb)
            last = cum[HD - 1 :, :]
            to_end = (keys * jnp.exp(last - cum)).astype(BF16)
            sum_ref[s, h, pl.ds(0, HD), :] = dot(vb, to_end, TN)
            sum_ref[s, h, pl.ds(HD, 8), :] = jnp.broadcast_to(jnp.exp(last), (8, HD))


def split_store(keep_ref, send_ref, core, make):
    half = keep_ref.shape[1]
    keep_ref[...] = make(pl.multiple_of(core * half, half), half)
    send_ref[...] = make(pl.multiple_of((1 - core) * half, half), half)


def mixer_out_kernel(core, qe_ref, state_ref, intra_ref, pre_ref, gain_ref, w_ref, mixed_ref, gated_ref, wide_ref, keep_ref, send_ref):
    slots, heads = state_ref.shape[:2]
    for s in range(slots):
        rows = pl.ds(s * HD, HD)
        for h in range(heads):
            cols = pl.ds(h * HD, HD)
            mixed = intra_ref[rows, cols] + dot(qe_ref[rows, cols], state_ref[s, h].astype(BF16), NT)
            mixed_ref[rows, cols] = mixed
            pre = pre_ref[0, rows, cols]
            gated = mixed * rms_scale(mixed) * gain_ref[:, cols] * (pre * sigmoid(pre))
            gated_ref[rows, cols] = gated.astype(BF16)
            wide_ref[rows, cols] = gated_ref[rows, cols].astype(F32)
    split_store(keep_ref, send_ref, core[0], lambda at, n: dot(gated_ref[...], w_ref[:, pl.ds(at, n)]))


def ffn_unit(xn, dy, w_gate, w_up, w_out):
    gate, up = dot(xn, w_gate), dot(xn, w_up)
    dact = dot(dy, w_out, NT)
    sig = sigmoid(gate)
    swish = gate * sig
    act = (swish * up).astype(BF16)
    dgate = (dact * up * (sig * (1.0 + gate * (1.0 - sig)))).astype(BF16)
    dup = (dact * swish).astype(BF16)
    return act, dgate, dup


def ffn_own_kernel(core, xn_ref, dy_ref, in_ref, out_ref, in_tail, out_tail, f_acc, d_keep, d_send, d_acc):
    step = pl.program_id(0)

    @pl.when(step == 0)
    def _():
        f_acc[...] = jnp.zeros_like(f_acc)
        d_acc[...] = jnp.zeros_like(d_acc)

    def add(w_in, w_out):
        act, dgate, dup = ffn_unit(xn_ref[...], dy_ref[...], w_in[0], w_in[1], w_out[...])
        f_acc[...] += dot(act, w_out[...])
        d_acc[...] += dot(dgate, w_in[0], NT) + dot(dup, w_in[1], NT)

    add(in_ref, out_ref)

    @pl.when(step == pl.num_programs(0) - 1)
    def _():
        add(in_tail, out_tail)
        split_store(d_keep, d_send, core[0], lambda at, n: d_acc[:, pl.ds(at, n)])


def widen_kernel(at, a_ref, out_ref, copy_ref):
    n = out_ref.shape[1]
    out_ref[...] = a_ref[:, pl.ds(pl.multiple_of(at[0] * n, n), n)].astype(F32)
    copy_ref[...] = a_ref[...]


def place_halves(out_ref, core, parts):
    n, terms = out_ref.shape[1] // 2, len(parts) // 2
    for k, which in ((0, core), (1, 1 - core)):
        mine = parts[k * terms : (k + 1) * terms]
        at = pl.ds(pl.multiple_of(which * n, n), n)
        out_ref[:, at] = mine[0][...] if terms == 1 else mine[0][...] + mine[1][...]


def second_norm_kernel(place, x_ref, p0, p1, p2, p3, gain_ref, hidden_ref, xn_ref, quarter_ref):
    core, head = place[0], place[1]
    place_halves(hidden_ref, core, (p0, p1, p2, p3))
    hidden = x_ref[...].astype(F32) + hidden_ref[...]
    hidden_ref[...] = hidden
    xn_ref[...] = (hidden * rms_scale(hidden) * gain_ref[...]).astype(BF16)
    n = quarter_ref.shape[1]
    quarter_ref[...] = xn_ref[:, pl.ds(pl.multiple_of(head * n, n), n)].astype(F32)


def first_back_kernel(d_ref, dhidden_ref, x_ref, gain_ref, grad_ref, part_ref):
    x, d = x_ref[...].astype(F32), d_ref[...]
    scale = rms_scale(x)
    hat = x * scale
    part_ref[...] = jnp.sum(d * hat, axis=0, keepdims=True)
    grad_ref[...] = (dhidden_ref[...] + norm_back(d, gain_ref[...], scale, hat)).astype(BF16)


def first_grad_kernel(d0, d1, d2, d3, w_ref, out_ref):
    out_ref[...] = sum(dot(d[...].astype(BF16), w_ref[c], NT) for c, d in enumerate((d0, d1, d2, d3)))


def assemble_kernel(at, here_ref, there_ref, *refs):
    out_ref = refs[-1]
    n = here_ref.shape[-1]
    for k, piece in enumerate((here_ref, there_ref)):
        for over in range(2):
            out_ref[:, pl.ds(pl.multiple_of(at[2 * over + k], n), n)] = piece[0, over].astype(BF16)


def join_kernel(parts_ref, _, out_ref):
    n = parts_ref.shape[2]
    for k in range(parts_ref.shape[0]):
        out_ref[:, pl.ds(k * n, n)] = parts_ref[k].astype(BF16)


def ffn_grad_kernel(tail, rows, xn_ref, dy_ref, *refs):
    weights, (mine_ref, away_ref, xt_ref, dyt_ref, act_ref, dgate_ref, dup_ref) = refs[:-7], refs[-7:]
    step = pl.program_id(0)
    n = mine_ref.shape[1]

    @pl.when(step == 0)
    def _():
        for which in range(2):
            at = pl.ds(pl.multiple_of(rows[which] * n, n), n)
            xt_ref[pl.ds(which * n, n), :] = xn_ref[:, at].T
            dyt_ref[pl.ds(which * n, n), :] = dy_ref[:, at].T

    def put(w_in, w_out, units):
        size = w_out.shape[0]
        block = xn_ref.shape[0] // 4
        for k in range(4):
            at = pl.ds(k * block, block)
            made = ffn_unit(xn_ref[at, :], dy_ref[at, :], w_in[0], w_in[1], w_out[...])
            act_ref[at, :size], dgate_ref[at, :size], dup_ref[at, :size] = made
        for k, (left, right) in enumerate(((xt_ref, dgate_ref), (xt_ref, dup_ref), (dyt_ref, act_ref))):
            both = dot(left[...], right[:, :size])
            mine_ref[k, :, units] = both[:n]
            away_ref[k, :, units] = both[n:]

    size = weights[1].shape[0]
    put(weights[0], weights[1], pl.ds(pl.multiple_of(step * size, size), size))
    if tail:

        @pl.when(step == pl.num_programs(0) - 1)
        def _():
            rest = weights[3].shape[0]
            put(weights[2], weights[3], pl.ds(mine_ref.shape[2] - rest, rest))


def turn_kernel(place, xn_ref, got_ref, out_ref):
    _, n, both = out_ref.shape
    z, x = place[0] // 2, place[0] % 2
    for k in range(4):
        high = z // 2 if k % 2 == 0 else 1 - z // 2
        row = 2 * high + (z % 2 if k < 2 else 1 - z % 2)
        a = xn_ref[:, pl.ds(pl.multiple_of((2 * row + x) * n, n), n)]
        b = got_ref[:, pl.ds(pl.multiple_of(row * n, n), n)].astype(BF16)
        out_ref[k, :, pl.ds(0, both // 2)] = a.T
        out_ref[k, :, pl.ds(both // 2, both // 2)] = b.T


def mix_grad_kernel(turned_ref, *refs):
    keep_ref, send_ref = refs[-2:]
    both = turned_ref.shape[2]
    for c in range(keep_ref.shape[0]):
        own, got = refs[2 * c][...].astype(BF16), refs[2 * c + 1][...].astype(BF16)
        for k in range(4):
            a = turned_ref[k]
            (keep_ref if k < 2 else send_ref)[c, k % 2] = dot(a[:, : both // 2], own) + dot(a[:, both // 2 :], got)


def norm_back_kernel(place, p0, p1, p2, p3, hidden_ref, dy_ref, norm_ref, w_ref, mixed_ref, pre_ref, gain_ref, qe_ref, sum_ref, dpre_ref, dm_ref, dgain_ref, back_ref, dhidden_ref, db_ref, away_ref, dnorm_ref, dg_ref):
    core, head, x = place[0], place[1], place[2]
    place_halves(dhidden_ref, core, (p0, p1, p2, p3))
    d, hidden = dhidden_ref[...], hidden_ref[...]
    scale = rms_scale(hidden)
    hat = hidden * scale
    dnorm_ref[...] = jnp.sum(d * hat, axis=0, keepdims=True)
    dhidden = dy_ref[...].astype(F32) + norm_back(d, norm_ref[...], scale, hat)
    dhidden_ref[...] = dhidden
    db_ref[...] = dhidden.astype(BF16)
    n = away_ref.shape[1]
    away_ref[...] = db_ref[:, pl.ds(pl.multiple_of((2 * head + 1 - x) * n, n), n)].astype(F32)
    dg_ref[...] = dot(db_ref[...], w_ref[...], NT)
    slots, heads = sum_ref.shape[:2]
    for h in range(heads):
        cols = pl.ds(h * HD, HD)
        gain = gain_ref[:, cols]
        total = jnp.zeros((1, HD), F32)
        for s in range(slots):
            rows = pl.ds(s * HD, HD)
            mixed, pre, dgated = mixed_ref[rows, cols], pre_ref[0, rows, cols], dg_ref[rows, cols]
            scale = rms_scale(mixed)
            hat = mixed * scale
            sig = sigmoid(pre)
            swish = pre * sig
            total += jnp.sum(dgated * hat * swish, axis=0, keepdims=True)
            dpre_ref[rows, cols] = (dgated * hat * gain * (sig * (1.0 + pre * (1.0 - sig)))).astype(BF16).astype(F32)
            dm = norm_back(dgated * swish, gain, scale, hat).astype(BF16)
            dm_ref[rows, cols] = dm
            back_ref[s, h, pl.ds(0, HD), :] = dot(dm, qe_ref[rows, cols], TN)
            back_ref[s, h, pl.ds(HD, 8), :] = sum_ref[s, h, pl.ds(HD, 8), :]
        dgain_ref[:, cols] = total


def intra_back_kernel(dm_ref, qe_ref, ke_ref, proj_ref, c_ref, state_ref, dq_ref, dk_ref, dv_ref, dl_ref):
    slots, heads = state_ref.shape[:2]
    lower = triangle("lower")
    upper = triangle("upper").astype(BF16)
    for s in range(slots):
        rows = pl.ds(s * HD, HD)
        for h in range(heads):
            cols = pl.ds(h * HD, HD)
            dm, qe, ke, cum = (r[rows, cols] for r in (dm_ref, qe_ref, ke_ref, c_ref))
            vb = proj_ref[2, rows, cols].astype(BF16)
            dscores = jnp.where(lower, dot(dm, vb, NT), 0.0).astype(BF16)
            to_q = dot(dscores, ke) + dot(dm, state_ref[s, h].astype(BF16))
            to_k = dot(dscores, qe, TN)
            pre = proj_ref[0, rows, cols]
            sig = sigmoid(pre)
            dq_ref[rows, cols] = (jnp.exp(cum) * to_q * (sig * (1.0 + pre * (1.0 - sig)))).astype(BF16).astype(F32)
            dk_ref[rows, cols] = jnp.exp(-cum) * to_k
            scores = jnp.where(lower, dot(qe, ke, NT), 0.0).astype(BF16)
            dv_ref[rows, cols] = dot(scores, dm, TN)
            dl_ref[rows, cols] = exact_dot(upper, qe.astype(F32) * to_q - ke.astype(F32) * to_k)


def state_back_kernel(pos, lengths, carried_ref, state_ref, ke_ref, forget_ref, value_ref, c_ref, bound_ref, dk_ref, dv_ref, dl_ref, dfv_ref, dbound_ref):
    slots, heads = state_ref.shape[:2]
    strict = triangle("strict").astype(BF16)
    for h in range(heads):
        cols = pl.ds(h * HD, HD)
        bound = bound_ref[:, cols]
        total = jnp.zeros((1, HD), F32)
        for s in range(slots):
            rows = pl.ds(s * HD, HD)
            ok = valid_rows(pos[0], lengths[s])
            cum, ke = c_ref[rows, cols], ke_ref[rows, cols]
            ending = carried_ref[s, h] * jnp.exp(cum[HD - 1 :, :])
            ending_low = ending.astype(BF16)
            to_k = dot(value_ref[0, rows, cols].astype(BF16), ending_low)
            dfv_ref[1, rows, cols] = (dv_ref[rows, cols] + dot(ke, ending_low, NT)).astype(BF16).astype(F32)
            through = jnp.sum(ending * state_ref[s, h], axis=0, keepdims=True)
            dlogf = dl_ref[rows, cols] + exact_dot(strict, ke.astype(F32) * to_k) + through
            dkeys = dk_ref[rows, cols] + jnp.exp(-cum) * to_k
            sig, forget = open_forget(forget_ref[0, rows, cols], bound, ok)
            dforget = jnp.where(ok, dlogf / forget - dkeys, 0.0)
            total += jnp.sum(dforget * (1.0 - sig), axis=0, keepdims=True)
            dfv_ref[0, rows, cols] = (dforget * (1.0 - bound) * sig * (1.0 - sig)).astype(BF16).astype(F32)
        dbound_ref[:, cols] = total


SMEM = pl.BlockSpec(memory_space=pltpu.SMEM)


def whole(shape, *index):
    index = index or (0,) * len(shape)
    return pl.BlockSpec(shape, lambda *_: index)


def sds(shape, dtype=F32):
    return jax.ShapeDtypeStruct(shape, dtype)


def call(kernel, name, outs, in_specs, out_specs, flops, moved, grid=(1,), scratch=(), vmem=48, aliases=None):
    return pl.pallas_call(
        kernel,
        name=name,
        grid=grid,
        out_shape=outs,
        in_specs=in_specs,
        out_specs=out_specs,
        scratch_shapes=list(scratch),
        input_output_aliases=aliases or {},
        compiler_params=pltpu.CompilerParams(vmem_limit_bytes=vmem * MIB),
        cost_estimate=pl.CostEstimate(flops=int(flops), bytes_accessed=int(moved), transcendentals=0),
    )


def entering_all(packed, backward):
    count, mine = lax.axis_size("seq"), lax.axis_index("seq")
    pieces = lax.all_gather(packed, "seq")
    if backward:
        pieces, mine = pieces[::-1], count - 1 - mine

    def step(position, state):
        piece = pieces[position]
        longer = piece[:, :, HD : HD + 1] * state + piece[:, :, :HD]
        return jnp.where(position < mine, longer, state)

    return lax.fori_loop(0, count - 1, step, jnp.zeros_like(packed[:, :, :HD]))


def decay(a):
    return a[:, HD : HD + 1]


def state(a):
    return a[:, :HD]


def join(a, b):
    both = decay(b) * state(a) + state(b)
    return jnp.concatenate([both, jnp.broadcast_to(decay(a) * decay(b), (a.shape[0], 8, HD))], axis=1)


def is_first(backward):
    is_low = lax.axis_index("seq") % 2 == 0
    return is_low, (~is_low if backward else is_low)


def pair_states(packed, backward):
    packed = packed.reshape(-1, PACKED, HD)
    half = packed.shape[0] // 2
    is_low, first = is_first(backward)
    mine = jnp.where(is_low, packed[:half], packed[half:])
    other = lax.ppermute(jnp.where(is_low, packed[half:], packed[:half]), "seq", X_SWAP)
    return jnp.where(first, mine, other), jnp.where(first, other, mine)


def pass_states(pair, backward):
    step = -1 if backward else 1
    before = lax.ppermute(pair, "seq", z_line(step))
    further = lax.ppermute(join(before, pair), "seq", z_line(2 * step))
    return decay(before) * state(further) + state(before)


def enter_states(early, into_first, shape, backward):
    is_low, first = is_first(backward)
    into_second = decay(early) * into_first + state(early)
    kept = jnp.where(first, into_first, into_second)
    given = lax.ppermute(jnp.where(first, into_second, into_first), "seq", X_SWAP)
    low, high = jnp.where(is_low, kept, given), jnp.where(is_low, given, kept)
    return jnp.concatenate([low, high]).reshape(shape)


def tie(*values):
    return lax.optimization_barrier(values)


def core_swap(a):
    return lax.ppermute(a, "head", CORE_SWAP)


def y_swap(a):
    return lax.ppermute(a, "head", Y_SWAP)


def x_swap(a):
    return lax.ppermute(a, "seq", X_SWAP)


def assemble(blocks, into=None, first=0):
    head = lax.axis_index("head")
    tokens, n = blocks[0][0].shape
    width = 4 * n
    here = jnp.stack([a for block in blocks for a in block]).reshape(len(blocks), 2, tokens, n)
    there = core_swap(here)
    at = jnp.stack([(head ^ k) * n for k in range(4)]).astype(jnp.int32)
    piece = pl.BlockSpec((1, 2, tokens, n), lambda i: (i, 0, 0, 0))
    out_spec = pl.BlockSpec((tokens, width), lambda i: (i + first, 0))
    grid = (len(blocks),)
    moved = 6 * len(blocks) * tokens * width
    if into is None:
        return call(assemble_kernel, "assemble", sds((len(blocks) * tokens, width), BF16), [SMEM, piece, piece], out_spec, 0, moved, grid=grid)(at, here, there)
    kept = pl.BlockSpec(memory_space=pl.ANY)
    return call(assemble_kernel, "assemble", sds(into.shape, BF16), [SMEM, piece, piece, kept], out_spec, 0, moved, grid=grid, aliases={3: 0})(at, here, there, into)


def join_heads(parts, into, first):
    heads, rows, n = parts.shape
    tokens = into.shape[0] // 4
    return call(
        join_kernel,
        "join",
        sds(into.shape, BF16),
        [pl.BlockSpec((heads, tokens, n), lambda i: (0, i, 0)), pl.BlockSpec(memory_space=pl.ANY)],
        pl.BlockSpec((tokens, heads * n), lambda i: (i + first, 0)),
        0,
        6 * rows * heads * n,
        grid=(rows // tokens,),
        aliases={1: 0},
    )(parts, into)


class Calls:
    def __init__(self, slots, length, width, local, units):
        self.slots, self.count, self.width, self.local, self.units = slots, slots * length, width, local, units
        self.heads = local // HD
        self.pair = 2 * HD
        self.steps = units // self.pair
        self.rest = units - self.steps * self.pair
        self.tall, self.channel = whole((self.count, width)), whole((self.count, local))
        self.row, self.w_spec = whole((1, local)), whole((local, width))
        self.half, self.half_spec = sds((self.count, width // 2)), whole((self.count, width // 2))
        self.state_shape = (slots, self.heads, HD, HD)
        self.packed_shape = (slots, self.heads, PACKED, HD)
        self.state_spec, self.packed_spec = whole(self.state_shape), whole(self.packed_shape)
        self.wide, self.norm_row = sds((self.count, width)), whole((1, width))
        self.low = sds((self.count, local), BF16)
        self.full = sds((self.count, local))

    def proj(self, *index):
        return whole((1, self.count, self.local), *index)

    def project(self, pos, lengths, tokens, norm, weight, bound):
        count, width, local, pair = self.count, self.width, self.local, self.pair
        block = pl.BlockSpec((count, pair), lambda i: (0, i))
        return call(
            project_kernel,
            "project",
            [sds((count, width), BF16), self.half, sds((4, count, local)), self.full, self.low, self.low, self.full, sds(self.packed_shape)],
            [SMEM, SMEM, self.tall, whole((1, width)), pl.BlockSpec((4, width, pair), lambda i: (0, 0, i)), pl.BlockSpec((1, pair), lambda i: (0, i))],
            [self.tall, self.half_spec, pl.BlockSpec((4, count, pair), lambda i: (0, 0, i))] + [block] * 4 + [pl.BlockSpec((self.slots, 2, PACKED, HD), lambda i: (0, i, 0, 0))],
            8 * count * width * local,
            20e6,
            grid=(local // pair,),
        )(pos, lengths, tokens, norm, weight, bound)

    def mixer_out(self, core, qe, states, intra, proj, gain, weight):
        return call(
            mixer_out_kernel,
            "mixer_out",
            [self.full, self.low, self.full, self.half, self.half],
            [SMEM, self.channel, self.state_spec, self.channel, self.proj(3, 0, 0), self.row, self.w_spec],
            [self.channel] * 3 + [self.half_spec] * 2,
            2 * self.count * self.width * self.local,
            10e6,
        )(core, qe, states, intra, proj, gain, weight)

    def ffn_specs(self, first=0, tail=True):
        width, pair, rest = self.width, self.pair, self.rest
        last = self.steps * pair // rest
        specs = [
            pl.BlockSpec((2, width, pair), lambda i: (0, 0, i + first)),
            pl.BlockSpec((pair, width), lambda i: (i + first, 0)),
            whole((2, width, rest), 0, 0, last),
            whole((rest, width), last, 0),
        ]
        return specs if tail else specs[:2]

    def ffn_own(self, core, xn2, dy, ffn_in, ffn_out):
        return call(
            ffn_own_kernel,
            "ffn_own",
            [self.wide, self.half, self.half],
            [SMEM, self.tall, self.tall, *self.ffn_specs()],
            [self.tall, self.half_spec, self.half_spec],
            12 * self.count * self.width * self.units,
            30e6,
            grid=(self.steps,),
            scratch=[pltpu.VMEM((self.count, self.width), F32)],
            vmem=60,
        )(core, xn2, dy, ffn_in, ffn_out, ffn_in, ffn_out)

    def norm_back(self, place, parts, hidden, dy, norm, weight, mixed, proj, gain, qe, packed):
        n = self.width // 8
        return call(
            norm_back_kernel,
            "norm_back",
            [self.full, self.low, sds((1, self.local)), sds(self.packed_shape), self.wide, sds((self.count, self.width), BF16), sds((self.count, n)), sds((1, self.width))],
            [SMEM] + [self.half_spec] * 4 + [self.tall, self.tall, self.norm_row, self.w_spec, self.channel, self.proj(3, 0, 0), self.row, self.channel, self.packed_spec],
            [self.channel, self.channel, self.row, self.packed_spec, self.tall, self.tall, whole((self.count, n)), self.norm_row],
            2 * self.count * self.width * self.local,
            10e6,
            scratch=[pltpu.VMEM((self.count, self.local), F32)],
        )(place, *parts, hidden, dy, norm, weight, mixed, proj, gain, qe, packed)

    def second_norm(self, place, tokens, parts, gain, lines):
        quarter = self.width // 4
        return call(
            second_norm_kernel,
            "second_norm",
            [self.wide, sds((lines * self.count, self.width), BF16), sds((self.count, quarter))],
            [SMEM, self.tall] + [self.half_spec] * 4 + [self.norm_row],
            [self.tall, self.tall, whole((self.count, quarter))],
            0,
            10e6,
        )(place, tokens, *parts, gain)

    def first_grad(self, dproj, weight):
        quarter = self.width // 4
        return call(
            first_grad_kernel,
            "first_grad",
            self.wide,
            [self.channel] * 4 + [pl.BlockSpec((4, quarter, self.local), lambda i: (0, i, 0))],
            pl.BlockSpec((self.count, quarter), lambda i: (0, i)),
            8 * self.count * self.width * self.local,
            15e6,
            grid=(4,),
        )(*dproj, weight)

    def first_back(self, dxn1, dhidden, tokens, gain):
        return call(
            first_back_kernel,
            "first_back",
            [sds((self.count, self.width), BF16), sds((1, self.width))],
            [self.tall, self.tall, self.tall, self.norm_row],
            [self.tall, self.norm_row],
            0,
            10e6,
        )(dxn1, dhidden, tokens, gain)

    def intra_back(self, dmixed, qe, ke, proj, cum, states):
        return call(
            intra_back_kernel,
            "intra_back",
            [self.full] * 4,
            [self.channel, self.channel, self.channel, whole((3, self.count, self.local)), self.channel, self.state_spec],
            [self.channel] * 4,
            14 * self.count * self.local * HD,
            10e6,
        )(dmixed, qe, ke, proj, cum, states)

    def state_back(self, pos, lengths, carried, states, ke, proj, cum, bound, dkeys, dvalues, dlogf):
        return call(
            state_back_kernel,
            "state_back",
            [sds((2, self.count, self.local)), sds((1, self.local))],
            [SMEM, SMEM, self.state_spec, self.state_spec, self.channel, self.proj(1, 0, 0), self.proj(2, 0, 0), self.channel, self.row] + [self.channel] * 3,
            [whole((2, self.count, self.local)), self.row],
            8 * self.count * self.local * HD,
            10e6,
        )(pos, lengths, carried, states, ke, proj, proj, cum, bound, dkeys, dvalues, dlogf)

    def widen(self, head, dy, lines):
        quarter = self.width // 4
        return call(
            widen_kernel,
            "widen",
            [sds((self.count, quarter)), sds((lines * self.count, self.width), BF16)],
            [SMEM, self.tall],
            [whole((self.count, quarter)), self.tall],
            0,
            4e6,
        )(head, dy)

    def turn(self, place, xn, got):
        shape = (4, self.width // 8, 2 * self.count)
        return call(turn_kernel, "turn", sds(shape, BF16), [SMEM, self.tall, self.half_spec], whole(shape), 0, 6e6)(place, xn, got)

    def mix_grad(self, turned, *grads):
        shape = (len(grads) // 2, 2, self.width // 8, self.local)
        return call(
            mix_grad_kernel,
            "mix_grad",
            [sds(shape)] * 2,
            [whole(turned.shape)] + [self.channel] * len(grads),
            [whole(shape)] * 2,
            len(grads) * self.count * self.width * self.local,
            10e6,
        )(turned, *grads)

    def ffn_grad(self, rows, xn, dy, ffn_in, ffn_out, first, steps):
        n, pair = self.width // 8, self.pair
        tail = first + steps == self.steps and self.rest > 0
        units = steps * pair + self.rest * tail
        out = sds((3, n, units))
        line = whole(xn.shape)
        return call(
            functools.partial(ffn_grad_kernel, tail),
            "ffn_grad",
            [out, out],
            [SMEM, line, line] + self.ffn_specs(first, tail),
            [whole(out.shape)] * 2,
            6 * xn.shape[0] * (self.width + 2 * n) * units,
            20e6,
            grid=(steps,),
            scratch=[pltpu.VMEM((2 * n, xn.shape[0]), BF16)] * 2 + [pltpu.VMEM((xn.shape[0], pair), BF16)] * 3,
            vmem=62,
        )(rows, xn, dy, *([ffn_in, ffn_out] * (2 if tail else 1)))


def scalar(v):
    return jnp.asarray(v, jnp.int32).reshape(1)


def body(tokens, lengths, norm_first, mix_weight, lower_bound, out_gain, w_out, norm_second, ffn_in, ffn_out, cotangent):
    shape = tokens.shape
    slots, length, width = shape
    local = lower_bound.shape[0]
    do = Calls(slots, length, width, local, ffn_out.shape[0])
    fast = lax.axis_size("seq") == 8 and lax.axis_size("head") == 4
    run = run_lines if fast else run_any
    output, grad_tokens, small, weights = run(
        do,
        tokens.reshape(do.count, width),
        lengths,
        norm_first.reshape(1, width),
        mix_weight,
        lower_bound.reshape(1, local),
        out_gain.reshape(1, local),
        w_out,
        norm_second.reshape(1, width),
        ffn_in,
        ffn_out,
        cotangent.reshape(do.count, width),
    )
    first, second = small[:width], small[width : 2 * width]
    bound_sum, gain_sum = small[2 * width : 2 * width + local], small[2 * width + local :]
    return (output.reshape(shape), grad_tokens.reshape(shape), first, weights[0], bound_sum, gain_sum, weights[1], second, weights[2], weights[3])


def run_any(do, tokens, lengths, norm_first, mix_weight, bound, gain, w_out, norm_second, ffn_in, ffn_out, dy):
    def total(halves):
        low, high = jnp.split(lax.psum(jnp.concatenate(halves, axis=1), "head"), 2, axis=1)
        return low, jnp.zeros_like(low), high, jnp.zeros_like(high)

    pos, core = scalar(lax.axis_index("seq")), scalar(0)
    nowhere = jnp.zeros((3,), jnp.int32)
    xn1, _, proj, cum, qe, ke, intra, packed = do.project(pos, lengths, tokens, norm_first, mix_weight, bound)
    states = entering_all(packed, False)
    mixed, gated, _, *halves = do.mixer_out(core, qe, states, intra, proj, gain, w_out)
    hidden, xn2, _ = do.second_norm(nowhere, tokens, total(halves), norm_second, 1)
    ffn, dkeep, dsend = do.ffn_own(core, xn2, dy, ffn_in, ffn_out)
    output = (hidden + lax.psum(ffn, "head")).astype(BF16)
    dpre_gate, dmixed, part_gain, back, dhidden, dbranch, _, part_norm_second = do.norm_back(
        nowhere, total((dkeep, dsend)), hidden, dy, norm_second, w_out, mixed, proj, gain, qe, packed
    )
    carried = entering_all(back, True)
    dpre_query, dkeys, dvalues, dlogf = do.intra_back(dmixed, qe, ke, proj, cum, states)
    dpre_fv, part_bound = do.state_back(pos, lengths, carried, states, ke, proj, cum, bound, dkeys, dvalues, dlogf)
    dproj = (dpre_query, dpre_fv[0], dpre_fv[1], dpre_gate)
    grad_tokens, part_norm_first = do.first_back(lax.psum(do.first_grad(dproj, mix_weight), "head"), dhidden, tokens, norm_first)
    weights = weight_grads_whole(xn1, dproj, gated, dbranch, xn2, dy, ffn_in, ffn_out)
    small = lax.psum(jnp.concatenate([part_norm_first[0], part_norm_second[0], part_bound[0], part_gain[0]]), "seq")
    return output, grad_tokens, small, weights


def run_lines(do, tokens, lengths, norm_first, mix_weight, bound, gain, w_out, norm_second, ffn_in, ffn_out, dy):
    width, local, quarter = do.width, do.local, do.width // 4
    seq, head = lax.axis_index("seq"), lax.axis_index("head")
    x, z = seq % 2, seq // 2
    seq_at, core = scalar(seq), scalar(head % 2)
    place = jnp.stack([head % 2, head, x]).astype(jnp.int32)

    def shift(a, k):
        return lax.ppermute(a, "seq", z_shift(k))

    def sum_cores(keep, send):
        return keep + core_swap(send)

    def sum_near(keep, send):
        got = lax.ppermute(send, "seq", flip(2))
        return (keep[:, 0], got[:, 0]), keep[:, 1] + got[:, 1]

    def sum_far(near):
        (a, b), far = near
        return a + b + lax.ppermute(far, "seq", flip(4))

    dy_quarter, dy_all = do.widen(scalar(head), dy, 4)
    dy1 = shift(dy_quarter, 1)
    xn1, xn1_away, proj, cum, qe, ke, intra, packed = do.project(seq_at, lengths, tokens, norm_first, mix_weight, bound)
    early, late = pair_states(packed, False)
    early, late, dy1 = tie(early, late, dy1)

    into = pass_states(join(early, late), False)
    dy1_over = y_swap(dy1)
    early, into, dy1_over, dy_quarter = tie(early, into, dy1_over, dy_quarter)

    states = enter_states(early, into, do.state_shape, False)
    mixed, gated, gated_wide, keep, send = do.mixer_out(core, qe, states, intra, proj, gain, w_out)
    half = sum_cores(keep, send)
    half, dy_quarter, xn1_away, dy1, dy1_over = tie(half, dy_quarter, xn1_away, dy1, dy1_over)

    over = y_swap(half)
    half_other = core_swap(half)
    dy2 = shift(dy_quarter, 2)
    xn1_got = x_swap(xn1_away)
    dy_all = assemble([(dy1, dy1_over)], dy_all, 1)
    half, half_other, over, dy2, gated_wide, xn1_got, dy_all = tie(half, half_other, over, dy2, gated_wide, xn1_got, dy_all)

    dy2_over = y_swap(dy2)
    hidden, xn_all, xn_quarter = do.second_norm(place, tokens, (half, over, half_other, core_swap(over)), norm_second, 4)
    xnl1 = shift(xn_quarter, 1)
    gated_got = x_swap(gated_wide)
    ffn, dkeep, dsend = do.ffn_own(core, xn_all, dy, ffn_in, ffn_out)
    dkeep, dsend, xn_quarter, dy2_over, xnl1, gated_got, ffn = tie(dkeep, dsend, xn_quarter, dy2_over, xnl1, gated_got, ffn)

    dhalf = sum_cores(dkeep, dsend)
    dhalf, xn_quarter, dy_all, xn1_got = tie(dhalf, xn_quarter, dy_all, xn1_got)
    dover = y_swap(dhalf)
    dhalf_other = core_swap(dhalf)
    xnl2 = shift(xn_quarter, 2)
    dy_all = assemble([(dy2, dy2_over)], dy_all, 2)
    xn1_turned = do.turn(seq_at, xn1, xn1_got)
    dhalf, dover, dhalf_other, xnl2, xn_quarter, xnl1, dy_all, xn1_turned = tie(dhalf, dover, dhalf_other, xnl2, xn_quarter, xnl1, dy_all, xn1_turned)

    xnl3 = shift(xn_quarter, 3)
    dpre_gate, dmixed, part_gain, back, dhidden, dbranch, dbranch_away, part_norm_second = do.norm_back(
        place, (dhalf, dover, dhalf_other, core_swap(dover)), hidden, dy, norm_second, w_out, mixed, proj, gain, qe, packed
    )
    back, dpre_gate, dmixed, dbranch, dbranch_away, dy_quarter = tie(back, dpre_gate, dmixed, dbranch, dbranch_away, dy_quarter)

    early, late = pair_states(back, True)
    dy3 = shift(dy_quarter, 3)
    early, late, dpre_gate, dmixed, dbranch_away, xnl3, dy3 = tie(early, late, dpre_gate, dmixed, dbranch_away, xnl3, dy3)
    xn_parts = lax.all_gather(jnp.concatenate([xnl1, xnl2, xnl3]), "head")
    into = pass_states(join(early, late), True)
    dbranch_own = x_swap(dbranch_away)
    dpre_query, dkeys, dvalues, dlogf = do.intra_back(dmixed, qe, ke, proj, cum, states)
    gate_got = x_swap(dpre_gate)
    dy3_over = y_swap(dy3)
    early, into, gate_got, dpre_query, dbranch_own, dy3_over = tie(early, into, gate_got, dpre_query, dbranch_own, dy3_over)

    dbranch_over = y_swap(dbranch_own)
    gate = do.mix_grad(xn1_turned, dpre_gate, gate_got)
    carried = enter_states(early, into, do.state_shape, True)
    dy_all = assemble([(dy3, dy3_over)], dy_all, 3)
    carried, gate = tie(carried, gate)
    dpre_fv, part_bound = do.state_back(seq_at, lengths, carried, states, ke, proj, cum, bound, dkeys, dvalues, dlogf)
    dpre_fv, dpre_query, gate, dbranch_over, dy_all = tie(dpre_fv, dpre_query, gate, dbranch_over, dy_all)

    fv_got = x_swap(dpre_fv)
    near_gate = sum_near(*gate)
    dxn1 = do.first_grad((dpre_query, dpre_fv[0], dpre_fv[1], dpre_gate), mix_weight)
    down = do.mix_grad(do.turn(seq_at, dbranch, assemble([(dbranch_own, dbranch_over)])), gated, gated_got)
    near_down = sum_near(*down)
    fv_got, near_gate, near_down, xn_all, dpre_query, xn_parts, dxn1, ffn = tie(fv_got, near_gate, near_down, xn_all, dpre_query, xn_parts, dxn1, ffn)
    dxn1, ffn = lax.psum((dxn1, ffn), "head")

    rows = jnp.stack([seq, seq ^ 1]).astype(jnp.int32)
    query_got = x_swap(dpre_query)
    grad_early = sum_far(tuple(jax.tree.map(lambda a, b: jnp.concatenate([a, b]), near_gate, near_down)))
    forget_values = do.mix_grad(xn1_turned, dpre_fv[0], fv_got[0], dpre_fv[1], fv_got[1])
    forget_values, xn_all, xn_parts = tie(forget_values, xn_all, xn_parts)
    near_fv = sum_near(*forget_values)
    xn_all = join_heads(xn_parts, xn_all, 1)
    mine_a, away_a = do.ffn_grad(rows, xn_all, dy_all, ffn_in, ffn_out, 0, 2)
    away_a, xn_all, query_got = tie(away_a, xn_all, query_got)
    got_a = x_swap(away_a)
    query = do.mix_grad(xn1_turned, dpre_query, query_got)
    mine_b, away_b = do.ffn_grad(rows, xn_all, dy_all, ffn_in, ffn_out, 2, 2)
    near_fv, grad_early, got_a, query, away_b, xn_all = tie(near_fv, grad_early, got_a, query, away_b, xn_all)

    got_b = x_swap(away_b)
    near_query, grad_fv = sum_near(*query), sum_far(near_fv)
    grad_tokens, part_norm_first = do.first_back(dxn1, dhidden, tokens, norm_first)
    mine_c, away_c = do.ffn_grad(rows, xn_all, dy_all, ffn_in, ffn_out, 4, do.steps - 4)
    small = jnp.concatenate([part_norm_first[0], part_norm_second[0], part_bound[0], part_gain[0]])
    got_b, near_query, grad_fv, small, away_c = tie(got_b, near_query, grad_fv, small, away_c)

    got_c = x_swap(away_c)
    grad_query = sum_far(near_query)
    for bit in (1, 2, 4):
        small = small + lax.ppermute(small, "seq", flip(bit))
    output = (hidden + ffn).astype(BF16)
    parts = ((mine_a, got_a), (mine_b, got_b), (mine_c, got_c))
    grad_in = jnp.concatenate([mine[:2] + got[:2] for mine, got in parts], axis=2)
    grad_out = jnp.concatenate([(mine[2] + got[2]).T for mine, got in parts], axis=0)
    grad_mix = jnp.concatenate([grad_query, grad_fv, grad_early[:1]])
    return output, grad_tokens, small, (grad_mix, grad_early[1].T, grad_in, grad_out)


def weight_grads_whole(xn1, dproj, gated, dbranch, xn2, dy, ffn_in, ffn_out):
    gate, up = dot(xn2, ffn_in[0]), dot(xn2, ffn_in[1])
    dact = dot(dy, ffn_out, NT)
    sig = sigmoid(gate)
    swish = gate * sig
    act = (swish * up).astype(BF16)
    dgate = (dact * up * (sig * (1.0 + gate * (1.0 - sig)))).astype(BF16)
    dup = (dact * swish).astype(BF16)

    def scatter(a, axis):
        return lax.psum_scatter(a, "seq", scatter_dimension=axis, tiled=True)

    return (
        jnp.stack([scatter(dot(xn1, d.astype(BF16), TN), 0) for d in dproj]),
        scatter(dot(gated, dbranch, TN), 1),
        jnp.stack([scatter(dot(xn2, d, TN), 0) for d in (dgate, dup)]),
        scatter(dot(act, dy, TN), 1),
    )


def solution(mesh):
    in_specs = (
        P(None, "seq", None),
        P(),
        P(),
        P(None, None, "head"),
        P("head"),
        P("head"),
        P("head", None),
        P(),
        P(None, None, "head"),
        P("head", None),
        P(None, "seq", None),
    )
    out_specs = (
        P(None, "seq", None),
        P(None, "seq", None),
        P(),
        P(None, "seq", "head"),
        P("head"),
        P("head"),
        P("head", "seq"),
        P(),
        P(None, "seq", "head"),
        P("head", "seq"),
    )
    return jax.shard_map(body, mesh=mesh, in_specs=in_specs, out_specs=out_specs, check_vma=False)
```

```python
import functools

import jax
import jax.numpy as jnp
from jax import lax
from jax.experimental import pallas as pl
from jax.experimental.pallas import tpu as pltpu
from jax.sharding import PartitionSpec as P

HD = 128
EPS = 1e-06
F32 = jnp.float32
BF16 = jnp.bfloat16
MIB = 1 << 20
PACKED = HD + 8

X_SWAP = [(p, p ^ 1) for p in range(8)]
CORE_SWAP = [(h, h ^ 1) for h in range(4)]
Y_SWAP = [(h, h ^ 2) for h in range(4)]


def z_shift(k):
    return [(p, (p + 2 * k) % 8) for p in range(8)]


def z_line(k):
    return [(p, p + 2 * k) for p in range(8) if 0 <= p + 2 * k < 8]


def flip(bit):
    return [(p, p ^ bit) for p in range(8)]


def rms_scale(v):
    return lax.rsqrt(jnp.mean(v * v, axis=-1, keepdims=True) + EPS)


def norm_back(grad_normed, gain, scale, normed_hat):
    scaled = grad_normed * gain
    return scale * (scaled - normed_hat * jnp.mean(scaled * normed_hat, axis=-1, keepdims=True))


def dot(a, b, dims=((1,), (0,))):
    return lax.dot_general(a, b, (dims, ((), ())), preferred_element_type=F32)


NT = ((1,), (1,))
TN = ((0,), (0,))


def sigmoid(v):
    return 1.0 / (1.0 + jnp.exp(-v))


def triangle(kind):
    row = lax.broadcasted_iota(jnp.int32, (HD, HD), 0)
    col = lax.broadcasted_iota(jnp.int32, (HD, HD), 1)
    return {"lower": row >= col, "strict": row > col, "upper": row <= col}[kind]


def exact_dot(ones, v, parts=3):
    total = None
    for _ in range(parts):
        part = v.astype(BF16)
        v = v - part.astype(F32)
        term = dot(ones, part)
        total = term if total is None else total + term
    return total


def valid_rows(pos, length):
    row = lax.broadcasted_iota(jnp.int32, (HD, 1), 0)
    return (pos * HD + row) < length


def open_forget(pre, bound, ok):
    sig = sigmoid(pre)
    return sig, jnp.where(ok, bound + (1.0 - bound) * sig, 1.0)


def project_kernel(pos, lengths, x_ref, gain_ref, w_ref, bound_ref, xn_ref, away_ref, proj_ref, c_ref, qe_ref, ke_ref, intra_ref, sum_ref):
    @pl.when(pl.program_id(0) == 0)
    def _():
        x = x_ref[...].astype(F32)
        xn_ref[...] = (x * rms_scale(x) * gain_ref[...]).astype(BF16)
        n = away_ref.shape[1] // 4
        for z in range(4):
            at = pl.multiple_of((2 * z + 1 - pos[0] % 2) * n, n)
            away_ref[:, pl.ds(z * n, n)] = xn_ref[:, pl.ds(at, n)].astype(F32)

    xn = xn_ref[...]
    for c in range(4):
        proj_ref[c] = dot(xn, w_ref[c])
    slots, heads = sum_ref.shape[:2]
    lower = triangle("lower")
    ones = lower.astype(BF16)
    for s in range(slots):
        rows = pl.ds(s * HD, HD)
        ok = valid_rows(pos[0], lengths[s])
        _, forget = open_forget(proj_ref[1, rows, :], bound_ref[...], ok)
        c_ref[rows, :] = exact_dot(ones, jnp.log(forget), 2)
        for h in range(heads):
            cols = pl.ds(h * HD, HD)
            pre_q, v, cum = proj_ref[0, rows, cols], proj_ref[2, rows, cols], c_ref[rows, cols]
            keys = 1.0 - forget[:, h * HD : (h + 1) * HD]
            qe = (pre_q * sigmoid(pre_q) * jnp.exp(cum)).astype(BF16)
            ke = (keys * jnp.exp(-cum)).astype(BF16)
            qe_ref[rows, cols] = qe
            ke_ref[rows, cols] = ke
            vb = v.astype(BF16)
            scores = jnp.where(lower, dot(qe, ke, NT), 0.0).astype(BF16)
            intra_ref[rows, cols] = dot(scores, vb)
            last = cum[HD - 1 :, :]
            to_end = (keys * jnp.exp(last - cum)).astype(BF16)
            sum_ref[s, h, pl.ds(0, HD), :] = dot(vb, to_end, TN)
            sum_ref[s, h, pl.ds(HD, 8), :] = jnp.broadcast_to(jnp.exp(last), (8, HD))


def split_store(keep_ref, send_ref, core, make):
    half = keep_ref.shape[1]
    keep_ref[...] = make(pl.multiple_of(core * half, half), half)
    send_ref[...] = make(pl.multiple_of((1 - core) * half, half), half)


def mixer_out_kernel(core, qe_ref, state_ref, intra_ref, pre_ref, gain_ref, w_ref, mixed_ref, gated_ref, wide_ref, keep_ref, send_ref):
    slots, heads = state_ref.shape[:2]
    for s in range(slots):
        rows = pl.ds(s * HD, HD)
        for h in range(heads):
            cols = pl.ds(h * HD, HD)
            mixed = intra_ref[rows, cols] + dot(qe_ref[rows, cols], state_ref[s, h].astype(BF16), NT)
            mixed_ref[rows, cols] = mixed
            pre = pre_ref[0, rows, cols]
            gated = mixed * rms_scale(mixed) * gain_ref[:, cols] * (pre * sigmoid(pre))
            gated_ref[rows, cols] = gated.astype(BF16)
            wide_ref[rows, cols] = gated_ref[rows, cols].astype(F32)
    split_store(keep_ref, send_ref, core[0], lambda at, n: dot(gated_ref[...], w_ref[:, pl.ds(at, n)]))


def ffn_unit(xn, dy, w_gate, w_up, w_out):
    gate, up = dot(xn, w_gate), dot(xn, w_up)
    dact = dot(dy, w_out, NT)
    sig = sigmoid(gate)
    swish = gate * sig
    act = (swish * up).astype(BF16)
    dgate = (dact * up * (sig * (1.0 + gate * (1.0 - sig)))).astype(BF16)
    dup = (dact * swish).astype(BF16)
    return act, dgate, dup


def ffn_own_kernel(core, xn_ref, dy_ref, in_ref, out_ref, in_tail, out_tail, f_acc, d_keep, d_send, d_acc):
    step = pl.program_id(0)

    @pl.when(step == 0)
    def _():
        f_acc[...] = jnp.zeros_like(f_acc)
        d_acc[...] = jnp.zeros_like(d_acc)

    def add(w_in, w_out):
        act, dgate, dup = ffn_unit(xn_ref[...], dy_ref[...], w_in[0], w_in[1], w_out[...])
        f_acc[...] += dot(act, w_out[...])
        d_acc[...] += dot(dgate, w_in[0], NT) + dot(dup, w_in[1], NT)

    add(in_ref, out_ref)

    @pl.when(step == pl.num_programs(0) - 1)
    def _():
        add(in_tail, out_tail)
        split_store(d_keep, d_send, core[0], lambda at, n: d_acc[:, pl.ds(at, n)])


def widen_kernel(at, a_ref, out_ref, copy_ref):
    n = out_ref.shape[1]
    out_ref[...] = a_ref[:, pl.ds(pl.multiple_of(at[0] * n, n), n)].astype(F32)
    copy_ref[...] = a_ref[...]


def place_halves(out_ref, core, parts):
    n, terms = out_ref.shape[1] // 2, len(parts) // 2
    for k, which in ((0, core), (1, 1 - core)):
        mine = parts[k * terms : (k + 1) * terms]
        at = pl.ds(pl.multiple_of(which * n, n), n)
        out_ref[:, at] = mine[0][...] if terms == 1 else mine[0][...] + mine[1][...]


def second_norm_kernel(place, x_ref, p0, p1, p2, p3, gain_ref, hidden_ref, xn_ref, quarter_ref):
    core, head = place[0], place[1]
    place_halves(hidden_ref, core, (p0, p1, p2, p3))
    hidden = x_ref[...].astype(F32) + hidden_ref[...]
    hidden_ref[...] = hidden
    xn_ref[...] = (hidden * rms_scale(hidden) * gain_ref[...]).astype(BF16)
    n = quarter_ref.shape[1]
    quarter_ref[...] = xn_ref[:, pl.ds(pl.multiple_of(head * n, n), n)].astype(F32)


def first_back_kernel(d_ref, dhidden_ref, x_ref, gain_ref, grad_ref, part_ref):
    x, d = x_ref[...].astype(F32), d_ref[...]
    scale = rms_scale(x)
    hat = x * scale
    part_ref[...] = jnp.sum(d * hat, axis=0, keepdims=True)
    grad_ref[...] = (dhidden_ref[...] + norm_back(d, gain_ref[...], scale, hat)).astype(BF16)


def first_grad_kernel(d0, d1, d2, d3, w_ref, out_ref):
    out_ref[...] = sum(dot(d[...].astype(BF16), w_ref[c], NT) for c, d in enumerate((d0, d1, d2, d3)))


def assemble_kernel(at, here_ref, there_ref, *refs):
    out_ref = refs[-1]
    n = here_ref.shape[-1]
    for k, piece in enumerate((here_ref, there_ref)):
        for over in range(2):
            out_ref[:, pl.ds(pl.multiple_of(at[2 * over + k], n), n)] = piece[0, over].astype(BF16)


def join_kernel(parts_ref, _, out_ref):
    n = parts_ref.shape[2]
    for k in range(parts_ref.shape[0]):
        out_ref[:, pl.ds(k * n, n)] = parts_ref[k].astype(BF16)


def ffn_grad_kernel(tail, rows, xn_ref, dy_ref, *refs):
    weights, (mine_ref, away_ref, xt_ref, dyt_ref, act_ref, dgate_ref, dup_ref) = refs[:-7], refs[-7:]
    step = pl.program_id(0)
    n = mine_ref.shape[1]

    @pl.when(step == 0)
    def _():
        for which in range(2):
            at = pl.ds(pl.multiple_of(rows[which] * n, n), n)
            xt_ref[pl.ds(which * n, n), :] = xn_ref[:, at].T
            dyt_ref[pl.ds(which * n, n), :] = dy_ref[:, at].T

    def put(w_in, w_out, units):
        size = w_out.shape[0]
        block = xn_ref.shape[0] // 4
        for k in range(4):
            at = pl.ds(k * block, block)
            made = ffn_unit(xn_ref[at, :], dy_ref[at, :], w_in[0], w_in[1], w_out[...])
            act_ref[at, :size], dgate_ref[at, :size], dup_ref[at, :size] = made
        for k, (left, right) in enumerate(((xt_ref, dgate_ref), (xt_ref, dup_ref), (dyt_ref, act_ref))):
            both = dot(left[...], right[:, :size])
            mine_ref[k, :, units] = both[:n]
            away_ref[k, :, units] = both[n:]

    size = weights[1].shape[0]
    put(weights[0], weights[1], pl.ds(pl.multiple_of(step * size, size), size))
    if tail:

        @pl.when(step == pl.num_programs(0) - 1)
        def _():
            rest = weights[3].shape[0]
            put(weights[2], weights[3], pl.ds(mine_ref.shape[2] - rest, rest))


def turn_kernel(place, xn_ref, got_ref, out_ref):
    _, n, both = out_ref.shape
    z, x = place[0] // 2, place[0] % 2
    for k in range(4):
        high = z // 2 if k % 2 == 0 else 1 - z // 2
        row = 2 * high + (z % 2 if k < 2 else 1 - z % 2)
        a = xn_ref[:, pl.ds(pl.multiple_of((2 * row + x) * n, n), n)]
        b = got_ref[:, pl.ds(pl.multiple_of(row * n, n), n)].astype(BF16)
        out_ref[k, :, pl.ds(0, both // 2)] = a.T
        out_ref[k, :, pl.ds(both // 2, both // 2)] = b.T


def mix_grad_kernel(turned_ref, *refs):
    keep_ref, send_ref = refs[-2:]
    both = turned_ref.shape[2]
    for c in range(keep_ref.shape[0]):
        own, got = refs[2 * c][...].astype(BF16), refs[2 * c + 1][...].astype(BF16)
        for k in range(4):
            a = turned_ref[k]
            (keep_ref if k < 2 else send_ref)[c, k % 2] = dot(a[:, : both // 2], own) + dot(a[:, both // 2 :], got)


def norm_back_kernel(place, p0, p1, p2, p3, hidden_ref, dy_ref, norm_ref, w_ref, mixed_ref, pre_ref, gain_ref, qe_ref, sum_ref, dpre_ref, dm_ref, dgain_ref, back_ref, dhidden_ref, db_ref, away_ref, dnorm_ref, dg_ref):
    core, head, x = place[0], place[1], place[2]
    place_halves(dhidden_ref, core, (p0, p1, p2, p3))
    d, hidden = dhidden_ref[...], hidden_ref[...]
    scale = rms_scale(hidden)
    hat = hidden * scale
    dnorm_ref[...] = jnp.sum(d * hat, axis=0, keepdims=True)
    dhidden = dy_ref[...].astype(F32) + norm_back(d, norm_ref[...], scale, hat)
    dhidden_ref[...] = dhidden
    db_ref[...] = dhidden.astype(BF16)
    n = away_ref.shape[1]
    away_ref[...] = db_ref[:, pl.ds(pl.multiple_of((2 * head + 1 - x) * n, n), n)].astype(F32)
    dg_ref[...] = dot(db_ref[...], w_ref[...], NT)
    slots, heads = sum_ref.shape[:2]
    for h in range(heads):
        cols = pl.ds(h * HD, HD)
        gain = gain_ref[:, cols]
        total = jnp.zeros((1, HD), F32)
        for s in range(slots):
            rows = pl.ds(s * HD, HD)
            mixed, pre, dgated = mixed_ref[rows, cols], pre_ref[0, rows, cols], dg_ref[rows, cols]
            scale = rms_scale(mixed)
            hat = mixed * scale
            sig = sigmoid(pre)
            swish = pre * sig
            total += jnp.sum(dgated * hat * swish, axis=0, keepdims=True)
            dpre_ref[rows, cols] = (dgated * hat * gain * (sig * (1.0 + pre * (1.0 - sig)))).astype(BF16).astype(F32)
            dm = norm_back(dgated * swish, gain, scale, hat).astype(BF16)
            dm_ref[rows, cols] = dm
            back_ref[s, h, pl.ds(0, HD), :] = dot(dm, qe_ref[rows, cols], TN)
            back_ref[s, h, pl.ds(HD, 8), :] = sum_ref[s, h, pl.ds(HD, 8), :]
        dgain_ref[:, cols] = total


def intra_back_kernel(dm_ref, qe_ref, ke_ref, proj_ref, c_ref, state_ref, dq_ref, dk_ref, dv_ref, dl_ref):
    slots, heads = state_ref.shape[:2]
    lower = triangle("lower")
    upper = triangle("upper").astype(BF16)
    for s in range(slots):
        rows = pl.ds(s * HD, HD)
        for h in range(heads):
            cols = pl.ds(h * HD, HD)
            dm, qe, ke, cum = (r[rows, cols] for r in (dm_ref, qe_ref, ke_ref, c_ref))
            vb = proj_ref[2, rows, cols].astype(BF16)
            dscores = jnp.where(lower, dot(dm, vb, NT), 0.0).astype(BF16)
            to_q = dot(dscores, ke) + dot(dm, state_ref[s, h].astype(BF16))
            to_k = dot(dscores, qe, TN)
            pre = proj_ref[0, rows, cols]
            sig = sigmoid(pre)
            dq_ref[rows, cols] = (jnp.exp(cum) * to_q * (sig * (1.0 + pre * (1.0 - sig)))).astype(BF16).astype(F32)
            dk_ref[rows, cols] = jnp.exp(-cum) * to_k
            scores = jnp.where(lower, dot(qe, ke, NT), 0.0).astype(BF16)
            dv_ref[rows, cols] = dot(scores, dm, TN)
            dl_ref[rows, cols] = exact_dot(upper, qe.astype(F32) * to_q - ke.astype(F32) * to_k)


def state_back_kernel(pos, lengths, carried_ref, state_ref, ke_ref, forget_ref, value_ref, c_ref, bound_ref, dk_ref, dv_ref, dl_ref, dfv_ref, dbound_ref):
    slots, heads = state_ref.shape[:2]
    strict = triangle("strict").astype(BF16)
    for h in range(heads):
        cols = pl.ds(h * HD, HD)
        bound = bound_ref[:, cols]
        total = jnp.zeros((1, HD), F32)
        for s in range(slots):
            rows = pl.ds(s * HD, HD)
            ok = valid_rows(pos[0], lengths[s])
            cum, ke = c_ref[rows, cols], ke_ref[rows, cols]
            ending = carried_ref[s, h] * jnp.exp(cum[HD - 1 :, :])
            ending_low = ending.astype(BF16)
            to_k = dot(value_ref[0, rows, cols].astype(BF16), ending_low)
            dfv_ref[1, rows, cols] = (dv_ref[rows, cols] + dot(ke, ending_low, NT)).astype(BF16).astype(F32)
            through = jnp.sum(ending * state_ref[s, h], axis=0, keepdims=True)
            dlogf = dl_ref[rows, cols] + exact_dot(strict, ke.astype(F32) * to_k) + through
            dkeys = dk_ref[rows, cols] + jnp.exp(-cum) * to_k
            sig, forget = open_forget(forget_ref[0, rows, cols], bound, ok)
            dforget = jnp.where(ok, dlogf / forget - dkeys, 0.0)
            total += jnp.sum(dforget * (1.0 - sig), axis=0, keepdims=True)
            dfv_ref[0, rows, cols] = (dforget * (1.0 - bound) * sig * (1.0 - sig)).astype(BF16).astype(F32)
        dbound_ref[:, cols] = total


SMEM = pl.BlockSpec(memory_space=pltpu.SMEM)


def whole(shape, *index):
    index = index or (0,) * len(shape)
    return pl.BlockSpec(shape, lambda *_: index)


def sds(shape, dtype=F32):
    return jax.ShapeDtypeStruct(shape, dtype)


def call(kernel, name, outs, in_specs, out_specs, flops, moved, grid=(1,), scratch=(), vmem=48, aliases=None):
    return pl.pallas_call(
        kernel,
        name=name,
        grid=grid,
        out_shape=outs,
        in_specs=in_specs,
        out_specs=out_specs,
        scratch_shapes=list(scratch),
        input_output_aliases=aliases or {},
        compiler_params=pltpu.CompilerParams(vmem_limit_bytes=vmem * MIB),
        cost_estimate=pl.CostEstimate(flops=int(flops), bytes_accessed=int(moved), transcendentals=0),
    )


def entering_all(packed, backward):
    count, mine = lax.axis_size("seq"), lax.axis_index("seq")
    pieces = lax.all_gather(packed, "seq")
    if backward:
        pieces, mine = pieces[::-1], count - 1 - mine

    def step(position, state):
        piece = pieces[position]
        longer = piece[:, :, HD : HD + 1] * state + piece[:, :, :HD]
        return jnp.where(position < mine, longer, state)

    return lax.fori_loop(0, count - 1, step, jnp.zeros_like(packed[:, :, :HD]))


def decay(a):
    return a[:, HD : HD + 1]


def state(a):
    return a[:, :HD]


def join(a, b):
    both = decay(b) * state(a) + state(b)
    return jnp.concatenate([both, jnp.broadcast_to(decay(a) * decay(b), (a.shape[0], 8, HD))], axis=1)


def is_first(backward):
    is_low = lax.axis_index("seq") % 2 == 0
    return is_low, (~is_low if backward else is_low)


def pair_states(packed, backward):
    packed = packed.reshape(-1, PACKED, HD)
    half = packed.shape[0] // 2
    is_low, first = is_first(backward)
    mine = jnp.where(is_low, packed[:half], packed[half:])
    other = lax.ppermute(jnp.where(is_low, packed[half:], packed[:half]), "seq", X_SWAP)
    return jnp.where(first, mine, other), jnp.where(first, other, mine)


def pass_states(pair, backward):
    step = -1 if backward else 1
    before = lax.ppermute(pair, "seq", z_line(step))
    further = lax.ppermute(join(before, pair), "seq", z_line(2 * step))
    return decay(before) * state(further) + state(before)


def enter_states(early, into_first, shape, backward):
    is_low, first = is_first(backward)
    into_second = decay(early) * into_first + state(early)
    kept = jnp.where(first, into_first, into_second)
    given = lax.ppermute(jnp.where(first, into_second, into_first), "seq", X_SWAP)
    low, high = jnp.where(is_low, kept, given), jnp.where(is_low, given, kept)
    return jnp.concatenate([low, high]).reshape(shape)


def tie(*values):
    return lax.optimization_barrier(values)


def core_swap(a):
    return lax.ppermute(a, "head", CORE_SWAP)


def y_swap(a):
    return lax.ppermute(a, "head", Y_SWAP)


def x_swap(a):
    return lax.ppermute(a, "seq", X_SWAP)


def assemble(blocks, into=None, first=0):
    head = lax.axis_index("head")
    tokens, n = blocks[0][0].shape
    width = 4 * n
    here = jnp.stack([a for block in blocks for a in block]).reshape(len(blocks), 2, tokens, n)
    there = core_swap(here)
    at = jnp.stack([(head ^ k) * n for k in range(4)]).astype(jnp.int32)
    piece = pl.BlockSpec((1, 2, tokens, n), lambda i: (i, 0, 0, 0))
    out_spec = pl.BlockSpec((tokens, width), lambda i: (i + first, 0))
    grid = (len(blocks),)
    moved = 6 * len(blocks) * tokens * width
    if into is None:
        return call(assemble_kernel, "assemble", sds((len(blocks) * tokens, width), BF16), [SMEM, piece, piece], out_spec, 0, moved, grid=grid)(at, here, there)
    kept = pl.BlockSpec(memory_space=pl.ANY)
    return call(assemble_kernel, "assemble", sds(into.shape, BF16), [SMEM, piece, piece, kept], out_spec, 0, moved, grid=grid, aliases={3: 0})(at, here, there, into)


def join_heads(parts, into, first):
    heads, rows, n = parts.shape
    tokens = into.shape[0] // 4
    return call(
        join_kernel,
        "join",
        sds(into.shape, BF16),
        [pl.BlockSpec((heads, tokens, n), lambda i: (0, i, 0)), pl.BlockSpec(memory_space=pl.ANY)],
        pl.BlockSpec((tokens, heads * n), lambda i: (i + first, 0)),
        0,
        6 * rows * heads * n,
        grid=(rows // tokens,),
        aliases={1: 0},
    )(parts, into)


class Calls:
    def __init__(self, slots, length, width, local, units):
        self.slots, self.count, self.width, self.local, self.units = slots, slots * length, width, local, units
        self.heads = local // HD
        self.pair = 2 * HD
        self.steps = units // self.pair
        self.rest = units - self.steps * self.pair
        self.tall, self.channel = whole((self.count, width)), whole((self.count, local))
        self.row, self.w_spec = whole((1, local)), whole((local, width))
        self.half, self.half_spec = sds((self.count, width // 2)), whole((self.count, width // 2))
        self.state_shape = (slots, self.heads, HD, HD)
        self.packed_shape = (slots, self.heads, PACKED, HD)
        self.state_spec, self.packed_spec = whole(self.state_shape), whole(self.packed_shape)
        self.wide, self.norm_row = sds((self.count, width)), whole((1, width))
        self.low = sds((self.count, local), BF16)
        self.full = sds((self.count, local))

    def proj(self, *index):
        return whole((1, self.count, self.local), *index)

    def project(self, pos, lengths, tokens, norm, weight, bound):
        count, width, local, pair = self.count, self.width, self.local, self.pair
        block = pl.BlockSpec((count, pair), lambda i: (0, i))
        return call(
            project_kernel,
            "project",
            [sds((count, width), BF16), self.half, sds((4, count, local)), self.full, self.low, self.low, self.full, sds(self.packed_shape)],
            [SMEM, SMEM, self.tall, whole((1, width)), pl.BlockSpec((4, width, pair), lambda i: (0, 0, i)), pl.BlockSpec((1, pair), lambda i: (0, i))],
            [self.tall, self.half_spec, pl.BlockSpec((4, count, pair), lambda i: (0, 0, i))] + [block] * 4 + [pl.BlockSpec((self.slots, 2, PACKED, HD), lambda i: (0, i, 0, 0))],
            8 * count * width * local,
            20e6,
            grid=(local // pair,),
        )(pos, lengths, tokens, norm, weight, bound)

    def mixer_out(self, core, qe, states, intra, proj, gain, weight):
        return call(
            mixer_out_kernel,
            "mixer_out",
            [self.full, self.low, self.full, self.half, self.half],
            [SMEM, self.channel, self.state_spec, self.channel, self.proj(3, 0, 0), self.row, self.w_spec],
            [self.channel] * 3 + [self.half_spec] * 2,
            2 * self.count * self.width * self.local,
            10e6,
        )(core, qe, states, intra, proj, gain, weight)

    def ffn_specs(self, first=0, tail=True):
        width, pair, rest = self.width, self.pair, self.rest
        last = self.steps * pair // rest
        specs = [
            pl.BlockSpec((2, width, pair), lambda i: (0, 0, i + first)),
            pl.BlockSpec((pair, width), lambda i: (i + first, 0)),
            whole((2, width, rest), 0, 0, last),
            whole((rest, width), last, 0),
        ]
        return specs if tail else specs[:2]

    def ffn_own(self, core, xn2, dy, ffn_in, ffn_out):
        return call(
            ffn_own_kernel,
            "ffn_own",
            [self.wide, self.half, self.half],
            [SMEM, self.tall, self.tall, *self.ffn_specs()],
            [self.tall, self.half_spec, self.half_spec],
            12 * self.count * self.width * self.units,
            30e6,
            grid=(self.steps,),
            scratch=[pltpu.VMEM((self.count, self.width), F32)],
            vmem=60,
        )(core, xn2, dy, ffn_in, ffn_out, ffn_in, ffn_out)

    def norm_back(self, place, parts, hidden, dy, norm, weight, mixed, proj, gain, qe, packed):
        n = self.width // 8
        return call(
            norm_back_kernel,
            "norm_back",
            [self.full, self.low, sds((1, self.local)), sds(self.packed_shape), self.wide, sds((self.count, self.width), BF16), sds((self.count, n)), sds((1, self.width))],
            [SMEM] + [self.half_spec] * 4 + [self.tall, self.tall, self.norm_row, self.w_spec, self.channel, self.proj(3, 0, 0), self.row, self.channel, self.packed_spec],
            [self.channel, self.channel, self.row, self.packed_spec, self.tall, self.tall, whole((self.count, n)), self.norm_row],
            2 * self.count * self.width * self.local,
            10e6,
            scratch=[pltpu.VMEM((self.count, self.local), F32)],
        )(place, *parts, hidden, dy, norm, weight, mixed, proj, gain, qe, packed)

    def second_norm(self, place, tokens, parts, gain, lines):
        quarter = self.width // 4
        return call(
            second_norm_kernel,
            "second_norm",
            [self.wide, sds((lines * self.count, self.width), BF16), sds((self.count, quarter))],
            [SMEM, self.tall] + [self.half_spec] * 4 + [self.norm_row],
            [self.tall, self.tall, whole((self.count, quarter))],
            0,
            10e6,
        )(place, tokens, *parts, gain)

    def first_grad(self, dproj, weight):
        quarter = self.width // 4
        return call(
            first_grad_kernel,
            "first_grad",
            self.wide,
            [self.channel] * 4 + [pl.BlockSpec((4, quarter, self.local), lambda i: (0, i, 0))],
            pl.BlockSpec((self.count, quarter), lambda i: (0, i)),
            8 * self.count * self.width * self.local,
            15e6,
            grid=(4,),
        )(*dproj, weight)

    def first_back(self, dxn1, dhidden, tokens, gain):
        return call(
            first_back_kernel,
            "first_back",
            [sds((self.count, self.width), BF16), sds((1, self.width))],
            [self.tall, self.tall, self.tall, self.norm_row],
            [self.tall, self.norm_row],
            0,
            10e6,
        )(dxn1, dhidden, tokens, gain)

    def intra_back(self, dmixed, qe, ke, proj, cum, states):
        return call(
            intra_back_kernel,
            "intra_back",
            [self.full] * 4,
            [self.channel, self.channel, self.channel, whole((3, self.count, self.local)), self.channel, self.state_spec],
            [self.channel] * 4,
            14 * self.count * self.local * HD,
            10e6,
        )(dmixed, qe, ke, proj, cum, states)

    def state_back(self, pos, lengths, carried, states, ke, proj, cum, bound, dkeys, dvalues, dlogf):
        return call(
            state_back_kernel,
            "state_back",
            [sds((2, self.count, self.local)), sds((1, self.local))],
            [SMEM, SMEM, self.state_spec, self.state_spec, self.channel, self.proj(1, 0, 0), self.proj(2, 0, 0), self.channel, self.row] + [self.channel] * 3,
            [whole((2, self.count, self.local)), self.row],
            8 * self.count * self.local * HD,
            10e6,
        )(pos, lengths, carried, states, ke, proj, proj, cum, bound, dkeys, dvalues, dlogf)

    def widen(self, head, dy, lines):
        quarter = self.width // 4
        return call(
            widen_kernel,
            "widen",
            [sds((self.count, quarter)), sds((lines * self.count, self.width), BF16)],
            [SMEM, self.tall],
            [whole((self.count, quarter)), self.tall],
            0,
            4e6,
        )(head, dy)

    def turn(self, place, xn, got):
        shape = (4, self.width // 8, 2 * self.count)
        return call(turn_kernel, "turn", sds(shape, BF16), [SMEM, self.tall, self.half_spec], whole(shape), 0, 6e6)(place, xn, got)

    def mix_grad(self, turned, *grads):
        shape = (len(grads) // 2, 2, self.width // 8, self.local)
        return call(
            mix_grad_kernel,
            "mix_grad",
            [sds(shape)] * 2,
            [whole(turned.shape)] + [self.channel] * len(grads),
            [whole(shape)] * 2,
            len(grads) * self.count * self.width * self.local,
            10e6,
        )(turned, *grads)

    def ffn_grad(self, rows, xn, dy, ffn_in, ffn_out, first, steps):
        n, pair = self.width // 8, self.pair
        tail = first + steps == self.steps and self.rest > 0
        units = steps * pair + self.rest * tail
        out = sds((3, n, units))
        line = whole(xn.shape)
        return call(
            functools.partial(ffn_grad_kernel, tail),
            "ffn_grad",
            [out, out],
            [SMEM, line, line] + self.ffn_specs(first, tail),
            [whole(out.shape)] * 2,
            6 * xn.shape[0] * (self.width + 2 * n) * units,
            20e6,
            grid=(steps,),
            scratch=[pltpu.VMEM((2 * n, xn.shape[0]), BF16)] * 2 + [pltpu.VMEM((xn.shape[0], pair), BF16)] * 3,
            vmem=62,
        )(rows, xn, dy, *([ffn_in, ffn_out] * (2 if tail else 1)))


def scalar(v):
    return jnp.asarray(v, jnp.int32).reshape(1)


def body(tokens, lengths, norm_first, mix_weight, lower_bound, out_gain, w_out, norm_second, ffn_in, ffn_out, cotangent):
    shape = tokens.shape
    slots, length, width = shape
    local = lower_bound.shape[0]
    do = Calls(slots, length, width, local, ffn_out.shape[0])
    fast = lax.axis_size("seq") == 8 and lax.axis_size("head") == 4
    run = run_lines if fast else run_any
    output, grad_tokens, small, weights = run(
        do,
        tokens.reshape(do.count, width),
        lengths,
        norm_first.reshape(1, width),
        mix_weight,
        lower_bound.reshape(1, local),
        out_gain.reshape(1, local),
        w_out,
        norm_second.reshape(1, width),
        ffn_in,
        ffn_out,
        cotangent.reshape(do.count, width),
    )
    first, second = small[:width], small[width : 2 * width]
    bound_sum, gain_sum = small[2 * width : 2 * width + local], small[2 * width + local :]
    return (output.reshape(shape), grad_tokens.reshape(shape), first, weights[0], bound_sum, gain_sum, weights[1], second, weights[2], weights[3])


def run_any(do, tokens, lengths, norm_first, mix_weight, bound, gain, w_out, norm_second, ffn_in, ffn_out, dy):
    def total(halves):
        low, high = jnp.split(lax.psum(jnp.concatenate(halves, axis=1), "head"), 2, axis=1)
        return low, jnp.zeros_like(low), high, jnp.zeros_like(high)

    pos, core = scalar(lax.axis_index("seq")), scalar(0)
    nowhere = jnp.zeros((3,), jnp.int32)
    xn1, _, proj, cum, qe, ke, intra, packed = do.project(pos, lengths, tokens, norm_first, mix_weight, bound)
    states = entering_all(packed, False)
    mixed, gated, _, *halves = do.mixer_out(core, qe, states, intra, proj, gain, w_out)
    hidden, xn2, _ = do.second_norm(nowhere, tokens, total(halves), norm_second, 1)
    ffn, dkeep, dsend = do.ffn_own(core, xn2, dy, ffn_in, ffn_out)
    output = (hidden + lax.psum(ffn, "head")).astype(BF16)
    dpre_gate, dmixed, part_gain, back, dhidden, dbranch, _, part_norm_second = do.norm_back(
        nowhere, total((dkeep, dsend)), hidden, dy, norm_second, w_out, mixed, proj, gain, qe, packed
    )
    carried = entering_all(back, True)
    dpre_query, dkeys, dvalues, dlogf = do.intra_back(dmixed, qe, ke, proj, cum, states)
    dpre_fv, part_bound = do.state_back(pos, lengths, carried, states, ke, proj, cum, bound, dkeys, dvalues, dlogf)
    dproj = (dpre_query, dpre_fv[0], dpre_fv[1], dpre_gate)
    grad_tokens, part_norm_first = do.first_back(lax.psum(do.first_grad(dproj, mix_weight), "head"), dhidden, tokens, norm_first)
    weights = weight_grads_whole(xn1, dproj, gated, dbranch, xn2, dy, ffn_in, ffn_out)
    small = lax.psum(jnp.concatenate([part_norm_first[0], part_norm_second[0], part_bound[0], part_gain[0]]), "seq")
    return output, grad_tokens, small, weights


def run_lines(do, tokens, lengths, norm_first, mix_weight, bound, gain, w_out, norm_second, ffn_in, ffn_out, dy):
    width, local, quarter = do.width, do.local, do.width // 4
    seq, head = lax.axis_index("seq"), lax.axis_index("head")
    x, z = seq % 2, seq // 2
    seq_at, core = scalar(seq), scalar(head % 2)
    place = jnp.stack([head % 2, head, x]).astype(jnp.int32)

    def shift(a, k):
        return lax.ppermute(a, "seq", z_shift(k))

    def sum_cores(keep, send):
        return keep + core_swap(send)

    def sum_near(keep, send):
        got = lax.ppermute(send, "seq", flip(2))
        return (keep[:, 0], got[:, 0]), keep[:, 1] + got[:, 1]

    def sum_far(near):
        (a, b), far = near
        return a + b + lax.ppermute(far, "seq", flip(4))

    dy_quarter, dy_all = do.widen(scalar(head), dy, 4)
    dy1 = shift(dy_quarter, 1)
    xn1, xn1_away, proj, cum, qe, ke, intra, packed = do.project(seq_at, lengths, tokens, norm_first, mix_weight, bound)
    early, late = pair_states(packed, False)
    early, late, dy1 = tie(early, late, dy1)

    into = pass_states(join(early, late), False)
    dy1_over = y_swap(dy1)
    early, into, dy1_over, dy_quarter = tie(early, into, dy1_over, dy_quarter)

    states = enter_states(early, into, do.state_shape, False)
    mixed, gated, gated_wide, keep, send = do.mixer_out(core, qe, states, intra, proj, gain, w_out)
    half = sum_cores(keep, send)
    half, dy_quarter, xn1_away, dy1, dy1_over = tie(half, dy_quarter, xn1_away, dy1, dy1_over)

    over = y_swap(half)
    half_other = core_swap(half)
    dy2 = shift(dy_quarter, 2)
    xn1_got = x_swap(xn1_away)
    dy_all = assemble([(dy1, dy1_over)], dy_all, 1)
    half, half_other, over, dy2, gated_wide, xn1_got, dy_all = tie(half, half_other, over, dy2, gated_wide, xn1_got, dy_all)

    dy2_over = y_swap(dy2)
    hidden, xn_all, xn_quarter = do.second_norm(place, tokens, (half, over, half_other, core_swap(over)), norm_second, 4)
    xnl1 = shift(xn_quarter, 1)
    gated_got = x_swap(gated_wide)
    ffn, dkeep, dsend = do.ffn_own(core, xn_all, dy, ffn_in, ffn_out)
    dkeep, dsend, xn_quarter, dy2_over, xnl1, gated_got, ffn = tie(dkeep, dsend, xn_quarter, dy2_over, xnl1, gated_got, ffn)

    dhalf = sum_cores(dkeep, dsend)
    dhalf, xn_quarter, dy_all, xn1_got = tie(dhalf, xn_quarter, dy_all, xn1_got)
    dover = y_swap(dhalf)
    dhalf_other = core_swap(dhalf)
    xnl2 = shift(xn_quarter, 2)
    dy_all = assemble([(dy2, dy2_over)], dy_all, 2)
    xn1_turned = do.turn(seq_at, xn1, xn1_got)
    dhalf, dover, dhalf_other, xnl2, xn_quarter, xnl1, dy_all, xn1_turned, ffn = tie(dhalf, dover, dhalf_other, xnl2, xn_quarter, xnl1, dy_all, xn1_turned, ffn)
    ffn = lax.psum(ffn, "head")

    xnl3 = shift(xn_quarter, 3)
    dpre_gate, dmixed, part_gain, back, dhidden, dbranch, dbranch_away, part_norm_second = do.norm_back(
        place, (dhalf, dover, dhalf_other, core_swap(dover)), hidden, dy, norm_second, w_out, mixed, proj, gain, qe, packed
    )
    back, dpre_gate, dmixed, dbranch, dbranch_away, dy_quarter = tie(back, dpre_gate, dmixed, dbranch, dbranch_away, dy_quarter)

    early, late = pair_states(back, True)
    dy3 = shift(dy_quarter, 3)
    early, late, dpre_gate, dmixed, dbranch_away, xnl3, dy3 = tie(early, late, dpre_gate, dmixed, dbranch_away, xnl3, dy3)
    xn_parts = lax.all_gather(jnp.concatenate([xnl1, xnl2, xnl3]), "head")
    into = pass_states(join(early, late), True)
    dbranch_own = x_swap(dbranch_away)
    dpre_query, dkeys, dvalues, dlogf = do.intra_back(dmixed, qe, ke, proj, cum, states)
    gate_got = x_swap(dpre_gate)
    dy3_over = y_swap(dy3)
    early, into, gate_got, dpre_query, dbranch_own, dy3_over = tie(early, into, gate_got, dpre_query, dbranch_own, dy3_over)

    gate = do.mix_grad(xn1_turned, dpre_gate, gate_got)
    early, into, gate, dbranch_own, dy3_over, ffn = tie(early, into, gate, dbranch_own, dy3_over, ffn)

    near_gate = sum_near(*gate)
    dbranch_over = y_swap(dbranch_own)
    carried = enter_states(early, into, do.state_shape, True)
    dy_all = assemble([(dy3, dy3_over)], dy_all, 3)
    dpre_fv, part_bound = do.state_back(seq_at, lengths, carried, states, ke, proj, cum, bound, dkeys, dvalues, dlogf)
    dpre_fv, dpre_query, dbranch_over, dy_all = tie(dpre_fv, dpre_query, dbranch_over, dy_all)

    fv_got = x_swap(dpre_fv)
    down = do.mix_grad(do.turn(seq_at, dbranch, assemble([(dbranch_own, dbranch_over)])), gated, gated_got)
    near_down = sum_near(*down)
    near_gate, down = tie(near_gate, down)
    grad_gate = sum_far(near_gate)
    dxn1 = do.first_grad((dpre_query, dpre_fv[0], dpre_fv[1], dpre_gate), mix_weight)
    xn_parts, dxn1, ffn = tie(xn_parts, dxn1, ffn)
    fv_got, grad_gate, near_down, xn_all, dpre_query, xn_parts = tie(fv_got, grad_gate, near_down, xn_all, dpre_query, xn_parts)
    dxn1 = lax.psum(dxn1, "head")

    rows = jnp.stack([seq, seq ^ 1]).astype(jnp.int32)
    query_got = x_swap(dpre_query)
    grad_w_out = sum_far(near_down)
    forget_values = do.mix_grad(xn1_turned, dpre_fv[0], fv_got[0], dpre_fv[1], fv_got[1])
    forget_values, xn_all, xn_parts = tie(forget_values, xn_all, xn_parts)
    near_fv = sum_near(*forget_values)
    xn_all = join_heads(xn_parts, xn_all, 1)
    mine_a, away_a = do.ffn_grad(rows, xn_all, dy_all, ffn_in, ffn_out, 0, 2)
    away_a, xn_all, query_got = tie(away_a, xn_all, query_got)
    got_a = x_swap(away_a)
    query = do.mix_grad(xn1_turned, dpre_query, query_got)
    mine_b, away_b = do.ffn_grad(rows, xn_all, dy_all, ffn_in, ffn_out, 2, 2)
    near_fv, grad_w_out, got_a, query, away_b, xn_all, dhidden, hidden = tie(near_fv, grad_w_out, got_a, query, away_b, xn_all, dhidden, hidden)

    got_b = x_swap(away_b)
    near_query, grad_fv = sum_near(*query), sum_far(near_fv)
    grad_tokens, part_norm_first = do.first_back(dxn1, dhidden, tokens, norm_first)
    mine_c, away_c = do.ffn_grad(rows, xn_all, dy_all, ffn_in, ffn_out, 4, do.steps - 4)
    small = jnp.concatenate([part_norm_first[0], part_norm_second[0], part_bound[0], part_gain[0]])
    small = small + lax.ppermute(small, "seq", flip(1))
    output = (hidden + ffn).astype(BF16)
    got_b, near_query, grad_fv, small, away_c, output = tie(got_b, near_query, grad_fv, small, away_c, output)

    got_c = x_swap(away_c)
    grad_query = sum_far(near_query)
    for bit in (2, 4):
        small = small + lax.ppermute(small, "seq", flip(bit))
    parts = ((mine_a, got_a), (mine_b, got_b), (mine_c, got_c))
    grad_in = jnp.concatenate([mine[:2] + got[:2] for mine, got in parts], axis=2)
    grad_out = jnp.concatenate([(mine[2] + got[2]).T for mine, got in parts], axis=0)
    grad_mix = jnp.concatenate([grad_query, grad_fv, grad_gate])
    return output, grad_tokens, small, (grad_mix, grad_w_out[0].T, grad_in, grad_out)


def weight_grads_whole(xn1, dproj, gated, dbranch, xn2, dy, ffn_in, ffn_out):
    gate, up = dot(xn2, ffn_in[0]), dot(xn2, ffn_in[1])
    dact = dot(dy, ffn_out, NT)
    sig = sigmoid(gate)
    swish = gate * sig
    act = (swish * up).astype(BF16)
    dgate = (dact * up * (sig * (1.0 + gate * (1.0 - sig)))).astype(BF16)
    dup = (dact * swish).astype(BF16)

    def scatter(a, axis):
        return lax.psum_scatter(a, "seq", scatter_dimension=axis, tiled=True)

    return (
        jnp.stack([scatter(dot(xn1, d.astype(BF16), TN), 0) for d in dproj]),
        scatter(dot(gated, dbranch, TN), 1),
        jnp.stack([scatter(dot(xn2, d, TN), 0) for d in (dgate, dup)]),
        scatter(dot(act, dy, TN), 1),
    )


def solution(mesh):
    in_specs = (
        P(None, "seq", None),
        P(),
        P(),
        P(None, None, "head"),
        P("head"),
        P("head"),
        P("head", None),
        P(),
        P(None, None, "head"),
        P("head", None),
        P(None, "seq", None),
    )
    out_specs = (
        P(None, "seq", None),
        P(None, "seq", None),
        P(),
        P(None, "seq", "head"),
        P("head"),
        P("head"),
        P("head", "seq"),
        P(),
        P(None, "seq", "head"),
        P("head", "seq"),
    )
    return jax.shard_map(body, mesh=mesh, in_specs=in_specs, out_specs=out_specs, check_vma=False)
```

```python
import functools

import jax
import jax.numpy as jnp
from jax import lax
from jax.experimental import pallas as pl
from jax.experimental.pallas import tpu as pltpu
from jax.sharding import PartitionSpec as P

HD = 128
EPS = 1e-06
F32 = jnp.float32
BF16 = jnp.bfloat16
MIB = 1 << 20
PACKED = HD + 8

X_SWAP = [(p, p ^ 1) for p in range(8)]
CORE_SWAP = [(h, h ^ 1) for h in range(4)]
Y_SWAP = [(h, h ^ 2) for h in range(4)]


def z_shift(k):
    return [(p, (p + 2 * k) % 8) for p in range(8)]


def z_line(k):
    return [(p, p + 2 * k) for p in range(8) if 0 <= p + 2 * k < 8]


def flip(bit):
    return [(p, p ^ bit) for p in range(8)]


def rms_scale(v):
    return lax.rsqrt(jnp.mean(v * v, axis=-1, keepdims=True) + EPS)


def norm_back(grad_normed, gain, scale, normed_hat):
    scaled = grad_normed * gain
    return scale * (scaled - normed_hat * jnp.mean(scaled * normed_hat, axis=-1, keepdims=True))


def dot(a, b, dims=((1,), (0,))):
    return lax.dot_general(a, b, (dims, ((), ())), preferred_element_type=F32)


NT = ((1,), (1,))
TN = ((0,), (0,))


def sigmoid(v):
    return 1.0 / (1.0 + jnp.exp(-v))


def triangle(kind):
    row = lax.broadcasted_iota(jnp.int32, (HD, HD), 0)
    col = lax.broadcasted_iota(jnp.int32, (HD, HD), 1)
    return {"lower": row >= col, "strict": row > col, "upper": row <= col}[kind]


def exact_dot(ones, v, parts=3):
    total = None
    for _ in range(parts):
        part = v.astype(BF16)
        v = v - part.astype(F32)
        term = dot(ones, part)
        total = term if total is None else total + term
    return total


def valid_rows(pos, length):
    row = lax.broadcasted_iota(jnp.int32, (HD, 1), 0)
    return (pos * HD + row) < length


def open_forget(pre, bound, ok):
    sig = sigmoid(pre)
    return sig, jnp.where(ok, bound + (1.0 - bound) * sig, 1.0)


def project_kernel(pos, lengths, x_ref, gain_ref, w_ref, bound_ref, xn_ref, away_ref, proj_ref, c_ref, qe_ref, ke_ref, intra_ref, sum_ref):
    @pl.when(pl.program_id(0) == 0)
    def _():
        x = x_ref[...].astype(F32)
        xn_ref[...] = (x * rms_scale(x) * gain_ref[...]).astype(BF16)
        n = away_ref.shape[1] // 4
        for z in range(4):
            at = pl.multiple_of((2 * z + 1 - pos[0] % 2) * n, n)
            away_ref[:, pl.ds(z * n, n)] = xn_ref[:, pl.ds(at, n)].astype(F32)

    xn = xn_ref[...]
    for c in range(4):
        proj_ref[c] = dot(xn, w_ref[c])
    slots, heads = sum_ref.shape[:2]
    lower = triangle("lower")
    ones = lower.astype(BF16)
    for s in range(slots):
        rows = pl.ds(s * HD, HD)
        ok = valid_rows(pos[0], lengths[s])
        _, forget = open_forget(proj_ref[1, rows, :], bound_ref[...], ok)
        c_ref[rows, :] = exact_dot(ones, jnp.log(forget), 2)
        for h in range(heads):
            cols = pl.ds(h * HD, HD)
            pre_q, v, cum = proj_ref[0, rows, cols], proj_ref[2, rows, cols], c_ref[rows, cols]
            keys = 1.0 - forget[:, h * HD : (h + 1) * HD]
            qe = (pre_q * sigmoid(pre_q) * jnp.exp(cum)).astype(BF16)
            ke = (keys * jnp.exp(-cum)).astype(BF16)
            qe_ref[rows, cols] = qe
            ke_ref[rows, cols] = ke
            vb = v.astype(BF16)
            scores = jnp.where(lower, dot(qe, ke, NT), 0.0).astype(BF16)
            intra_ref[rows, cols] = dot(scores, vb)
            last = cum[HD - 1 :, :]
            to_end = (keys * jnp.exp(last - cum)).astype(BF16)
            sum_ref[s, h, pl.ds(0, HD), :] = dot(vb, to_end, TN)
            sum_ref[s, h, pl.ds(HD, 8), :] = jnp.broadcast_to(jnp.exp(last), (8, HD))


def split_store(keep_ref, send_ref, core, make):
    half = keep_ref.shape[1]
    keep_ref[...] = make(pl.multiple_of(core * half, half), half)
    send_ref[...] = make(pl.multiple_of((1 - core) * half, half), half)


def mixer_out_kernel(core, qe_ref, state_ref, intra_ref, pre_ref, gain_ref, w_ref, mixed_ref, gated_ref, wide_ref, keep_ref, send_ref):
    slots, heads = state_ref.shape[:2]
    for s in range(slots):
        rows = pl.ds(s * HD, HD)
        for h in range(heads):
            cols = pl.ds(h * HD, HD)
            mixed = intra_ref[rows, cols] + dot(qe_ref[rows, cols], state_ref[s, h].astype(BF16), NT)
            mixed_ref[rows, cols] = mixed
            pre = pre_ref[0, rows, cols]
            gated = mixed * rms_scale(mixed) * gain_ref[:, cols] * (pre * sigmoid(pre))
            gated_ref[rows, cols] = gated.astype(BF16)
            wide_ref[rows, cols] = gated_ref[rows, cols].astype(F32)
    split_store(keep_ref, send_ref, core[0], lambda at, n: dot(gated_ref[...], w_ref[:, pl.ds(at, n)]))


def ffn_unit(xn, dy, w_gate, w_up, w_out):
    gate, up = dot(xn, w_gate), dot(xn, w_up)
    dact = dot(dy, w_out, NT)
    sig = sigmoid(gate)
    swish = gate * sig
    act = (swish * up).astype(BF16)
    dgate = (dact * up * (sig * (1.0 + gate * (1.0 - sig)))).astype(BF16)
    dup = (dact * swish).astype(BF16)
    return act, dgate, dup


def ffn_own_kernel(core, xn_ref, dy_ref, in_ref, out_ref, in_tail, out_tail, f_acc, d_keep, d_send, d_acc):
    step = pl.program_id(0)

    @pl.when(step == 0)
    def _():
        f_acc[...] = jnp.zeros_like(f_acc)
        d_acc[...] = jnp.zeros_like(d_acc)

    def add(w_in, w_out):
        act, dgate, dup = ffn_unit(xn_ref[...], dy_ref[...], w_in[0], w_in[1], w_out[...])
        f_acc[...] += dot(act, w_out[...])
        d_acc[...] += dot(dgate, w_in[0], NT) + dot(dup, w_in[1], NT)

    add(in_ref, out_ref)

    @pl.when(step == pl.num_programs(0) - 1)
    def _():
        add(in_tail, out_tail)
        split_store(d_keep, d_send, core[0], lambda at, n: d_acc[:, pl.ds(at, n)])


def widen_kernel(at, a_ref, out_ref, copy_ref):
    n = out_ref.shape[1]
    out_ref[...] = a_ref[:, pl.ds(pl.multiple_of(at[0] * n, n), n)].astype(F32)
    copy_ref[...] = a_ref[...]


def place_halves(out_ref, core, parts):
    n, terms = out_ref.shape[1] // 2, len(parts) // 2
    for k, which in ((0, core), (1, 1 - core)):
        mine = parts[k * terms : (k + 1) * terms]
        at = pl.ds(pl.multiple_of(which * n, n), n)
        out_ref[:, at] = mine[0][...] if terms == 1 else mine[0][...] + mine[1][...]


def second_norm_kernel(place, x_ref, p0, p1, p2, p3, gain_ref, hidden_ref, xn_ref, quarter_ref):
    core, head = place[0], place[1]
    place_halves(hidden_ref, core, (p0, p1, p2, p3))
    hidden = x_ref[...].astype(F32) + hidden_ref[...]
    hidden_ref[...] = hidden
    xn_ref[...] = (hidden * rms_scale(hidden) * gain_ref[...]).astype(BF16)
    n = quarter_ref.shape[1]
    quarter_ref[...] = xn_ref[:, pl.ds(pl.multiple_of(head * n, n), n)].astype(F32)


def first_back_kernel(d_ref, dhidden_ref, x_ref, gain_ref, grad_ref, part_ref):
    x, d = x_ref[...].astype(F32), d_ref[...]
    scale = rms_scale(x)
    hat = x * scale
    part_ref[...] = jnp.sum(d * hat, axis=0, keepdims=True)
    grad_ref[...] = (dhidden_ref[...] + norm_back(d, gain_ref[...], scale, hat)).astype(BF16)


def first_grad_kernel(d0, d1, d2, d3, w_ref, out_ref):
    out_ref[...] = sum(dot(d[...].astype(BF16), w_ref[c], NT) for c, d in enumerate((d0, d1, d2, d3)))


def assemble_kernel(at, here_ref, there_ref, *refs):
    out_ref = refs[-1]
    n = here_ref.shape[-1]
    for k, piece in enumerate((here_ref, there_ref)):
        for over in range(2):
            out_ref[:, pl.ds(pl.multiple_of(at[2 * over + k], n), n)] = piece[0, over].astype(BF16)


def join_kernel(parts_ref, _, out_ref):
    n = parts_ref.shape[2]
    for k in range(parts_ref.shape[0]):
        out_ref[:, pl.ds(k * n, n)] = parts_ref[k].astype(BF16)


def ffn_grad_kernel(tail, rows, xn_ref, dy_ref, *refs):
    weights, (mine_ref, away_ref, xt_ref, dyt_ref, act_ref, dgate_ref, dup_ref) = refs[:-7], refs[-7:]
    step = pl.program_id(0)
    n = mine_ref.shape[1]

    @pl.when(step == 0)
    def _():
        for which in range(2):
            at = pl.ds(pl.multiple_of(rows[which] * n, n), n)
            xt_ref[pl.ds(which * n, n), :] = xn_ref[:, at].T
            dyt_ref[pl.ds(which * n, n), :] = dy_ref[:, at].T

    def put(w_in, w_out, units):
        size = w_out.shape[0]
        block = xn_ref.shape[0] // 4
        for k in range(4):
            at = pl.ds(k * block, block)
            made = ffn_unit(xn_ref[at, :], dy_ref[at, :], w_in[0], w_in[1], w_out[...])
            act_ref[at, :size], dgate_ref[at, :size], dup_ref[at, :size] = made
        for k, (left, right) in enumerate(((xt_ref, dgate_ref), (xt_ref, dup_ref), (dyt_ref, act_ref))):
            both = dot(left[...], right[:, :size])
            mine_ref[k, :, units] = both[:n]
            away_ref[k, :, units] = both[n:]

    size = weights[1].shape[0]
    put(weights[0], weights[1], pl.ds(pl.multiple_of(step * size, size), size))
    if tail:

        @pl.when(step == pl.num_programs(0) - 1)
        def _():
            rest = weights[3].shape[0]
            put(weights[2], weights[3], pl.ds(mine_ref.shape[2] - rest, rest))


def turn_kernel(place, xn_ref, got_ref, out_ref):
    _, n, both = out_ref.shape
    z, x = place[0] // 2, place[0] % 2
    for k in range(4):
        high = z // 2 if k % 2 == 0 else 1 - z // 2
        row = 2 * high + (z % 2 if k < 2 else 1 - z % 2)
        a = xn_ref[:, pl.ds(pl.multiple_of((2 * row + x) * n, n), n)]
        b = got_ref[:, pl.ds(pl.multiple_of(row * n, n), n)].astype(BF16)
        out_ref[k, :, pl.ds(0, both // 2)] = a.T
        out_ref[k, :, pl.ds(both // 2, both // 2)] = b.T


def mix_grad_kernel(turned_ref, *refs):
    keep_ref, send_ref = refs[-2:]
    both = turned_ref.shape[2]
    for c in range(keep_ref.shape[0]):
        own, got = refs[2 * c][...].astype(BF16), refs[2 * c + 1][...].astype(BF16)
        for k in range(4):
            a = turned_ref[k]
            (keep_ref if k < 2 else send_ref)[c, k % 2] = dot(a[:, : both // 2], own) + dot(a[:, both // 2 :], got)


def norm_back_kernel(place, p0, p1, p2, p3, hidden_ref, dy_ref, norm_ref, w_ref, mixed_ref, pre_ref, gain_ref, qe_ref, sum_ref, dpre_ref, dm_ref, dgain_ref, back_ref, dhidden_ref, db_ref, away_ref, dnorm_ref, dg_ref):
    core, head, x = place[0], place[1], place[2]
    place_halves(dhidden_ref, core, (p0, p1, p2, p3))
    d, hidden = dhidden_ref[...], hidden_ref[...]
    scale = rms_scale(hidden)
    hat = hidden * scale
    dnorm_ref[...] = jnp.sum(d * hat, axis=0, keepdims=True)
    dhidden = dy_ref[...].astype(F32) + norm_back(d, norm_ref[...], scale, hat)
    dhidden_ref[...] = dhidden
    db_ref[...] = dhidden.astype(BF16)
    n = away_ref.shape[1]
    away_ref[...] = db_ref[:, pl.ds(pl.multiple_of((2 * head + 1 - x) * n, n), n)].astype(F32)
    dg_ref[...] = dot(db_ref[...], w_ref[...], NT)
    slots, heads = sum_ref.shape[:2]
    for h in range(heads):
        cols = pl.ds(h * HD, HD)
        gain = gain_ref[:, cols]
        total = jnp.zeros((1, HD), F32)
        for s in range(slots):
            rows = pl.ds(s * HD, HD)
            mixed, pre, dgated = mixed_ref[rows, cols], pre_ref[0, rows, cols], dg_ref[rows, cols]
            scale = rms_scale(mixed)
            hat = mixed * scale
            sig = sigmoid(pre)
            swish = pre * sig
            total += jnp.sum(dgated * hat * swish, axis=0, keepdims=True)
            dpre_ref[rows, cols] = (dgated * hat * gain * (sig * (1.0 + pre * (1.0 - sig)))).astype(BF16).astype(F32)
            dm = norm_back(dgated * swish, gain, scale, hat).astype(BF16)
            dm_ref[rows, cols] = dm
            back_ref[s, h, pl.ds(0, HD), :] = dot(dm, qe_ref[rows, cols], TN)
            back_ref[s, h, pl.ds(HD, 8), :] = sum_ref[s, h, pl.ds(HD, 8), :]
        dgain_ref[:, cols] = total


def intra_back_kernel(dm_ref, qe_ref, ke_ref, proj_ref, c_ref, state_ref, dq_ref, dk_ref, dv_ref, dl_ref):
    slots, heads = state_ref.shape[:2]
    lower = triangle("lower")
    upper = triangle("upper").astype(BF16)
    for s in range(slots):
        rows = pl.ds(s * HD, HD)
        for h in range(heads):
            cols = pl.ds(h * HD, HD)
            dm, qe, ke, cum = (r[rows, cols] for r in (dm_ref, qe_ref, ke_ref, c_ref))
            vb = proj_ref[2, rows, cols].astype(BF16)
            dscores = jnp.where(lower, dot(dm, vb, NT), 0.0).astype(BF16)
            to_q = dot(dscores, ke) + dot(dm, state_ref[s, h].astype(BF16))
            to_k = dot(dscores, qe, TN)
            pre = proj_ref[0, rows, cols]
            sig = sigmoid(pre)
            dq_ref[rows, cols] = (jnp.exp(cum) * to_q * (sig * (1.0 + pre * (1.0 - sig)))).astype(BF16).astype(F32)
            dk_ref[rows, cols] = jnp.exp(-cum) * to_k
            scores = jnp.where(lower, dot(qe, ke, NT), 0.0).astype(BF16)
            dv_ref[rows, cols] = dot(scores, dm, TN)
            dl_ref[rows, cols] = exact_dot(upper, qe.astype(F32) * to_q - ke.astype(F32) * to_k)


def state_back_kernel(pos, lengths, carried_ref, state_ref, ke_ref, forget_ref, value_ref, c_ref, bound_ref, dk_ref, dv_ref, dl_ref, dfv_ref, dbound_ref):
    slots, heads = state_ref.shape[:2]
    strict = triangle("strict").astype(BF16)
    for h in range(heads):
        cols = pl.ds(h * HD, HD)
        bound = bound_ref[:, cols]
        total = jnp.zeros((1, HD), F32)
        for s in range(slots):
            rows = pl.ds(s * HD, HD)
            ok = valid_rows(pos[0], lengths[s])
            cum, ke = c_ref[rows, cols], ke_ref[rows, cols]
            ending = carried_ref[s, h] * jnp.exp(cum[HD - 1 :, :])
            ending_low = ending.astype(BF16)
            to_k = dot(value_ref[0, rows, cols].astype(BF16), ending_low)
            dfv_ref[1, rows, cols] = (dv_ref[rows, cols] + dot(ke, ending_low, NT)).astype(BF16).astype(F32)
            through = jnp.sum(ending * state_ref[s, h], axis=0, keepdims=True)
            dlogf = dl_ref[rows, cols] + exact_dot(strict, ke.astype(F32) * to_k) + through
            dkeys = dk_ref[rows, cols] + jnp.exp(-cum) * to_k
            sig, forget = open_forget(forget_ref[0, rows, cols], bound, ok)
            dforget = jnp.where(ok, dlogf / forget - dkeys, 0.0)
            total += jnp.sum(dforget * (1.0 - sig), axis=0, keepdims=True)
            dfv_ref[0, rows, cols] = (dforget * (1.0 - bound) * sig * (1.0 - sig)).astype(BF16).astype(F32)
        dbound_ref[:, cols] = total


SMEM = pl.BlockSpec(memory_space=pltpu.SMEM)


def whole(shape, *index):
    index = index or (0,) * len(shape)
    return pl.BlockSpec(shape, lambda *_: index)


def sds(shape, dtype=F32):
    return jax.ShapeDtypeStruct(shape, dtype)


def call(kernel, name, outs, in_specs, out_specs, flops, moved, grid=(1,), scratch=(), vmem=48, aliases=None):
    return pl.pallas_call(
        kernel,
        name=name,
        grid=grid,
        out_shape=outs,
        in_specs=in_specs,
        out_specs=out_specs,
        scratch_shapes=list(scratch),
        input_output_aliases=aliases or {},
        compiler_params=pltpu.CompilerParams(vmem_limit_bytes=vmem * MIB),
        cost_estimate=pl.CostEstimate(flops=int(flops), bytes_accessed=int(moved), transcendentals=0),
    )


def entering_all(packed, backward):
    count, mine = lax.axis_size("seq"), lax.axis_index("seq")
    pieces = lax.all_gather(packed, "seq")
    if backward:
        pieces, mine = pieces[::-1], count - 1 - mine

    def step(position, state):
        piece = pieces[position]
        longer = piece[:, :, HD : HD + 1] * state + piece[:, :, :HD]
        return jnp.where(position < mine, longer, state)

    return lax.fori_loop(0, count - 1, step, jnp.zeros_like(packed[:, :, :HD]))


def decay(a):
    return a[:, HD : HD + 1]


def state(a):
    return a[:, :HD]


def join(a, b):
    both = decay(b) * state(a) + state(b)
    return jnp.concatenate([both, jnp.broadcast_to(decay(a) * decay(b), (a.shape[0], 8, HD))], axis=1)


def is_first(backward):
    is_low = lax.axis_index("seq") % 2 == 0
    return is_low, (~is_low if backward else is_low)


def pair_states(packed, backward):
    packed = packed.reshape(-1, PACKED, HD)
    half = packed.shape[0] // 2
    is_low, first = is_first(backward)
    mine = jnp.where(is_low, packed[:half], packed[half:])
    other = lax.ppermute(jnp.where(is_low, packed[half:], packed[:half]), "seq", X_SWAP)
    return jnp.where(first, mine, other), jnp.where(first, other, mine)


def pass_states(pair, backward):
    step = -1 if backward else 1
    before = lax.ppermute(pair, "seq", z_line(step))
    further = lax.ppermute(join(before, pair), "seq", z_line(2 * step))
    return decay(before) * state(further) + state(before)


def enter_states(early, into_first, shape, backward):
    is_low, first = is_first(backward)
    into_second = decay(early) * into_first + state(early)
    kept = jnp.where(first, into_first, into_second)
    given = lax.ppermute(jnp.where(first, into_second, into_first), "seq", X_SWAP)
    low, high = jnp.where(is_low, kept, given), jnp.where(is_low, given, kept)
    return jnp.concatenate([low, high]).reshape(shape)


def tie(*values):
    return lax.optimization_barrier(values)


def core_swap(a):
    return lax.ppermute(a, "head", CORE_SWAP)


def y_swap(a):
    return lax.ppermute(a, "head", Y_SWAP)


def x_swap(a):
    return lax.ppermute(a, "seq", X_SWAP)


def assemble(blocks, into=None, first=0):
    head = lax.axis_index("head")
    tokens, n = blocks[0][0].shape
    width = 4 * n
    here = jnp.stack([a for block in blocks for a in block]).reshape(len(blocks), 2, tokens, n)
    there = core_swap(here)
    at = jnp.stack([(head ^ k) * n for k in range(4)]).astype(jnp.int32)
    piece = pl.BlockSpec((1, 2, tokens, n), lambda i: (i, 0, 0, 0))
    out_spec = pl.BlockSpec((tokens, width), lambda i: (i + first, 0))
    grid = (len(blocks),)
    moved = 6 * len(blocks) * tokens * width
    if into is None:
        return call(assemble_kernel, "assemble", sds((len(blocks) * tokens, width), BF16), [SMEM, piece, piece], out_spec, 0, moved, grid=grid)(at, here, there)
    kept = pl.BlockSpec(memory_space=pl.ANY)
    return call(assemble_kernel, "assemble", sds(into.shape, BF16), [SMEM, piece, piece, kept], out_spec, 0, moved, grid=grid, aliases={3: 0})(at, here, there, into)


def join_heads(parts, into, first):
    heads, rows, n = parts.shape
    tokens = into.shape[0] // 4
    return call(
        join_kernel,
        "join",
        sds(into.shape, BF16),
        [pl.BlockSpec((heads, tokens, n), lambda i: (0, i, 0)), pl.BlockSpec(memory_space=pl.ANY)],
        pl.BlockSpec((tokens, heads * n), lambda i: (i + first, 0)),
        0,
        6 * rows * heads * n,
        grid=(rows // tokens,),
        aliases={1: 0},
    )(parts, into)


class Calls:
    def __init__(self, slots, length, width, local, units):
        self.slots, self.count, self.width, self.local, self.units = slots, slots * length, width, local, units
        self.heads = local // HD
        self.pair = 2 * HD
        self.steps = units // self.pair
        self.rest = units - self.steps * self.pair
        self.tall, self.channel = whole((self.count, width)), whole((self.count, local))
        self.row, self.w_spec = whole((1, local)), whole((local, width))
        self.half, self.half_spec = sds((self.count, width // 2)), whole((self.count, width // 2))
        self.state_shape = (slots, self.heads, HD, HD)
        self.packed_shape = (slots, self.heads, PACKED, HD)
        self.state_spec, self.packed_spec = whole(self.state_shape), whole(self.packed_shape)
        self.wide, self.norm_row = sds((self.count, width)), whole((1, width))
        self.low = sds((self.count, local), BF16)
        self.full = sds((self.count, local))

    def proj(self, *index):
        return whole((1, self.count, self.local), *index)

    def project(self, pos, lengths, tokens, norm, weight, bound):
        count, width, local, pair = self.count, self.width, self.local, self.pair
        block = pl.BlockSpec((count, pair), lambda i: (0, i))
        return call(
            project_kernel,
            "project",
            [sds((count, width), BF16), self.half, sds((4, count, local)), self.full, self.low, self.low, self.full, sds(self.packed_shape)],
            [SMEM, SMEM, self.tall, whole((1, width)), pl.BlockSpec((4, width, pair), lambda i: (0, 0, i)), pl.BlockSpec((1, pair), lambda i: (0, i))],
            [self.tall, self.half_spec, pl.BlockSpec((4, count, pair), lambda i: (0, 0, i))] + [block] * 4 + [pl.BlockSpec((self.slots, 2, PACKED, HD), lambda i: (0, i, 0, 0))],
            8 * count * width * local,
            20e6,
            grid=(local // pair,),
        )(pos, lengths, tokens, norm, weight, bound)

    def mixer_out(self, core, qe, states, intra, proj, gain, weight):
        return call(
            mixer_out_kernel,
            "mixer_out",
            [self.full, self.low, self.full, self.half, self.half],
            [SMEM, self.channel, self.state_spec, self.channel, self.proj(3, 0, 0), self.row, self.w_spec],
            [self.channel] * 3 + [self.half_spec] * 2,
            2 * self.count * self.width * self.local,
            10e6,
        )(core, qe, states, intra, proj, gain, weight)

    def ffn_specs(self, first=0, tail=True):
        width, pair, rest = self.width, self.pair, self.rest
        last = self.steps * pair // rest
        specs = [
            pl.BlockSpec((2, width, pair), lambda i: (0, 0, i + first)),
            pl.BlockSpec((pair, width), lambda i: (i + first, 0)),
            whole((2, width, rest), 0, 0, last),
            whole((rest, width), last, 0),
        ]
        return specs if tail else specs[:2]

    def ffn_own(self, core, xn2, dy, ffn_in, ffn_out):
        return call(
            ffn_own_kernel,
            "ffn_own",
            [self.wide, self.half, self.half],
            [SMEM, self.tall, self.tall, *self.ffn_specs()],
            [self.tall, self.half_spec, self.half_spec],
            12 * self.count * self.width * self.units,
            30e6,
            grid=(self.steps,),
            scratch=[pltpu.VMEM((self.count, self.width), F32)],
            vmem=60,
        )(core, xn2, dy, ffn_in, ffn_out, ffn_in, ffn_out)

    def norm_back(self, place, parts, hidden, dy, norm, weight, mixed, proj, gain, qe, packed):
        n = self.width // 8
        return call(
            norm_back_kernel,
            "norm_back",
            [self.full, self.low, sds((1, self.local)), sds(self.packed_shape), self.wide, sds((self.count, self.width), BF16), sds((self.count, n)), sds((1, self.width))],
            [SMEM] + [self.half_spec] * 4 + [self.tall, self.tall, self.norm_row, self.w_spec, self.channel, self.proj(3, 0, 0), self.row, self.channel, self.packed_spec],
            [self.channel, self.channel, self.row, self.packed_spec, self.tall, self.tall, whole((self.count, n)), self.norm_row],
            2 * self.count * self.width * self.local,
            10e6,
            scratch=[pltpu.VMEM((self.count, self.local), F32)],
        )(place, *parts, hidden, dy, norm, weight, mixed, proj, gain, qe, packed)

    def second_norm(self, place, tokens, parts, gain, lines):
        quarter = self.width // 4
        return call(
            second_norm_kernel,
            "second_norm",
            [self.wide, sds((lines * self.count, self.width), BF16), sds((self.count, quarter))],
            [SMEM, self.tall] + [self.half_spec] * 4 + [self.norm_row],
            [self.tall, self.tall, whole((self.count, quarter))],
            0,
            10e6,
        )(place, tokens, *parts, gain)

    def first_grad(self, dproj, weight):
        quarter = self.width // 4
        return call(
            first_grad_kernel,
            "first_grad",
            self.wide,
            [self.channel] * 4 + [pl.BlockSpec((4, quarter, self.local), lambda i: (0, i, 0))],
            pl.BlockSpec((self.count, quarter), lambda i: (0, i)),
            8 * self.count * self.width * self.local,
            15e6,
            grid=(4,),
        )(*dproj, weight)

    def first_back(self, dxn1, dhidden, tokens, gain):
        return call(
            first_back_kernel,
            "first_back",
            [sds((self.count, self.width), BF16), sds((1, self.width))],
            [self.tall, self.tall, self.tall, self.norm_row],
            [self.tall, self.norm_row],
            0,
            10e6,
        )(dxn1, dhidden, tokens, gain)

    def intra_back(self, dmixed, qe, ke, proj, cum, states):
        return call(
            intra_back_kernel,
            "intra_back",
            [self.full] * 4,
            [self.channel, self.channel, self.channel, whole((3, self.count, self.local)), self.channel, self.state_spec],
            [self.channel] * 4,
            14 * self.count * self.local * HD,
            10e6,
        )(dmixed, qe, ke, proj, cum, states)

    def state_back(self, pos, lengths, carried, states, ke, proj, cum, bound, dkeys, dvalues, dlogf):
        return call(
            state_back_kernel,
            "state_back",
            [sds((2, self.count, self.local)), sds((1, self.local))],
            [SMEM, SMEM, self.state_spec, self.state_spec, self.channel, self.proj(1, 0, 0), self.proj(2, 0, 0), self.channel, self.row] + [self.channel] * 3,
            [whole((2, self.count, self.local)), self.row],
            8 * self.count * self.local * HD,
            10e6,
        )(pos, lengths, carried, states, ke, proj, proj, cum, bound, dkeys, dvalues, dlogf)

    def widen(self, head, dy, lines):
        quarter = self.width // 4
        return call(
            widen_kernel,
            "widen",
            [sds((self.count, quarter)), sds((lines * self.count, self.width), BF16)],
            [SMEM, self.tall],
            [whole((self.count, quarter)), self.tall],
            0,
            4e6,
        )(head, dy)

    def turn(self, place, xn, got):
        shape = (4, self.width // 8, 2 * self.count)
        return call(turn_kernel, "turn", sds(shape, BF16), [SMEM, self.tall, self.half_spec], whole(shape), 0, 6e6)(place, xn, got)

    def mix_grad(self, turned, *grads):
        shape = (len(grads) // 2, 2, self.width // 8, self.local)
        return call(
            mix_grad_kernel,
            "mix_grad",
            [sds(shape)] * 2,
            [whole(turned.shape)] + [self.channel] * len(grads),
            [whole(shape)] * 2,
            len(grads) * self.count * self.width * self.local,
            10e6,
        )(turned, *grads)

    def ffn_grad(self, rows, xn, dy, ffn_in, ffn_out, first, steps):
        n, pair = self.width // 8, self.pair
        tail = first + steps == self.steps and self.rest > 0
        units = steps * pair + self.rest * tail
        out = sds((3, n, units))
        line = whole(xn.shape)
        return call(
            functools.partial(ffn_grad_kernel, tail),
            "ffn_grad",
            [out, out],
            [SMEM, line, line] + self.ffn_specs(first, tail),
            [whole(out.shape)] * 2,
            6 * xn.shape[0] * (self.width + 2 * n) * units,
            20e6,
            grid=(steps,),
            scratch=[pltpu.VMEM((2 * n, xn.shape[0]), BF16)] * 2 + [pltpu.VMEM((xn.shape[0], pair), BF16)] * 3,
            vmem=62,
        )(rows, xn, dy, *([ffn_in, ffn_out] * (2 if tail else 1)))


def scalar(v):
    return jnp.asarray(v, jnp.int32).reshape(1)


def body(tokens, lengths, norm_first, mix_weight, lower_bound, out_gain, w_out, norm_second, ffn_in, ffn_out, cotangent):
    shape = tokens.shape
    slots, length, width = shape
    local = lower_bound.shape[0]
    do = Calls(slots, length, width, local, ffn_out.shape[0])
    fast = lax.axis_size("seq") == 8 and lax.axis_size("head") == 4
    run = run_lines if fast else run_any
    output, grad_tokens, small, weights = run(
        do,
        tokens.reshape(do.count, width),
        lengths,
        norm_first.reshape(1, width),
        mix_weight,
        lower_bound.reshape(1, local),
        out_gain.reshape(1, local),
        w_out,
        norm_second.reshape(1, width),
        ffn_in,
        ffn_out,
        cotangent.reshape(do.count, width),
    )
    first, second = small[:width], small[width : 2 * width]
    bound_sum, gain_sum = small[2 * width : 2 * width + local], small[2 * width + local :]
    return (output.reshape(shape), grad_tokens.reshape(shape), first, weights[0], bound_sum, gain_sum, weights[1], second, weights[2], weights[3])


def run_any(do, tokens, lengths, norm_first, mix_weight, bound, gain, w_out, norm_second, ffn_in, ffn_out, dy):
    def total(halves):
        low, high = jnp.split(lax.psum(jnp.concatenate(halves, axis=1), "head"), 2, axis=1)
        return low, jnp.zeros_like(low), high, jnp.zeros_like(high)

    pos, core = scalar(lax.axis_index("seq")), scalar(0)
    nowhere = jnp.zeros((3,), jnp.int32)
    xn1, _, proj, cum, qe, ke, intra, packed = do.project(pos, lengths, tokens, norm_first, mix_weight, bound)
    states = entering_all(packed, False)
    mixed, gated, _, *halves = do.mixer_out(core, qe, states, intra, proj, gain, w_out)
    hidden, xn2, _ = do.second_norm(nowhere, tokens, total(halves), norm_second, 1)
    ffn, dkeep, dsend = do.ffn_own(core, xn2, dy, ffn_in, ffn_out)
    output = (hidden + lax.psum(ffn, "head")).astype(BF16)
    dpre_gate, dmixed, part_gain, back, dhidden, dbranch, _, part_norm_second = do.norm_back(
        nowhere, total((dkeep, dsend)), hidden, dy, norm_second, w_out, mixed, proj, gain, qe, packed
    )
    carried = entering_all(back, True)
    dpre_query, dkeys, dvalues, dlogf = do.intra_back(dmixed, qe, ke, proj, cum, states)
    dpre_fv, part_bound = do.state_back(pos, lengths, carried, states, ke, proj, cum, bound, dkeys, dvalues, dlogf)
    dproj = (dpre_query, dpre_fv[0], dpre_fv[1], dpre_gate)
    grad_tokens, part_norm_first = do.first_back(lax.psum(do.first_grad(dproj, mix_weight), "head"), dhidden, tokens, norm_first)
    weights = weight_grads_whole(xn1, dproj, gated, dbranch, xn2, dy, ffn_in, ffn_out)
    small = lax.psum(jnp.concatenate([part_norm_first[0], part_norm_second[0], part_bound[0], part_gain[0]]), "seq")
    return output, grad_tokens, small, weights


def run_lines(do, tokens, lengths, norm_first, mix_weight, bound, gain, w_out, norm_second, ffn_in, ffn_out, dy):
    width, local, quarter = do.width, do.local, do.width // 4
    seq, head = lax.axis_index("seq"), lax.axis_index("head")
    x, z = seq % 2, seq // 2
    seq_at, core = scalar(seq), scalar(head % 2)
    place = jnp.stack([head % 2, head, x]).astype(jnp.int32)

    def shift(a, k):
        return lax.ppermute(a, "seq", z_shift(k))

    def sum_cores(keep, send):
        return keep + core_swap(send)

    def sum_near(keep, send):
        got = lax.ppermute(send, "seq", flip(2))
        return (keep[:, 0], got[:, 0]), keep[:, 1] + got[:, 1]

    def sum_far(near):
        return lax.ppermute(near[1], "seq", flip(4))

    def summed(near, far):
        return near[0][0] + near[0][1] + far

    dy_quarter, dy_all = do.widen(scalar(head), dy, 4)
    dy1 = shift(dy_quarter, 1)
    xn1, xn1_away, proj, cum, qe, ke, intra, packed = do.project(seq_at, lengths, tokens, norm_first, mix_weight, bound)
    early, late = pair_states(packed, False)
    early, late, dy1 = tie(early, late, dy1)

    into = pass_states(join(early, late), False)
    dy1_over = y_swap(dy1)
    early, into, dy1_over, dy_quarter = tie(early, into, dy1_over, dy_quarter)

    states = enter_states(early, into, do.state_shape, False)
    mixed, gated, gated_wide, keep, send = do.mixer_out(core, qe, states, intra, proj, gain, w_out)
    half = sum_cores(keep, send)
    half, dy_quarter, xn1_away, dy1, dy1_over = tie(half, dy_quarter, xn1_away, dy1, dy1_over)

    over = y_swap(half)
    half_other = core_swap(half)
    dy2 = shift(dy_quarter, 2)
    xn1_got = x_swap(xn1_away)
    dy_all = assemble([(dy1, dy1_over)], dy_all, 1)
    half, half_other, over, dy2, gated_wide, xn1_got, dy_all = tie(half, half_other, over, dy2, gated_wide, xn1_got, dy_all)

    dy2_over = y_swap(dy2)
    hidden, xn_all, xn_quarter = do.second_norm(place, tokens, (half, over, half_other, core_swap(over)), norm_second, 4)
    xnl1 = shift(xn_quarter, 1)
    gated_got = x_swap(gated_wide)
    ffn, dkeep, dsend = do.ffn_own(core, xn_all, dy, ffn_in, ffn_out)
    dkeep, dsend, xn_quarter, dy2_over, xnl1, gated_got, ffn = tie(dkeep, dsend, xn_quarter, dy2_over, xnl1, gated_got, ffn)

    dhalf = sum_cores(dkeep, dsend)
    dhalf, xn_quarter, dy_all, xn1_got = tie(dhalf, xn_quarter, dy_all, xn1_got)
    dover = y_swap(dhalf)
    dhalf_other = core_swap(dhalf)
    xnl2 = shift(xn_quarter, 2)
    dy_all = assemble([(dy2, dy2_over)], dy_all, 2)
    xn1_turned = do.turn(seq_at, xn1, xn1_got)
    dhalf, dover, dhalf_other, xnl2, xn_quarter, xnl1, dy_all, xn1_turned, ffn = tie(dhalf, dover, dhalf_other, xnl2, xn_quarter, xnl1, dy_all, xn1_turned, ffn)
    ffn = lax.psum(ffn, "head")

    xnl3 = shift(xn_quarter, 3)
    dpre_gate, dmixed, part_gain, back, dhidden, dbranch, dbranch_away, part_norm_second = do.norm_back(
        place, (dhalf, dover, dhalf_other, core_swap(dover)), hidden, dy, norm_second, w_out, mixed, proj, gain, qe, packed
    )
    back, dpre_gate, dmixed, dbranch, dbranch_away, dy_quarter = tie(back, dpre_gate, dmixed, dbranch, dbranch_away, dy_quarter)

    early, late = pair_states(back, True)
    dy3 = shift(dy_quarter, 3)
    early, late, dpre_gate, dmixed, dbranch_away, xnl3, dy3 = tie(early, late, dpre_gate, dmixed, dbranch_away, xnl3, dy3)
    xn_parts = lax.all_gather(jnp.concatenate([xnl1, xnl2, xnl3]), "head")
    into = pass_states(join(early, late), True)
    dbranch_own = x_swap(dbranch_away)
    dpre_query, dkeys, dvalues, dlogf = do.intra_back(dmixed, qe, ke, proj, cum, states)
    gate_got = x_swap(dpre_gate)
    dy3_over = y_swap(dy3)
    early, into, gate_got, dpre_query, dbranch_own, dy3_over = tie(early, into, gate_got, dpre_query, dbranch_own, dy3_over)

    gate = do.mix_grad(xn1_turned, dpre_gate, gate_got)
    early, into, gate, dbranch_own, dy3_over, ffn = tie(early, into, gate, dbranch_own, dy3_over, ffn)

    near_gate = sum_near(*gate)
    dbranch_over = y_swap(dbranch_own)
    carried = enter_states(early, into, do.state_shape, True)
    dy_all = assemble([(dy3, dy3_over)], dy_all, 3)
    dpre_fv, part_bound = do.state_back(seq_at, lengths, carried, states, ke, proj, cum, bound, dkeys, dvalues, dlogf)
    dpre_fv, dpre_query, dbranch_over, dy_all = tie(dpre_fv, dpre_query, dbranch_over, dy_all)

    fv_got = x_swap(dpre_fv)
    down = do.mix_grad(do.turn(seq_at, dbranch, assemble([(dbranch_own, dbranch_over)])), gated, gated_got)
    near_down = sum_near(*down)
    near_gate, down = tie(near_gate, down)
    gate_far = sum_far(near_gate)
    dxn1 = do.first_grad((dpre_query, dpre_fv[0], dpre_fv[1], dpre_gate), mix_weight)
    xn_parts, dxn1, ffn = tie(xn_parts, dxn1, ffn)
    fv_got, gate_far, near_down, xn_all, dpre_query, xn_parts = tie(fv_got, gate_far, near_down, xn_all, dpre_query, xn_parts)
    dxn1 = lax.psum(dxn1, "head")

    rows = jnp.stack([seq, seq ^ 1]).astype(jnp.int32)
    query_got = x_swap(dpre_query)
    w_far = sum_far(near_down)
    forget_values = do.mix_grad(xn1_turned, dpre_fv[0], fv_got[0], dpre_fv[1], fv_got[1])
    forget_values, xn_all, xn_parts = tie(forget_values, xn_all, xn_parts)
    near_fv = sum_near(*forget_values)
    xn_all = join_heads(xn_parts, xn_all, 1)
    mine_a, away_a = do.ffn_grad(rows, xn_all, dy_all, ffn_in, ffn_out, 0, 2)
    away_a, xn_all, query_got = tie(away_a, xn_all, query_got)
    got_a = x_swap(away_a)
    query = do.mix_grad(xn1_turned, dpre_query, query_got)
    mine_b, away_b = do.ffn_grad(rows, xn_all, dy_all, ffn_in, ffn_out, 2, 2)
    near_fv, w_far, got_a, query, away_b, xn_all, dhidden, hidden = tie(near_fv, w_far, got_a, query, away_b, xn_all, dhidden, hidden)

    got_b = x_swap(away_b)
    near_query, fv_far = sum_near(*query), sum_far(near_fv)
    grad_tokens, part_norm_first = do.first_back(dxn1, dhidden, tokens, norm_first)
    mine_c, away_c = do.ffn_grad(rows, xn_all, dy_all, ffn_in, ffn_out, 4, do.steps - 4)
    small = jnp.concatenate([part_norm_first[0], part_norm_second[0], part_bound[0], part_gain[0]])
    small = small + lax.ppermute(small, "seq", flip(1))
    output = (hidden + ffn).astype(BF16)
    got_b, near_query, fv_far, small, away_c, output = tie(got_b, near_query, fv_far, small, away_c, output)

    got_c = x_swap(away_c)
    query_far = sum_far(near_query)
    for bit in (2, 4):
        small = small + lax.ppermute(small, "seq", flip(bit))
    parts = ((mine_a, got_a), (mine_b, got_b), (mine_c, got_c))
    grad_in = jnp.concatenate([mine[:2] + got[:2] for mine, got in parts], axis=2)
    grad_out = jnp.concatenate([(mine[2] + got[2]).T for mine, got in parts], axis=0)
    grad_mix = jnp.concatenate([summed(near_query, query_far), summed(near_fv, fv_far), summed(near_gate, gate_far)])
    grad_w_out = summed(near_down, w_far)
    return output, grad_tokens, small, (grad_mix, grad_w_out[0].T, grad_in, grad_out)


def weight_grads_whole(xn1, dproj, gated, dbranch, xn2, dy, ffn_in, ffn_out):
    gate, up = dot(xn2, ffn_in[0]), dot(xn2, ffn_in[1])
    dact = dot(dy, ffn_out, NT)
    sig = sigmoid(gate)
    swish = gate * sig
    act = (swish * up).astype(BF16)
    dgate = (dact * up * (sig * (1.0 + gate * (1.0 - sig)))).astype(BF16)
    dup = (dact * swish).astype(BF16)

    def scatter(a, axis):
        return lax.psum_scatter(a, "seq", scatter_dimension=axis, tiled=True)

    return (
        jnp.stack([scatter(dot(xn1, d.astype(BF16), TN), 0) for d in dproj]),
        scatter(dot(gated, dbranch, TN), 1),
        jnp.stack([scatter(dot(xn2, d, TN), 0) for d in (dgate, dup)]),
        scatter(dot(act, dy, TN), 1),
    )


def solution(mesh):
    in_specs = (
        P(None, "seq", None),
        P(),
        P(),
        P(None, None, "head"),
        P("head"),
        P("head"),
        P("head", None),
        P(),
        P(None, None, "head"),
        P("head", None),
        P(None, "seq", None),
    )
    out_specs = (
        P(None, "seq", None),
        P(None, "seq", None),
        P(),
        P(None, "seq", "head"),
        P("head"),
        P("head"),
        P("head", "seq"),
        P(),
        P(None, "seq", "head"),
        P("head", "seq"),
    )
    return jax.shard_map(body, mesh=mesh, in_specs=in_specs, out_specs=out_specs, check_vma=False)
```

```python
import functools

import jax
import jax.numpy as jnp
from jax import lax
from jax.experimental import pallas as pl
from jax.experimental.pallas import tpu as pltpu
from jax.sharding import PartitionSpec as P

HD = 128
EPS = 1e-06
F32 = jnp.float32
BF16 = jnp.bfloat16
MIB = 1 << 20
PACKED = HD + 8

X_SWAP = [(p, p ^ 1) for p in range(8)]
CORE_SWAP = [(h, h ^ 1) for h in range(4)]
Y_SWAP = [(h, h ^ 2) for h in range(4)]


def z_shift(k):
    return [(p, (p + 2 * k) % 8) for p in range(8)]


def z_line(k):
    return [(p, p + 2 * k) for p in range(8) if 0 <= p + 2 * k < 8]


def flip(bit):
    return [(p, p ^ bit) for p in range(8)]


def rms_scale(v):
    return lax.rsqrt(jnp.mean(v * v, axis=-1, keepdims=True) + EPS)


def norm_back(grad_normed, gain, scale, normed_hat):
    scaled = grad_normed * gain
    return scale * (scaled - normed_hat * jnp.mean(scaled * normed_hat, axis=-1, keepdims=True))


def dot(a, b, dims=((1,), (0,))):
    return lax.dot_general(a, b, (dims, ((), ())), preferred_element_type=F32)


NT = ((1,), (1,))
TN = ((0,), (0,))


def sigmoid(v):
    return 1.0 / (1.0 + jnp.exp(-v))


def triangle(kind):
    row = lax.broadcasted_iota(jnp.int32, (HD, HD), 0)
    col = lax.broadcasted_iota(jnp.int32, (HD, HD), 1)
    return {"lower": row >= col, "strict": row > col, "upper": row <= col}[kind]


def exact_dot(ones, v, parts=3):
    total = None
    for _ in range(parts):
        part = v.astype(BF16)
        v = v - part.astype(F32)
        term = dot(ones, part)
        total = term if total is None else total + term
    return total


def valid_rows(pos, length):
    row = lax.broadcasted_iota(jnp.int32, (HD, 1), 0)
    return (pos * HD + row) < length


def open_forget(pre, bound, ok):
    sig = sigmoid(pre)
    return sig, jnp.where(ok, bound + (1.0 - bound) * sig, 1.0)


def project_kernel(pos, lengths, x_ref, gain_ref, w_ref, bound_ref, xn_ref, away_ref, proj_ref, c_ref, qe_ref, ke_ref, intra_ref, sum_ref):
    @pl.when(pl.program_id(0) == 0)
    def _():
        x = x_ref[...].astype(F32)
        xn_ref[...] = (x * rms_scale(x) * gain_ref[...]).astype(BF16)
        n = away_ref.shape[1] // 4
        for z in range(4):
            at = pl.multiple_of((2 * z + 1 - pos[0] % 2) * n, n)
            away_ref[:, pl.ds(z * n, n)] = xn_ref[:, pl.ds(at, n)].astype(F32)

    xn = xn_ref[...]
    for c in range(4):
        proj_ref[c] = dot(xn, w_ref[c])
    slots, heads = sum_ref.shape[:2]
    lower = triangle("lower")
    ones = lower.astype(BF16)
    for s in range(slots):
        rows = pl.ds(s * HD, HD)
        ok = valid_rows(pos[0], lengths[s])
        _, forget = open_forget(proj_ref[1, rows, :], bound_ref[...], ok)
        c_ref[rows, :] = exact_dot(ones, jnp.log(forget), 2)
        for h in range(heads):
            cols = pl.ds(h * HD, HD)
            pre_q, v, cum = proj_ref[0, rows, cols], proj_ref[2, rows, cols], c_ref[rows, cols]
            keys = 1.0 - forget[:, h * HD : (h + 1) * HD]
            qe = (pre_q * sigmoid(pre_q) * jnp.exp(cum)).astype(BF16)
            ke = (keys * jnp.exp(-cum)).astype(BF16)
            qe_ref[rows, cols] = qe
            ke_ref[rows, cols] = ke
            vb = v.astype(BF16)
            scores = jnp.where(lower, dot(qe, ke, NT), 0.0).astype(BF16)
            intra_ref[rows, cols] = dot(scores, vb)
            last = cum[HD - 1 :, :]
            to_end = (keys * jnp.exp(last - cum)).astype(BF16)
            sum_ref[s, h, pl.ds(0, HD), :] = dot(vb, to_end, TN)
            sum_ref[s, h, pl.ds(HD, 8), :] = jnp.broadcast_to(jnp.exp(last), (8, HD))


def split_store(keep_ref, send_ref, core, make):
    half = keep_ref.shape[1]
    keep_ref[...] = make(pl.multiple_of(core * half, half), half)
    send_ref[...] = make(pl.multiple_of((1 - core) * half, half), half)


def mixer_out_kernel(core, qe_ref, state_ref, intra_ref, pre_ref, gain_ref, w_ref, mixed_ref, gated_ref, wide_ref, keep_ref, send_ref):
    slots, heads = state_ref.shape[:2]
    for s in range(slots):
        rows = pl.ds(s * HD, HD)
        for h in range(heads):
            cols = pl.ds(h * HD, HD)
            mixed = intra_ref[rows, cols] + dot(qe_ref[rows, cols], state_ref[s, h].astype(BF16), NT)
            mixed_ref[rows, cols] = mixed
            pre = pre_ref[0, rows, cols]
            gated = mixed * rms_scale(mixed) * gain_ref[:, cols] * (pre * sigmoid(pre))
            gated_ref[rows, cols] = gated.astype(BF16)
            wide_ref[rows, cols] = gated_ref[rows, cols].astype(F32)
    split_store(keep_ref, send_ref, core[0], lambda at, n: dot(gated_ref[...], w_ref[:, pl.ds(at, n)]))


def ffn_unit(xn, dy, w_gate, w_up, w_out):
    gate, up = dot(xn, w_gate), dot(xn, w_up)
    dact = dot(dy, w_out, NT)
    sig = sigmoid(gate)
    swish = gate * sig
    act = (swish * up).astype(BF16)
    dgate = (dact * up * (sig * (1.0 + gate * (1.0 - sig)))).astype(BF16)
    dup = (dact * swish).astype(BF16)
    return act, dgate, dup


def ffn_own_kernel(core, xn_ref, dy_ref, in_ref, out_ref, in_tail, out_tail, f_acc, d_keep, d_send, d_acc):
    step = pl.program_id(0)

    @pl.when(step == 0)
    def _():
        f_acc[...] = jnp.zeros_like(f_acc)
        d_acc[...] = jnp.zeros_like(d_acc)

    def add(w_in, w_out):
        act, dgate, dup = ffn_unit(xn_ref[...], dy_ref[...], w_in[0], w_in[1], w_out[...])
        f_acc[...] += dot(act, w_out[...])
        d_acc[...] += dot(dgate, w_in[0], NT) + dot(dup, w_in[1], NT)

    add(in_ref, out_ref)

    @pl.when(step == pl.num_programs(0) - 1)
    def _():
        add(in_tail, out_tail)
        split_store(d_keep, d_send, core[0], lambda at, n: d_acc[:, pl.ds(at, n)])


def widen_kernel(at, a_ref, out_ref, copy_ref):
    n = out_ref.shape[1]
    out_ref[...] = a_ref[:, pl.ds(pl.multiple_of(at[0] * n, n), n)].astype(F32)
    copy_ref[...] = a_ref[...]


def place_halves(out_ref, core, parts):
    n, terms = out_ref.shape[1] // 2, len(parts) // 2
    for k, which in ((0, core), (1, 1 - core)):
        mine = parts[k * terms : (k + 1) * terms]
        at = pl.ds(pl.multiple_of(which * n, n), n)
        out_ref[:, at] = mine[0][...] if terms == 1 else mine[0][...] + mine[1][...]


def second_norm_kernel(place, x_ref, p0, p1, p2, p3, gain_ref, hidden_ref, xn_ref, quarter_ref):
    core, head = place[0], place[1]
    place_halves(hidden_ref, core, (p0, p1, p2, p3))
    hidden = x_ref[...].astype(F32) + hidden_ref[...]
    hidden_ref[...] = hidden
    xn_ref[...] = (hidden * rms_scale(hidden) * gain_ref[...]).astype(BF16)
    n = quarter_ref.shape[1]
    quarter_ref[...] = xn_ref[:, pl.ds(pl.multiple_of(head * n, n), n)].astype(F32)


def first_back_kernel(d_ref, dhidden_ref, x_ref, gain_ref, grad_ref, part_ref):
    x, d = x_ref[...].astype(F32), d_ref[...]
    scale = rms_scale(x)
    hat = x * scale
    part_ref[...] = jnp.sum(d * hat, axis=0, keepdims=True)
    grad_ref[...] = (dhidden_ref[...] + norm_back(d, gain_ref[...], scale, hat)).astype(BF16)


def first_grad_kernel(d0, d1, d2, d3, w_ref, out_ref):
    out_ref[...] = sum(dot(d[...].astype(BF16), w_ref[c], NT) for c, d in enumerate((d0, d1, d2, d3)))


def assemble_kernel(at, here_ref, there_ref, *refs):
    out_ref = refs[-1]
    n = here_ref.shape[-1]
    for k, piece in enumerate((here_ref, there_ref)):
        for over in range(2):
            out_ref[:, pl.ds(pl.multiple_of(at[2 * over + k], n), n)] = piece[0, over].astype(BF16)


def join_kernel(parts_ref, _, out_ref):
    n = parts_ref.shape[2]
    for k in range(parts_ref.shape[0]):
        out_ref[:, pl.ds(k * n, n)] = parts_ref[k].astype(BF16)


def ffn_grad_kernel(tail, rows, xn_ref, dy_ref, *refs):
    weights, (mine_ref, away_ref, xt_ref, dyt_ref, act_ref, dgate_ref, dup_ref) = refs[:-7], refs[-7:]
    step = pl.program_id(0)
    n = mine_ref.shape[1]

    @pl.when(step == 0)
    def _():
        for which in range(2):
            at = pl.ds(pl.multiple_of(rows[which] * n, n), n)
            xt_ref[pl.ds(which * n, n), :] = xn_ref[:, at].T
            dyt_ref[pl.ds(which * n, n), :] = dy_ref[:, at].T

    def put(w_in, w_out, units):
        size = w_out.shape[0]
        block = xn_ref.shape[0] // 4
        for k in range(4):
            at = pl.ds(k * block, block)
            made = ffn_unit(xn_ref[at, :], dy_ref[at, :], w_in[0], w_in[1], w_out[...])
            act_ref[at, :size], dgate_ref[at, :size], dup_ref[at, :size] = made
        for k, (left, right) in enumerate(((xt_ref, dgate_ref), (xt_ref, dup_ref), (dyt_ref, act_ref))):
            both = dot(left[...], right[:, :size])
            mine_ref[k, :, units] = both[:n]
            away_ref[k, :, units] = both[n:]

    size = weights[1].shape[0]
    put(weights[0], weights[1], pl.ds(pl.multiple_of(step * size, size), size))
    if tail:

        @pl.when(step == pl.num_programs(0) - 1)
        def _():
            rest = weights[3].shape[0]
            put(weights[2], weights[3], pl.ds(mine_ref.shape[2] - rest, rest))


def turn_kernel(place, xn_ref, got_ref, out_ref):
    _, n, both = out_ref.shape
    z, x = place[0] // 2, place[0] % 2
    for k in range(4):
        high = z // 2 if k % 2 == 0 else 1 - z // 2
        row = 2 * high + (z % 2 if k < 2 else 1 - z % 2)
        a = xn_ref[:, pl.ds(pl.multiple_of((2 * row + x) * n, n), n)]
        b = got_ref[:, pl.ds(pl.multiple_of(row * n, n), n)].astype(BF16)
        out_ref[k, :, pl.ds(0, both // 2)] = a.T
        out_ref[k, :, pl.ds(both // 2, both // 2)] = b.T


def mix_grad_kernel(turned_ref, *refs):
    keep_ref, send_ref = refs[-2:]
    both = turned_ref.shape[2]
    for c in range(keep_ref.shape[0]):
        own, got = refs[2 * c][...].astype(BF16), refs[2 * c + 1][...].astype(BF16)
        for k in range(4):
            a = turned_ref[k]
            (keep_ref if k < 2 else send_ref)[c, k % 2] = dot(a[:, : both // 2], own) + dot(a[:, both // 2 :], got)


def norm_back_kernel(place, p0, p1, p2, p3, hidden_ref, dy_ref, norm_ref, w_ref, mixed_ref, pre_ref, gain_ref, qe_ref, sum_ref, dpre_ref, dm_ref, dgain_ref, back_ref, dhidden_ref, db_ref, away_ref, dnorm_ref, dg_ref):
    core, head, x = place[0], place[1], place[2]
    place_halves(dhidden_ref, core, (p0, p1, p2, p3))
    d, hidden = dhidden_ref[...], hidden_ref[...]
    scale = rms_scale(hidden)
    hat = hidden * scale
    dnorm_ref[...] = jnp.sum(d * hat, axis=0, keepdims=True)
    dhidden = dy_ref[...].astype(F32) + norm_back(d, norm_ref[...], scale, hat)
    dhidden_ref[...] = dhidden
    db_ref[...] = dhidden.astype(BF16)
    n = away_ref.shape[1]
    away_ref[...] = db_ref[:, pl.ds(pl.multiple_of((2 * head + 1 - x) * n, n), n)].astype(F32)
    dg_ref[...] = dot(db_ref[...], w_ref[...], NT)
    slots, heads = sum_ref.shape[:2]
    for h in range(heads):
        cols = pl.ds(h * HD, HD)
        gain = gain_ref[:, cols]
        total = jnp.zeros((1, HD), F32)
        for s in range(slots):
            rows = pl.ds(s * HD, HD)
            mixed, pre, dgated = mixed_ref[rows, cols], pre_ref[0, rows, cols], dg_ref[rows, cols]
            scale = rms_scale(mixed)
            hat = mixed * scale
            sig = sigmoid(pre)
            swish = pre * sig
            total += jnp.sum(dgated * hat * swish, axis=0, keepdims=True)
            dpre_ref[rows, cols] = (dgated * hat * gain * (sig * (1.0 + pre * (1.0 - sig)))).astype(BF16).astype(F32)
            dm = norm_back(dgated * swish, gain, scale, hat).astype(BF16)
            dm_ref[rows, cols] = dm
            back_ref[s, h, pl.ds(0, HD), :] = dot(dm, qe_ref[rows, cols], TN)
            back_ref[s, h, pl.ds(HD, 8), :] = sum_ref[s, h, pl.ds(HD, 8), :]
        dgain_ref[:, cols] = total


def intra_back_kernel(dm_ref, qe_ref, ke_ref, proj_ref, c_ref, state_ref, dq_ref, dk_ref, dv_ref, dl_ref):
    slots, heads = state_ref.shape[:2]
    lower = triangle("lower")
    upper = triangle("upper").astype(BF16)
    for s in range(slots):
        rows = pl.ds(s * HD, HD)
        for h in range(heads):
            cols = pl.ds(h * HD, HD)
            dm, qe, ke, cum = (r[rows, cols] for r in (dm_ref, qe_ref, ke_ref, c_ref))
            vb = proj_ref[2, rows, cols].astype(BF16)
            dscores = jnp.where(lower, dot(dm, vb, NT), 0.0).astype(BF16)
            to_q = dot(dscores, ke) + dot(dm, state_ref[s, h].astype(BF16))
            to_k = dot(dscores, qe, TN)
            pre = proj_ref[0, rows, cols]
            sig = sigmoid(pre)
            dq_ref[rows, cols] = (jnp.exp(cum) * to_q * (sig * (1.0 + pre * (1.0 - sig)))).astype(BF16).astype(F32)
            dk_ref[rows, cols] = jnp.exp(-cum) * to_k
            scores = jnp.where(lower, dot(qe, ke, NT), 0.0).astype(BF16)
            dv_ref[rows, cols] = dot(scores, dm, TN)
            dl_ref[rows, cols] = exact_dot(upper, qe.astype(F32) * to_q - ke.astype(F32) * to_k)


def state_back_kernel(pos, lengths, carried_ref, state_ref, ke_ref, forget_ref, value_ref, c_ref, bound_ref, dk_ref, dv_ref, dl_ref, dfv_ref, dbound_ref):
    slots, heads = state_ref.shape[:2]
    strict = triangle("strict").astype(BF16)
    for h in range(heads):
        cols = pl.ds(h * HD, HD)
        bound = bound_ref[:, cols]
        total = jnp.zeros((1, HD), F32)
        for s in range(slots):
            rows = pl.ds(s * HD, HD)
            ok = valid_rows(pos[0], lengths[s])
            cum, ke = c_ref[rows, cols], ke_ref[rows, cols]
            ending = carried_ref[s, h] * jnp.exp(cum[HD - 1 :, :])
            ending_low = ending.astype(BF16)
            to_k = dot(value_ref[0, rows, cols].astype(BF16), ending_low)
            dfv_ref[1, rows, cols] = (dv_ref[rows, cols] + dot(ke, ending_low, NT)).astype(BF16).astype(F32)
            through = jnp.sum(ending * state_ref[s, h], axis=0, keepdims=True)
            dlogf = dl_ref[rows, cols] + exact_dot(strict, ke.astype(F32) * to_k) + through
            dkeys = dk_ref[rows, cols] + jnp.exp(-cum) * to_k
            sig, forget = open_forget(forget_ref[0, rows, cols], bound, ok)
            dforget = jnp.where(ok, dlogf / forget - dkeys, 0.0)
            total += jnp.sum(dforget * (1.0 - sig), axis=0, keepdims=True)
            dfv_ref[0, rows, cols] = (dforget * (1.0 - bound) * sig * (1.0 - sig)).astype(BF16).astype(F32)
        dbound_ref[:, cols] = total


SMEM = pl.BlockSpec(memory_space=pltpu.SMEM)


def whole(shape, *index):
    index = index or (0,) * len(shape)
    return pl.BlockSpec(shape, lambda *_: index)


def sds(shape, dtype=F32):
    return jax.ShapeDtypeStruct(shape, dtype)


def call(kernel, name, outs, in_specs, out_specs, flops, moved, grid=(1,), scratch=(), vmem=48, aliases=None):
    return pl.pallas_call(
        kernel,
        name=name,
        grid=grid,
        out_shape=outs,
        in_specs=in_specs,
        out_specs=out_specs,
        scratch_shapes=list(scratch),
        input_output_aliases=aliases or {},
        compiler_params=pltpu.CompilerParams(vmem_limit_bytes=vmem * MIB),
        cost_estimate=pl.CostEstimate(flops=int(flops), bytes_accessed=int(moved), transcendentals=0),
    )


def entering_all(packed, backward):
    count, mine = lax.axis_size("seq"), lax.axis_index("seq")
    pieces = lax.all_gather(packed, "seq")
    if backward:
        pieces, mine = pieces[::-1], count - 1 - mine

    def step(position, state):
        piece = pieces[position]
        longer = piece[:, :, HD : HD + 1] * state + piece[:, :, :HD]
        return jnp.where(position < mine, longer, state)

    return lax.fori_loop(0, count - 1, step, jnp.zeros_like(packed[:, :, :HD]))


def decay(a):
    return a[:, HD : HD + 1]


def state(a):
    return a[:, :HD]


def join(a, b):
    both = decay(b) * state(a) + state(b)
    return jnp.concatenate([both, jnp.broadcast_to(decay(a) * decay(b), (a.shape[0], 8, HD))], axis=1)


def is_first(backward):
    is_low = lax.axis_index("seq") % 2 == 0
    return is_low, (~is_low if backward else is_low)


def pair_states(packed, backward):
    packed = packed.reshape(-1, PACKED, HD)
    half = packed.shape[0] // 2
    is_low, first = is_first(backward)
    mine = jnp.where(is_low, packed[:half], packed[half:])
    other = lax.ppermute(jnp.where(is_low, packed[half:], packed[:half]), "seq", X_SWAP)
    return jnp.where(first, mine, other), jnp.where(first, other, mine)


def pass_states(pair, backward):
    step = -1 if backward else 1
    before = lax.ppermute(pair, "seq", z_line(step))
    further = lax.ppermute(join(before, pair), "seq", z_line(2 * step))
    return decay(before) * state(further) + state(before)


def enter_states(early, into_first, shape, backward):
    is_low, first = is_first(backward)
    into_second = decay(early) * into_first + state(early)
    kept = jnp.where(first, into_first, into_second)
    given = lax.ppermute(jnp.where(first, into_second, into_first), "seq", X_SWAP)
    low, high = jnp.where(is_low, kept, given), jnp.where(is_low, given, kept)
    return jnp.concatenate([low, high]).reshape(shape)


def tie(*values):
    return lax.optimization_barrier(values)


def core_swap(a):
    return lax.ppermute(a, "head", CORE_SWAP)


def y_swap(a):
    return lax.ppermute(a, "head", Y_SWAP)


def x_swap(a):
    return lax.ppermute(a, "seq", X_SWAP)


def assemble(blocks, into=None, first=0):
    head = lax.axis_index("head")
    tokens, n = blocks[0][0].shape
    width = 4 * n
    here = jnp.stack([a for block in blocks for a in block]).reshape(len(blocks), 2, tokens, n)
    there = core_swap(here)
    at = jnp.stack([(head ^ k) * n for k in range(4)]).astype(jnp.int32)
    piece = pl.BlockSpec((1, 2, tokens, n), lambda i: (i, 0, 0, 0))
    out_spec = pl.BlockSpec((tokens, width), lambda i: (i + first, 0))
    grid = (len(blocks),)
    moved = 6 * len(blocks) * tokens * width
    if into is None:
        return call(assemble_kernel, "assemble", sds((len(blocks) * tokens, width), BF16), [SMEM, piece, piece], out_spec, 0, moved, grid=grid)(at, here, there)
    kept = pl.BlockSpec(memory_space=pl.ANY)
    return call(assemble_kernel, "assemble", sds(into.shape, BF16), [SMEM, piece, piece, kept], out_spec, 0, moved, grid=grid, aliases={3: 0})(at, here, there, into)


def join_heads(parts, into, first):
    heads, rows, n = parts.shape
    tokens = into.shape[0] // 4
    return call(
        join_kernel,
        "join",
        sds(into.shape, BF16),
        [pl.BlockSpec((heads, tokens, n), lambda i: (0, i, 0)), pl.BlockSpec(memory_space=pl.ANY)],
        pl.BlockSpec((tokens, heads * n), lambda i: (i + first, 0)),
        0,
        6 * rows * heads * n,
        grid=(rows // tokens,),
        aliases={1: 0},
    )(parts, into)


class Calls:
    def __init__(self, slots, length, width, local, units):
        self.slots, self.count, self.width, self.local, self.units = slots, slots * length, width, local, units
        self.heads = local // HD
        self.pair = 2 * HD
        self.steps = units // self.pair
        self.rest = units - self.steps * self.pair
        self.tall, self.channel = whole((self.count, width)), whole((self.count, local))
        self.row, self.w_spec = whole((1, local)), whole((local, width))
        self.half, self.half_spec = sds((self.count, width // 2)), whole((self.count, width // 2))
        self.state_shape = (slots, self.heads, HD, HD)
        self.packed_shape = (slots, self.heads, PACKED, HD)
        self.state_spec, self.packed_spec = whole(self.state_shape), whole(self.packed_shape)
        self.wide, self.norm_row = sds((self.count, width)), whole((1, width))
        self.low = sds((self.count, local), BF16)
        self.full = sds((self.count, local))

    def proj(self, *index):
        return whole((1, self.count, self.local), *index)

    def project(self, pos, lengths, tokens, norm, weight, bound):
        count, width, local, pair = self.count, self.width, self.local, self.pair
        block = pl.BlockSpec((count, pair), lambda i: (0, i))
        return call(
            project_kernel,
            "project",
            [sds((count, width), BF16), self.half, sds((4, count, local)), self.full, self.low, self.low, self.full, sds(self.packed_shape)],
            [SMEM, SMEM, self.tall, whole((1, width)), pl.BlockSpec((4, width, pair), lambda i: (0, 0, i)), pl.BlockSpec((1, pair), lambda i: (0, i))],
            [self.tall, self.half_spec, pl.BlockSpec((4, count, pair), lambda i: (0, 0, i))] + [block] * 4 + [pl.BlockSpec((self.slots, 2, PACKED, HD), lambda i: (0, i, 0, 0))],
            8 * count * width * local,
            20e6,
            grid=(local // pair,),
        )(pos, lengths, tokens, norm, weight, bound)

    def mixer_out(self, core, qe, states, intra, proj, gain, weight):
        return call(
            mixer_out_kernel,
            "mixer_out",
            [self.full, self.low, self.full, self.half, self.half],
            [SMEM, self.channel, self.state_spec, self.channel, self.proj(3, 0, 0), self.row, self.w_spec],
            [self.channel] * 3 + [self.half_spec] * 2,
            2 * self.count * self.width * self.local,
            10e6,
        )(core, qe, states, intra, proj, gain, weight)

    def ffn_specs(self, first=0, tail=True):
        width, pair, rest = self.width, self.pair, self.rest
        last = self.steps * pair // rest
        specs = [
            pl.BlockSpec((2, width, pair), lambda i: (0, 0, i + first)),
            pl.BlockSpec((pair, width), lambda i: (i + first, 0)),
            whole((2, width, rest), 0, 0, last),
            whole((rest, width), last, 0),
        ]
        return specs if tail else specs[:2]

    def ffn_own(self, core, xn2, dy, ffn_in, ffn_out):
        return call(
            ffn_own_kernel,
            "ffn_own",
            [self.wide, self.half, self.half],
            [SMEM, self.tall, self.tall, *self.ffn_specs()],
            [self.tall, self.half_spec, self.half_spec],
            12 * self.count * self.width * self.units,
            30e6,
            grid=(self.steps,),
            scratch=[pltpu.VMEM((self.count, self.width), F32)],
            vmem=60,
        )(core, xn2, dy, ffn_in, ffn_out, ffn_in, ffn_out)

    def norm_back(self, place, parts, hidden, dy, norm, weight, mixed, proj, gain, qe, packed):
        n = self.width // 8
        return call(
            norm_back_kernel,
            "norm_back",
            [self.full, self.low, sds((1, self.local)), sds(self.packed_shape), self.wide, sds((self.count, self.width), BF16), sds((self.count, n)), sds((1, self.width))],
            [SMEM] + [self.half_spec] * 4 + [self.tall, self.tall, self.norm_row, self.w_spec, self.channel, self.proj(3, 0, 0), self.row, self.channel, self.packed_spec],
            [self.channel, self.channel, self.row, self.packed_spec, self.tall, self.tall, whole((self.count, n)), self.norm_row],
            2 * self.count * self.width * self.local,
            10e6,
            scratch=[pltpu.VMEM((self.count, self.local), F32)],
        )(place, *parts, hidden, dy, norm, weight, mixed, proj, gain, qe, packed)

    def second_norm(self, place, tokens, parts, gain, lines):
        quarter = self.width // 4
        return call(
            second_norm_kernel,
            "second_norm",
            [self.wide, sds((lines * self.count, self.width), BF16), sds((self.count, quarter))],
            [SMEM, self.tall] + [self.half_spec] * 4 + [self.norm_row],
            [self.tall, self.tall, whole((self.count, quarter))],
            0,
            10e6,
        )(place, tokens, *parts, gain)

    def first_grad(self, dproj, weight):
        quarter = self.width // 4
        return call(
            first_grad_kernel,
            "first_grad",
            self.wide,
            [self.channel] * 4 + [pl.BlockSpec((4, quarter, self.local), lambda i: (0, i, 0))],
            pl.BlockSpec((self.count, quarter), lambda i: (0, i)),
            8 * self.count * self.width * self.local,
            15e6,
            grid=(4,),
        )(*dproj, weight)

    def first_back(self, dxn1, dhidden, tokens, gain):
        return call(
            first_back_kernel,
            "first_back",
            [sds((self.count, self.width), BF16), sds((1, self.width))],
            [self.tall, self.tall, self.tall, self.norm_row],
            [self.tall, self.norm_row],
            0,
            10e6,
        )(dxn1, dhidden, tokens, gain)

    def intra_back(self, dmixed, qe, ke, proj, cum, states):
        return call(
            intra_back_kernel,
            "intra_back",
            [self.full] * 4,
            [self.channel, self.channel, self.channel, whole((3, self.count, self.local)), self.channel, self.state_spec],
            [self.channel] * 4,
            14 * self.count * self.local * HD,
            10e6,
        )(dmixed, qe, ke, proj, cum, states)

    def state_back(self, pos, lengths, carried, states, ke, proj, cum, bound, dkeys, dvalues, dlogf):
        return call(
            state_back_kernel,
            "state_back",
            [sds((2, self.count, self.local)), sds((1, self.local))],
            [SMEM, SMEM, self.state_spec, self.state_spec, self.channel, self.proj(1, 0, 0), self.proj(2, 0, 0), self.channel, self.row] + [self.channel] * 3,
            [whole((2, self.count, self.local)), self.row],
            8 * self.count * self.local * HD,
            10e6,
        )(pos, lengths, carried, states, ke, proj, proj, cum, bound, dkeys, dvalues, dlogf)

    def widen(self, head, dy, lines):
        quarter = self.width // 4
        return call(
            widen_kernel,
            "widen",
            [sds((self.count, quarter)), sds((lines * self.count, self.width), BF16)],
            [SMEM, self.tall],
            [whole((self.count, quarter)), self.tall],
            0,
            4e6,
        )(head, dy)

    def turn(self, place, xn, got):
        shape = (4, self.width // 8, 2 * self.count)
        return call(turn_kernel, "turn", sds(shape, BF16), [SMEM, self.tall, self.half_spec], whole(shape), 0, 6e6)(place, xn, got)

    def mix_grad(self, turned, *grads):
        shape = (len(grads) // 2, 2, self.width // 8, self.local)
        return call(
            mix_grad_kernel,
            "mix_grad",
            [sds(shape)] * 2,
            [whole(turned.shape)] + [self.channel] * len(grads),
            [whole(shape)] * 2,
            len(grads) * self.count * self.width * self.local,
            10e6,
        )(turned, *grads)

    def ffn_grad(self, rows, xn, dy, ffn_in, ffn_out, first, steps):
        n, pair = self.width // 8, self.pair
        tail = first + steps == self.steps and self.rest > 0
        units = steps * pair + self.rest * tail
        out = sds((3, n, units))
        line = whole(xn.shape)
        return call(
            functools.partial(ffn_grad_kernel, tail),
            "ffn_grad",
            [out, out],
            [SMEM, line, line] + self.ffn_specs(first, tail),
            [whole(out.shape)] * 2,
            6 * xn.shape[0] * (self.width + 2 * n) * units,
            20e6,
            grid=(steps,),
            scratch=[pltpu.VMEM((2 * n, xn.shape[0]), BF16)] * 2 + [pltpu.VMEM((xn.shape[0], pair), BF16)] * 3,
            vmem=62,
        )(rows, xn, dy, *([ffn_in, ffn_out] * (2 if tail else 1)))


def scalar(v):
    return jnp.asarray(v, jnp.int32).reshape(1)


def body(tokens, lengths, norm_first, mix_weight, lower_bound, out_gain, w_out, norm_second, ffn_in, ffn_out, cotangent):
    shape = tokens.shape
    slots, length, width = shape
    local = lower_bound.shape[0]
    do = Calls(slots, length, width, local, ffn_out.shape[0])
    fast = lax.axis_size("seq") == 8 and lax.axis_size("head") == 4
    run = run_lines if fast else run_any
    output, grad_tokens, small, weights = run(
        do,
        tokens.reshape(do.count, width),
        lengths,
        norm_first.reshape(1, width),
        mix_weight,
        lower_bound.reshape(1, local),
        out_gain.reshape(1, local),
        w_out,
        norm_second.reshape(1, width),
        ffn_in,
        ffn_out,
        cotangent.reshape(do.count, width),
    )
    first, second = small[:width], small[width : 2 * width]
    bound_sum, gain_sum = small[2 * width : 2 * width + local], small[2 * width + local :]
    return (output.reshape(shape), grad_tokens.reshape(shape), first, weights[0], bound_sum, gain_sum, weights[1], second, weights[2], weights[3])


def run_any(do, tokens, lengths, norm_first, mix_weight, bound, gain, w_out, norm_second, ffn_in, ffn_out, dy):
    def total(halves):
        low, high = jnp.split(lax.psum(jnp.concatenate(halves, axis=1), "head"), 2, axis=1)
        return low, jnp.zeros_like(low), high, jnp.zeros_like(high)

    pos, core = scalar(lax.axis_index("seq")), scalar(0)
    nowhere = jnp.zeros((3,), jnp.int32)
    xn1, _, proj, cum, qe, ke, intra, packed = do.project(pos, lengths, tokens, norm_first, mix_weight, bound)
    states = entering_all(packed, False)
    mixed, gated, _, *halves = do.mixer_out(core, qe, states, intra, proj, gain, w_out)
    hidden, xn2, _ = do.second_norm(nowhere, tokens, total(halves), norm_second, 1)
    ffn, dkeep, dsend = do.ffn_own(core, xn2, dy, ffn_in, ffn_out)
    output = (hidden + lax.psum(ffn, "head")).astype(BF16)
    dpre_gate, dmixed, part_gain, back, dhidden, dbranch, _, part_norm_second = do.norm_back(
        nowhere, total((dkeep, dsend)), hidden, dy, norm_second, w_out, mixed, proj, gain, qe, packed
    )
    carried = entering_all(back, True)
    dpre_query, dkeys, dvalues, dlogf = do.intra_back(dmixed, qe, ke, proj, cum, states)
    dpre_fv, part_bound = do.state_back(pos, lengths, carried, states, ke, proj, cum, bound, dkeys, dvalues, dlogf)
    dproj = (dpre_query, dpre_fv[0], dpre_fv[1], dpre_gate)
    grad_tokens, part_norm_first = do.first_back(lax.psum(do.first_grad(dproj, mix_weight), "head"), dhidden, tokens, norm_first)
    weights = weight_grads_whole(xn1, dproj, gated, dbranch, xn2, dy, ffn_in, ffn_out)
    small = lax.psum(jnp.concatenate([part_norm_first[0], part_norm_second[0], part_bound[0], part_gain[0]]), "seq")
    return output, grad_tokens, small, weights


def run_lines(do, tokens, lengths, norm_first, mix_weight, bound, gain, w_out, norm_second, ffn_in, ffn_out, dy):
    width, local, quarter = do.width, do.local, do.width // 4
    seq, head = lax.axis_index("seq"), lax.axis_index("head")
    x, z = seq % 2, seq // 2
    seq_at, core = scalar(seq), scalar(head % 2)
    place = jnp.stack([head % 2, head, x]).astype(jnp.int32)

    def shift(a, k):
        return lax.ppermute(a, "seq", z_shift(k))

    def sum_cores(keep, send):
        return keep + core_swap(send)

    def sum_near(keep, send):
        got = lax.ppermute(send, "seq", flip(2))
        return (keep[:, 0], got[:, 0]), keep[:, 1] + got[:, 1]

    def sum_far(near):
        return lax.ppermute(near[1], "seq", flip(4))

    def summed(near, far):
        return near[0][0] + near[0][1] + far

    dy_quarter, dy_all = do.widen(scalar(head), dy, 4)
    dy1 = shift(dy_quarter, 1)
    xn1, xn1_away, proj, cum, qe, ke, intra, packed = do.project(seq_at, lengths, tokens, norm_first, mix_weight, bound)
    early, late = pair_states(packed, False)
    early, late, dy1 = tie(early, late, dy1)

    into = pass_states(join(early, late), False)
    dy1_over = y_swap(dy1)
    early, into, dy1_over, dy_quarter = tie(early, into, dy1_over, dy_quarter)

    states = enter_states(early, into, do.state_shape, False)
    mixed, gated, gated_wide, keep, send = do.mixer_out(core, qe, states, intra, proj, gain, w_out)
    half = sum_cores(keep, send)
    half, dy_quarter, xn1_away, dy1, dy1_over = tie(half, dy_quarter, xn1_away, dy1, dy1_over)

    over = y_swap(half)
    half_other = core_swap(half)
    dy2 = shift(dy_quarter, 2)
    xn1_got = x_swap(xn1_away)
    dy_all = assemble([(dy1, dy1_over)], dy_all, 1)
    half, half_other, over, dy2, gated_wide, xn1_got, dy_all = tie(half, half_other, over, dy2, gated_wide, xn1_got, dy_all)

    dy2_over = y_swap(dy2)
    hidden, xn_all, xn_quarter = do.second_norm(place, tokens, (half, over, half_other, core_swap(over)), norm_second, 4)
    xnl1 = shift(xn_quarter, 1)
    gated_got = x_swap(gated_wide)
    ffn, dkeep, dsend = do.ffn_own(core, xn_all, dy, ffn_in, ffn_out)
    dkeep, dsend, xn_quarter, dy2_over, xnl1, gated_got, ffn = tie(dkeep, dsend, xn_quarter, dy2_over, xnl1, gated_got, ffn)

    dhalf = sum_cores(dkeep, dsend)
    dhalf, xn_quarter, dy_all, xn1_got = tie(dhalf, xn_quarter, dy_all, xn1_got)
    dover = y_swap(dhalf)
    dhalf_other = core_swap(dhalf)
    xnl2 = shift(xn_quarter, 2)
    dy_all = assemble([(dy2, dy2_over)], dy_all, 2)
    xn1_turned = do.turn(seq_at, xn1, xn1_got)
    dhalf, dover, dhalf_other, xnl2, xn_quarter, xnl1, dy_all, xn1_turned, ffn = tie(dhalf, dover, dhalf_other, xnl2, xn_quarter, xnl1, dy_all, xn1_turned, ffn)
    ffn = lax.psum(ffn, "head")

    xnl3 = shift(xn_quarter, 3)
    dpre_gate, dmixed, part_gain, back, dhidden, dbranch, dbranch_away, part_norm_second = do.norm_back(
        place, (dhalf, dover, dhalf_other, core_swap(dover)), hidden, dy, norm_second, w_out, mixed, proj, gain, qe, packed
    )
    back, dpre_gate, dmixed, dbranch, dbranch_away, dy_quarter = tie(back, dpre_gate, dmixed, dbranch, dbranch_away, dy_quarter)

    early, late = pair_states(back, True)
    dy3 = shift(dy_quarter, 3)
    early, late, dpre_gate, dmixed, dbranch_away, xnl3, dy3 = tie(early, late, dpre_gate, dmixed, dbranch_away, xnl3, dy3)
    xn_parts = lax.all_gather(jnp.concatenate([xnl1, xnl2, xnl3]), "head")
    into = pass_states(join(early, late), True)
    dbranch_own = x_swap(dbranch_away)
    dpre_query, dkeys, dvalues, dlogf = do.intra_back(dmixed, qe, ke, proj, cum, states)
    gate_got = x_swap(dpre_gate)
    dy3_over = y_swap(dy3)
    early, into, gate_got, dpre_query = tie(early, into, gate_got, dpre_query)

    gate = do.mix_grad(xn1_turned, dpre_gate, gate_got)
    early, into, gate, dbranch_own, dy3_over, ffn = tie(early, into, gate, dbranch_own, dy3_over, ffn)

    near_gate = sum_near(*gate)
    dbranch_over = y_swap(dbranch_own)
    carried = enter_states(early, into, do.state_shape, True)
    dy_all = assemble([(dy3, dy3_over)], dy_all, 3)
    dpre_fv, part_bound = do.state_back(seq_at, lengths, carried, states, ke, proj, cum, bound, dkeys, dvalues, dlogf)
    dpre_fv, dpre_query, dbranch_over, dy_all = tie(dpre_fv, dpre_query, dbranch_over, dy_all)

    fv_got = x_swap(dpre_fv)
    down = do.mix_grad(do.turn(seq_at, dbranch, assemble([(dbranch_own, dbranch_over)])), gated, gated_got)
    near_down = sum_near(*down)
    near_gate, down = tie(near_gate, down)
    gate_far = sum_far(near_gate)
    dxn1 = do.first_grad((dpre_query, dpre_fv[0], dpre_fv[1], dpre_gate), mix_weight)
    xn_parts, dxn1, ffn = tie(xn_parts, dxn1, ffn)
    fv_got, gate_far, near_down, xn_all, dpre_query, xn_parts = tie(fv_got, gate_far, near_down, xn_all, dpre_query, xn_parts)
    dxn1 = lax.psum(dxn1, "head")

    rows = jnp.stack([seq, seq ^ 1]).astype(jnp.int32)
    query_got = x_swap(dpre_query)
    w_far = sum_far(near_down)
    forget_values = do.mix_grad(xn1_turned, dpre_fv[0], fv_got[0], dpre_fv[1], fv_got[1])
    forget_values, xn_all, xn_parts = tie(forget_values, xn_all, xn_parts)
    near_fv = sum_near(*forget_values)
    xn_all = join_heads(xn_parts, xn_all, 1)
    mine_a, away_a = do.ffn_grad(rows, xn_all, dy_all, ffn_in, ffn_out, 0, 2)
    away_a, xn_all, query_got = tie(away_a, xn_all, query_got)
    got_a = x_swap(away_a)
    query = do.mix_grad(xn1_turned, dpre_query, query_got)
    mine_b, away_b = do.ffn_grad(rows, xn_all, dy_all, ffn_in, ffn_out, 2, 2)
    near_fv, w_far, got_a, query, away_b, xn_all, dhidden, hidden = tie(near_fv, w_far, got_a, query, away_b, xn_all, dhidden, hidden)

    got_b = x_swap(away_b)
    near_query, fv_far = sum_near(*query), sum_far(near_fv)
    grad_tokens, part_norm_first = do.first_back(dxn1, dhidden, tokens, norm_first)
    mine_c, away_c = do.ffn_grad(rows, xn_all, dy_all, ffn_in, ffn_out, 4, do.steps - 4)
    small = jnp.concatenate([part_norm_first[0], part_norm_second[0], part_bound[0], part_gain[0]])
    small = small + lax.ppermute(small, "seq", flip(1))
    output = (hidden + ffn).astype(BF16)
    got_b, near_query, fv_far, small, away_c, output = tie(got_b, near_query, fv_far, small, away_c, output)

    got_c = x_swap(away_c)
    query_far = sum_far(near_query)
    for bit in (2, 4):
        small = small + lax.ppermute(small, "seq", flip(bit))
    parts = ((mine_a, got_a), (mine_b, got_b), (mine_c, got_c))
    grad_in = jnp.concatenate([mine[:2] + got[:2] for mine, got in parts], axis=2)
    grad_out = jnp.concatenate([(mine[2] + got[2]).T for mine, got in parts], axis=0)
    grad_mix = jnp.concatenate([summed(near_query, query_far), summed(near_fv, fv_far), summed(near_gate, gate_far)])
    grad_w_out = summed(near_down, w_far)
    return output, grad_tokens, small, (grad_mix, grad_w_out[0].T, grad_in, grad_out)


def weight_grads_whole(xn1, dproj, gated, dbranch, xn2, dy, ffn_in, ffn_out):
    gate, up = dot(xn2, ffn_in[0]), dot(xn2, ffn_in[1])
    dact = dot(dy, ffn_out, NT)
    sig = sigmoid(gate)
    swish = gate * sig
    act = (swish * up).astype(BF16)
    dgate = (dact * up * (sig * (1.0 + gate * (1.0 - sig)))).astype(BF16)
    dup = (dact * swish).astype(BF16)

    def scatter(a, axis):
        return lax.psum_scatter(a, "seq", scatter_dimension=axis, tiled=True)

    return (
        jnp.stack([scatter(dot(xn1, d.astype(BF16), TN), 0) for d in dproj]),
        scatter(dot(gated, dbranch, TN), 1),
        jnp.stack([scatter(dot(xn2, d, TN), 0) for d in (dgate, dup)]),
        scatter(dot(act, dy, TN), 1),
    )


def solution(mesh):
    in_specs = (
        P(None, "seq", None),
        P(),
        P(),
        P(None, None, "head"),
        P("head"),
        P("head"),
        P("head", None),
        P(),
        P(None, None, "head"),
        P("head", None),
        P(None, "seq", None),
    )
    out_specs = (
        P(None, "seq", None),
        P(None, "seq", None),
        P(),
        P(None, "seq", "head"),
        P("head"),
        P("head"),
        P("head", "seq"),
        P(),
        P(None, "seq", "head"),
        P("head", "seq"),
    )
    return jax.shard_map(body, mesh=mesh, in_specs=in_specs, out_specs=out_specs, check_vma=False)
```
